32 devices in a mesh: dp: 16 (over z, y, x), mp: 2 (over core).
Axes of the slice: x: 2, y: 2, z: 4, core: 2. Of those that a mesh axis runs over, the one named last changes fastest.
Arguments:
- tokens: bfloat16 [32768, 768], P(('dp', 'mp')), may hold values from -6 to 6
- timesteps: int32 [256], P('dp'), may hold values from 0 to 1999
- src_len: int32 [256], P('dp'), may hold values from 1 to 64
- tgt_len: int32 [256], P('dp'), may hold values from 1 to 64
- sample_weight: float32 [256], P('dp'), may hold values from 0.25 to 4
- w_qkv: bfloat16 [3, 768, 768], P(None, None, 'mp'), may hold values from -0.21875 to 0.21875
- bias_qv: bfloat16 [2, 768], P(None, 'mp'), may hold values from -3 to 3
- w_out: bfloat16 [768, 768], P('mp'), may hold values from -1.25 to 1.25
- bias_out: float32 [768], replicated, may hold values from -2 to 2
- gain_attn: float32 [768], replicated, may hold values from 0.5 to 1.5
- shift_attn: float32 [768], replicated, may hold values from -3 to 3
- w_up: bfloat16 [768, 3072], P(None, 'mp'), may hold values from -0.21875 to 0.21875
- bias_up: bfloat16 [3072], P('mp'), may hold values from -3 to 3
- w_down: bfloat16 [3072, 768], P('mp'), may hold values from -0.109375 to 0.109375
- bias_down: float32 [768], replicated, may hold values from -2 to 2
- gain_mlp: float32 [768], replicated, may hold values from 0.5 to 1.5
- shift_mlp: float32 [768], replicated, may hold values from -3 to 3
- cotangent: bfloat16 [32768, 768], P(('dp', 'mp')), may hold values from -6 to 6
Outputs:
- layer_out: float32 [32768, 768], P(('dp', 'mp'))
- tokens_grad: float32 [32768, 768], P(('dp', 'mp'))
- grad_w_qkv: float32 [3, 768, 768], P(None, 'dp', 'mp')
- grad_w_out: float32 [768, 768], P(('mp', 'dp'))
- grad_w_up: float32 [768, 3072], P('dp', 'mp')
- grad_w_down: float32 [3072, 768], P(('mp', 'dp'))
- grad_bias_qv: float32 [2, 768], P(None, 'mp')
- grad_bias_up: float32 [3072], P('mp')
- grad_bias_out: float32 [768], replicated
- grad_rows: float32 [5, 768], replicated
The draws below stay inside these ranges and needn't reach their ends.
Inputs may be any that keep to these rules, and one draw needn't show every extreme that they name: A sequence holds src_len source tokens, then tgt_len target tokens, then padding.
All inputs are finite; a program needn't handle non-finite values.
Results may differ from the reference program's by a relative error of at most 0.018.
The reference program's roundings to bfloat16 on the way count: a program that leaves them out, or rounds other values in their place, can miss the bound.
Values may be sent and summed in bfloat16 or wider, within the bound.
No kernel may reach another device: no remote copies, remote signals or barrier semaphores. Data moves between devices by JAX's collectives and lax.ppermute only.
A program may use at most 192 MiB of HBM per device.

```python
import math
import jax
import jax.numpy as jnp
from jax import lax

D = 768
HD = 64
FF = 3072
LEN = 128
DIFF_STEPS = 2000
SEQS = 256
TOKENS = 32768


def with_ends(entries, key, least, high):
    place = [jax.random.randint(jax.random.fold_in(key, axis), (), 0, length) for axis, length in enumerate(entries.shape)]
    main_axis = entries.shape.index(max(entries.shape))
    neighbour = place[:main_axis] + [(place[main_axis] + 1) % entries.shape[main_axis]] + place[main_axis + 1:]
    return entries.at[tuple(place)].set(least).at[tuple(neighbour)].set(high)


def with_spikes(array, stream_key, source, target, shards_of, factor):
    def block_of(dim):
        return (jnp.arange(array.shape[dim]) // (array.shape[dim] // shards_of)).reshape((-1,) + (1,) * (array.ndim - 1 - dim))

    near = jax.random.permutation(stream_key, shards_of)[block_of(target)]
    second = (block_of(target) + shards_of // 2) % shards_of
    return jnp.where((block_of(source) == near) | (block_of(source) == second), factor * array, array)


def levels(own_key, dims, split, smallest, top_value):
    loudness, own = 1.0, jax.random.fold_in(own_key, 6)
    for dim, blocks in split:
        heights = jnp.exp(jax.random.uniform(jax.random.fold_in(own, dim), (blocks,), jnp.float32, smallest / len(split), top_value / len(split)))
        loudness = loudness * jnp.repeat(heights, dims[dim] // blocks).reshape([-1 if axis == dim else 1 for axis in range(len(dims))])
    return loudness


def normal_values(stream_key, extent, scale, bound, split=(), kind=jnp.bfloat16):
    entries = scale * jax.random.normal(stream_key, extent, jnp.float32)
    if split:
        entries = entries * levels(stream_key, extent, split, -0.22, 0.18)
    return jnp.clip(entries, -bound, bound).astype(kind)


def gaussian_with(key, extent, scale, most, pieces, heavy, held_as=jnp.bfloat16):
    array = scale * jax.random.normal(key, extent, jnp.float32)
    if pieces:
        array = array * levels(key, extent, pieces, -0.22, 0.18)
    return jnp.clip(with_spikes(array, jax.random.fold_in(key, 3), *heavy), -most, most).astype(held_as)


def setup_inputs(seed: int = 0) -> dict:
    key_of = jax.random.split(jax.random.key(seed), 19)
    tokens = gaussian_with(key_of[0], (TOKENS, D), 1.0, 6.0, ((0, 32),), (0, 1, 32, 2.75))
    timesteps = with_ends(jax.random.randint(key_of[1], (SEQS,), 0, DIFF_STEPS), jax.random.fold_in(key_of[1], 1), 0, DIFF_STEPS - 1).astype(jnp.int32)
    src_len = with_ends(jax.random.randint(key_of[2], (SEQS,), 1, LEN // 2 + 1), jax.random.fold_in(key_of[2], 1), 1, (LEN // 2 + 1) - 1).astype(jnp.int32)
    tgt_len = with_ends(jax.random.randint(key_of[3], (SEQS,), 1, LEN // 2 + 1), jax.random.fold_in(key_of[3], 1), 1, (LEN // 2 + 1) - 1).astype(jnp.int32)
    sample_weight = jnp.clip(jnp.exp(math.log(4.0) - 2.7725887 * jax.random.uniform(key_of[4], (SEQS,), jnp.float32) ** levels(key_of[4], (SEQS,), ((0, 16),), -0.2, 0.2)), 0.25, 4.0)
    w_qkv = normal_values(key_of[5], (3, D, D), D ** -0.5, 0.21875, ((2, 2),))
    bias_qv = normal_values(key_of[6], (2, D), 0.5, 3.0, ((1, 2),))
    w_out = normal_values(key_of[7], (D, D), (D // 32) ** -0.5, 1.25, ((0, 2),))
    bias_out = normal_values(key_of[8], (D,), 0.3, 2.0, (), jnp.float32)
    gain_attn = jnp.clip(1.0 + 0.1 * jax.random.normal(key_of[9], (D,), jnp.float32), 0.5, 1.5)
    shift_attn = normal_values(key_of[10], (D,), 0.5, 3.0, (), jnp.float32)
    w_up = normal_values(key_of[11], (D, FF), D ** -0.5, 0.21875, ((1, 2),))
    bias_up = normal_values(key_of[12], (FF,), 0.5, 3.0, ((0, 2),))
    w_down = normal_values(key_of[13], (FF, D), FF ** -0.5, 0.109375, ((0, 2),))
    bias_down = normal_values(key_of[14], (D,), 0.3, 2.0, (), jnp.float32)
    gain_mlp = jnp.clip(1.0 + 0.1 * jax.random.normal(key_of[15], (D,), jnp.float32), 0.5, 1.5)
    shift_mlp = normal_values(key_of[16], (D,), 0.5, 3.0, (), jnp.float32)
    cotangent = gaussian_with(key_of[17], (TOKENS, D), 1.0, 6.0, ((0, 32),), (0, 1, 32, 2.75))
    return dict(tokens=tokens, timesteps=timesteps, src_len=src_len, tgt_len=tgt_len, sample_weight=sample_weight, w_qkv=w_qkv, bias_qv=bias_qv, w_out=w_out, bias_out=bias_out, gain_attn=gain_attn, shift_attn=shift_attn, w_up=w_up, bias_up=bias_up, w_down=w_down, bias_down=bias_down, gain_mlp=gain_mlp, shift_mlp=shift_mlp, cotangent=cotangent)


NORM_EPS = 1e-05
MASK_FILL = -1e+30
PRECISE = lax.Precision.HIGHEST

@jax.custom_vjp
def low(v):
    return lax.optimization_barrier(v.astype(jnp.bfloat16)).astype(jnp.float32)

@jax.custom_vjp
def low_back(v):
    return v

def low_keep(v):
    return (low(v), None)

def low_pass(kept, grad):
    return (grad,)

def back_keep(v):
    return (v, None)

def back_low(kept, grad):
    return (low(grad),)
low.defvjp(low_keep, low_pass)
low_back.defvjp(back_keep, back_low)

def time_table(timesteps, width):
    half_width = width // 2
    frequency = jnp.exp(-math.log(10000.0) * jnp.arange(half_width, dtype=jnp.float32) / half_width)
    angles = timesteps.astype(jnp.float32)[:, None] * frequency[None, :]
    return jnp.concatenate([jnp.sin(angles), jnp.cos(angles)], axis=1)

def layer_norm(value, gain_vec, shift_vec):
    row_mean = lax.optimization_barrier(jnp.mean(value, axis=-1, keepdims=True))
    centred = value - row_mean
    inv_std = lax.rsqrt(lax.optimization_barrier(jnp.mean(centred * centred, axis=-1, keepdims=True)) + NORM_EPS)
    return centred * inv_std * gain_vec + shift_vec

def layer_block(start_x, lengths, weights):
    w_qkv, bias_qv, w_out, bias_out, gain_attn, shift_attn, w_up, bias_up, w_down, bias_down, gain_mlp, shift_mlp = weights
    groups = start_x.shape[0]
    head_count = D // HD
    x_low = low(start_x)
    projected = jnp.einsum('gtd,sde->sgte', x_low, w_qkv, precision=PRECISE)
    queries = low(low_back(projected[0] + bias_qv[0])).reshape(groups, LEN, head_count, HD)
    keys_low = low(low_back(projected[1])).reshape(groups, LEN, head_count, HD)
    values = low(low_back(projected[2] + bias_qv[1])).reshape(groups, LEN, head_count, HD)
    scores = low_back(jnp.einsum('gqhe,gkhe->ghqk', queries, keys_low, precision=PRECISE) * HD ** (-0.5))
    live_keys = (jnp.arange(LEN)[None, :] < lengths[:, None])[:, None, None, :]
    scores = jnp.where(live_keys, scores, MASK_FILL)
    row_max = lax.optimization_barrier(jnp.max(scores, axis=-1, keepdims=True))
    exp_scores = jnp.exp(scores - row_max)
    attn_prob = low(exp_scores / lax.optimization_barrier(jnp.sum(exp_scores, axis=-1, keepdims=True)))
    context = jnp.einsum('ghqk,gkhe->gqhe', attn_prob, values, precision=PRECISE).reshape(groups, LEN, D)
    context = low(low_back(context))
    attn_out = low_back(jnp.einsum('gtc,cd->gtd', context, w_out, precision=PRECISE) + bias_out)
    mid_x = layer_norm(start_x + attn_out, gain_attn, shift_attn)
    pre_act = low_back(jnp.einsum('gtd,df->gtf', low(mid_x), w_up, precision=PRECISE) + bias_up)
    hidden = low(jax.nn.gelu(pre_act, approximate=False))
    mlp_out = low_back(jnp.einsum('gtf,fd->gtd', hidden, w_down, precision=PRECISE) + bias_down)
    return layer_norm(mid_x + mlp_out, gain_mlp, shift_mlp)

def reference(tokens, timesteps, src_len, tgt_len, sample_weight, w_qkv, bias_qv, w_out, bias_out, gain_attn, shift_attn, w_up, bias_up, w_down, bias_down, gain_mlp, shift_mlp, cotangent):
    lengths = src_len + tgt_len
    start_x = tokens.astype(jnp.float32).reshape(SEQS, LEN, D) + time_table(timesteps, D)[:, None, :]
    position = jnp.arange(LEN)[None, :]
    target_scale = ((position >= src_len[:, None]) & (position < lengths[:, None])).astype(jnp.float32) * sample_weight[:, None]
    out_grad = cotangent.astype(jnp.float32).reshape(SEQS, LEN, D) * target_scale[:, :, None]
    weights = tuple((param.astype(jnp.float32) for param in (w_qkv, bias_qv, w_out, bias_out, gain_attn, shift_attn, w_up, bias_up, w_down, bias_down, gain_mlp, shift_mlp)))
    per_block = math.gcd(SEQS, 32)
    blocks = SEQS // per_block
    run_block = jax.checkpoint(layer_block)

    def whole(x_in, params):
        outputs = lax.map(lambda packed: run_block(packed[0], packed[1], params), (x_in.reshape(blocks, per_block, LEN, D), lengths.reshape(blocks, per_block)))
        return outputs.reshape(SEQS, LEN, D)
    output, pullback = jax.vjp(whole, start_x, weights)
    input_grad, grads = pullback(out_grad)
    grad_qkv, grad_qv, grad_wout, grad_bo, grad_ga, grad_sa, grad_wup, grad_bu, grad_wdown, grad_bd, grad_gm, grad_sm = grads
    grad_rows = jnp.stack([grad_ga, grad_sa, grad_bd, grad_gm, grad_sm])
    return (output.reshape(TOKENS, D), input_grad.reshape(TOKENS, D), grad_qkv, grad_wout, grad_wup, grad_wdown, grad_qv, grad_bu, grad_bo, grad_rows)
```

```python
import functools
import math

import jax
import jax.numpy as jnp
from jax import lax
from jax.experimental import pallas as pl
from jax.experimental.pallas import tpu as pltpu
from jax.sharding import PartitionSpec as P

HD = 64
LEN = 128
PAIR = 2 * HD
NORM_EPS = 1e-05
MASK_FILL = -1e30
BF = jnp.bfloat16
F32 = jnp.float32
MIB = 1 << 20

NN = (((1,), (0,)), ((), ()))
NT = (((1,), (1,)), ((), ()))
TN = (((0,), (0,)), ((), ()))

VMEM_SPEC = pl.BlockSpec(memory_space=pltpu.VMEM)
SMEM_SPEC = pl.BlockSpec(memory_space=pltpu.SMEM)


def mm(a, b, dims=NN):
    return lax.dot_general(a, b, dims, preferred_element_type=F32)


def fixed(shape):
    zeros = (0,) * len(shape)
    return pl.BlockSpec(shape, lambda *_: zeros)


def params(mib):
    return pltpu.CompilerParams(vmem_limit_bytes=mib * MIB)


def time_table(timesteps, width):
    half_width = width // 2
    frequency = jnp.exp(-math.log(10000.0) * jnp.arange(half_width, dtype=F32) / half_width)
    angles = timesteps.astype(F32)[:, None] * frequency[None, :]
    return jnp.concatenate([jnp.sin(angles), jnp.cos(angles)], axis=1)


def add_table(tok_ref, table_ref, first_seq, count):
    rows = []
    for s in range(count):
        part = tok_ref[s * LEN : (s + 1) * LEN, :].astype(F32)
        rows.append(part + table_ref[pl.ds(first_seq + s, 1), :])
    return jnp.concatenate(rows, axis=0)


def half_masks(rows, value=1.0):
    lane = lax.broadcasted_iota(jnp.int32, (rows, PAIR), 1)
    first = jnp.where(lane < HD, value, 0.0).astype(BF)
    second = jnp.where(lane < HD, 0.0, value).astype(BF)
    return first, second


def fold8(value):
    rows, cols = value.shape
    return jnp.sum(value.reshape(rows // 8, 8, cols), axis=0)


def attend_kernel(seqs, emit_x, len_ref, tok_ref, table_ref, w_ref, bias_ref, *outs):
    if emit_x:
        qkv_ref, prob_ref, ctx_ref, x_ref = outs
    else:
        qkv_ref, prob_ref, ctx_ref = outs
    first_seq = pl.program_id(0) * seqs
    x_low = add_table(tok_ref, table_ref, first_seq, seqs).astype(BF)
    if emit_x:
        x_ref[...] = x_low
    q = (mm(x_low, w_ref[0]) + bias_ref[0:1, :]).astype(BF)
    k = mm(x_low, w_ref[1]).astype(BF)
    v = (mm(x_low, w_ref[2]) + bias_ref[1:2, :]).astype(BF)
    qkv_ref[0] = q
    qkv_ref[1] = k
    qkv_ref[2] = v
    scale_a, scale_b = half_masks(LEN, HD**-0.5)
    one_a, one_b = half_masks(LEN)
    key_pos = lax.broadcasted_iota(jnp.int32, (LEN, 2 * LEN), 1) % LEN
    for s in range(seqs):
        live = key_pos < len_ref[first_seq + s]
        rows = slice(s * LEN, (s + 1) * LEN)
        for j in range(q.shape[1] // PAIR):
            cols = slice(j * PAIR, (j + 1) * PAIR)
            q2, k2, v2 = q[rows, cols], k[rows, cols], v[rows, cols]
            kcat = jnp.concatenate([k2 * scale_a, k2 * scale_b], axis=0)
            vcat = jnp.concatenate([v2 * one_a, v2 * one_b], axis=0)
            scores = jnp.where(live, mm(q2, kcat, NT), MASK_FILL)
            halves = []
            for h in range(2):
                part = scores[:, h * LEN : (h + 1) * LEN]
                e = jnp.exp(part - jnp.max(part, axis=1, keepdims=True))
                halves.append(e / jnp.sum(e, axis=1, keepdims=True))
            probs = jnp.concatenate(halves, axis=1)
            prob_ref[s, j] = probs
            ctx_ref[rows, cols] = mm(probs.astype(BF), vcat).astype(BF)


def attend(tokens, table, lengths, w_half, bias_half, emit_x):
    rows, width = tokens.shape
    cols = w_half.shape[2]
    seqs = 2
    block = seqs * LEN
    pairs = cols // PAIR
    out_shape = [
        jax.ShapeDtypeStruct((3, rows, cols), BF),
        jax.ShapeDtypeStruct((rows // LEN, pairs, LEN, 2 * LEN), F32),
        jax.ShapeDtypeStruct((rows, cols), BF),
    ]
    out_specs = [
        pl.BlockSpec((3, block, cols), lambda i: (0, i, 0)),
        pl.BlockSpec((seqs, pairs, LEN, 2 * LEN), lambda i: (i, 0, 0, 0)),
        pl.BlockSpec((block, cols), lambda i: (i, 0)),
    ]
    if emit_x:
        out_shape.append(jax.ShapeDtypeStruct((rows, width), BF))
        out_specs.append(pl.BlockSpec((block, width), lambda i: (i, 0)))
    return pl.pallas_call(
        functools.partial(attend_kernel, seqs, emit_x),
        grid=(rows // block,),
        in_specs=[
            SMEM_SPEC,
            pl.BlockSpec((block, width), lambda i: (i, 0)),
            fixed(table.shape),
            fixed(w_half.shape),
            fixed(bias_half.shape),
        ],
        out_specs=out_specs,
        out_shape=out_shape,
        compiler_params=params(40),
        name="attend",
    )(lengths, tokens, table, w_half, bias_half)


def normalize(value):
    centred = value - jnp.mean(value, axis=1, keepdims=True)
    inv_std = lax.rsqrt(jnp.mean(centred * centred, axis=1, keepdims=True) + NORM_EPS)
    return centred * inv_std, inv_std


def normalize_back(scaled, normed, inv_std):
    return inv_std * (
        scaled
        - jnp.mean(scaled, axis=1, keepdims=True)
        - normed * jnp.mean(scaled * normed, axis=1, keepdims=True)
    )


def gelu_pair(v):
    u = jnp.abs(v) * (0.3275911 / math.sqrt(2.0)) + 1.0
    t = 1.0 / u
    e = jnp.exp(v * v * -0.5)
    poly = 0.5 * 1.061405429
    for coef in (-1.453152027, 1.421413741, -0.284496736, 0.254829592):
        poly = poly * t + 0.5 * coef
    tail = poly * t * e
    cdf = jnp.where(v < 0.0, tail, 1.0 - tail)
    return v * cdf, cdf + v * e * (1.0 / math.sqrt(2.0 * math.pi))


def mlp_kernel(
    seqs, chunk,
    src_ref, len_ref, weight_ref, tok_ref, table_ref, ctx_own_ref, ctx_oth_ref, cot_ref,
    wo_own_ref, wo_oth_ref, bo_ref, ga_ref, sa_ref,
    wu_own_ref, wu_oth_ref, bu_own_ref, bu_oth_ref, wd_own_ref, wd_oth_ref, bd_ref, gm_ref, sm_ref,
    normed_ref, inv_ref, mid_ref, hid_own_ref, hid_oth_ref, dg_own_ref, dg_oth_ref,
    out_ref, ograd_ref, mgrad_ref, sums_ref,
):
    step = pl.program_id(0)
    first_seq = step * seqs
    start_x = add_table(tok_ref, table_ref, first_seq, seqs)
    mid_in = start_x + (mm(ctx_own_ref[...], wo_own_ref[...]) + mm(ctx_oth_ref[...], wo_oth_ref[...])) + bo_ref[...]
    normed, inv = normalize(mid_in)
    normed_ref[...] = normed
    inv_ref[...] = inv
    mid_x = normed * ga_ref[...] + sa_ref[...]
    mid_low = mid_x.astype(BF)
    mid_ref[...] = mid_low
    total = mid_x + bd_ref[...]
    for wu_ref, bu_ref, wd_ref, hid_ref, dg_ref in (
        (wu_own_ref, bu_own_ref, wd_own_ref, hid_own_ref, dg_own_ref),
        (wu_oth_ref, bu_oth_ref, wd_oth_ref, hid_oth_ref, dg_oth_ref),
    ):
        for c in range(0, wu_ref.shape[1], chunk):
            pre = mm(mid_low, wu_ref[:, c : c + chunk]) + bu_ref[:, c : c + chunk].astype(F32)
            hidden, slope = gelu_pair(pre)
            hidden = hidden.astype(BF)
            hid_ref[:, c : c + chunk] = hidden
            dg_ref[:, c : c + chunk] = slope.astype(BF)
            total = total + mm(hidden, wd_ref[c : c + chunk, :])
    normed2, inv2 = normalize(total)
    out_ref[...] = normed2 * gm_ref[...] + sm_ref[...]
    scales = []
    pos = lax.broadcasted_iota(jnp.int32, (LEN, 1), 0)
    for s in range(seqs):
        inside = (pos >= src_ref[first_seq + s]) & (pos < len_ref[first_seq + s])
        scales.append(jnp.where(inside, weight_ref[first_seq + s], 0.0))
    e = cot_ref[...].astype(F32) * jnp.concatenate(scales, axis=0)
    ograd = normalize_back(e * gm_ref[...], normed2, inv2)
    ograd_ref[...] = ograd
    mgrad = ograd.astype(BF)
    mgrad_ref[...] = mgrad
    part = jnp.stack([fold8(mgrad.astype(F32)), fold8(e * normed2), fold8(e)])

    @pl.when(step == 0)
    def _():
        sums_ref[...] = part

    @pl.when(step > 0)
    def _():
        sums_ref[...] += part


def mlp(src, lengths, weight, tokens, table, ctx_own, ctx_oth, cot, wo_own, wo_oth, bo, ga, sa,
        wu_own, wu_oth, bu_own, bu_oth, wd_own, wd_oth, bd, gm, sm):
    rows, width = tokens.shape
    seqs = 2
    block = seqs * LEN
    cols = ctx_own.shape[1]
    ff = wu_own.shape[1]
    row_block = lambda n: pl.BlockSpec((block, n), lambda i: (i, 0))
    resident = (wo_own, wo_oth, bo, ga, sa, wu_own, wu_oth, bu_own, bu_oth, wd_own, wd_oth, bd, gm, sm)
    sds = jax.ShapeDtypeStruct
    return pl.pallas_call(
        functools.partial(mlp_kernel, seqs, 512),
        grid=(rows // block,),
        in_specs=[SMEM_SPEC] * 3
        + [row_block(width), fixed(table.shape), row_block(cols), row_block(cols), row_block(width)]
        + [fixed(a.shape) for a in resident],
        out_specs=[
            row_block(width), row_block(1), row_block(width),
            row_block(ff), row_block(ff), row_block(ff), row_block(ff),
            row_block(width), row_block(width), row_block(width),
            fixed((3, 8, width)),
        ],
        out_shape=[
            sds((rows, width), F32), sds((rows, 1), F32), sds((rows, width), BF),
            sds((rows, ff), BF), sds((rows, ff), BF), sds((rows, ff), BF), sds((rows, ff), BF),
            sds((rows, width), F32), sds((rows, width), F32), sds((rows, width), BF),
            sds((3, 8, width), F32),
        ],
        compiler_params=params(56),
        name="mlp",
    )(src, lengths, weight, tokens, table, ctx_own, ctx_oth, cot, *resident)


def pre_kernel(mgrad_ref, wd_own_ref, wd_oth_ref, dg_own_ref, dg_oth_ref, pg_own_ref, pg_oth_ref, sum_own_ref, sum_oth_ref):
    for wd_ref, dg_ref, pg_ref, sum_ref in (
        (wd_oth_ref, dg_oth_ref, pg_oth_ref, sum_oth_ref),
        (wd_own_ref, dg_own_ref, pg_own_ref, sum_own_ref),
    ):
        pg = (mm(mgrad_ref[...], wd_ref[...], NT) * dg_ref[...].astype(F32)).astype(BF)
        pg_ref[...] = pg
        sum_ref[...] = fold8(pg.astype(F32))


def pre_grads(mgrad, wd_own, wd_oth, dg_own, dg_oth):
    rows, width = mgrad.shape
    ff = wd_own.shape[0]
    chunk = 256
    sds = jax.ShapeDtypeStruct
    wspec = pl.BlockSpec((chunk, width), lambda i: (i, 0))
    cspec = pl.BlockSpec((rows, chunk), lambda i: (0, i))
    sspec = pl.BlockSpec((8, chunk), lambda i: (0, i))
    return pl.pallas_call(
        pre_kernel,
        grid=(ff // chunk,),
        in_specs=[fixed(mgrad.shape), wspec, wspec, cspec, cspec],
        out_specs=[cspec, cspec, sspec, sspec],
        out_shape=[sds((rows, ff), BF), sds((rows, ff), BF), sds((8, ff), F32), sds((8, ff), F32)],
        compiler_params=params(40),
        name="pre_grads",
    )(mgrad, wd_own, wd_oth, dg_own, dg_oth)


def wgrad_kernel(groups, per_group, has_recv, lhs_ref, rhs_ref, *refs):
    out_ref = refs[-1]
    full = mm(lhs_ref[...], rhs_ref[...], TN)
    size = full.shape[0] // (groups * per_group)
    for g in range(groups):
        for k in range(per_group):
            first = (g * per_group + k) * size
            piece = full[first : first + size]
            if has_recv:
                piece = piece + refs[0][k, g].astype(F32)
            out_ref[k, g] = piece.astype(BF)


def wgrad(lhs, rhs, dp, plane, recv=None):
    rows, m = lhs.shape
    n = rhs.shape[1]
    outer = dp // plane
    steps = outer
    while (m // steps) % 128:
        steps //= 2
    groups = outer // steps
    size = m // dp
    spec = pl.BlockSpec((plane, groups, size, n), lambda i: (0, i, 0, 0))
    extra = [] if recv is None else [recv]
    return pl.pallas_call(
        functools.partial(wgrad_kernel, groups, plane, recv is not None),
        grid=(steps,),
        in_specs=[pl.BlockSpec((rows, m // steps), lambda i: (0, i)), fixed(rhs.shape)] + [spec] * len(extra),
        out_specs=spec,
        out_shape=jax.ShapeDtypeStruct((plane, outer, size, n), BF),
        compiler_params=params(40),
        name="wgrad",
    )(lhs, rhs, *extra)


def attn_wgrad_kernel(outer, plane, has_recv, x_ref, dqkv_ref, ctx_ref, agrad_ref, *refs):
    out_ref = refs[-1]

    def put(k, g, s, first, piece):
        last = first + piece.shape[0]
        if has_recv:
            piece = piece + refs[0][k, g, s, first:last, :].astype(F32)
        out_ref[k, g, s, first:last, :] = piece.astype(BF)

    cols = dqkv_ref.shape[2]
    size = x_ref.shape[1] // (outer * plane)
    for s in range(3):
        full = mm(x_ref[...], dqkv_ref[s], TN)
        for g in range(outer):
            for k in range(plane):
                first = (g * plane + k) * size
                put(k, g, s, 0, full[first : first + size])
    full = mm(ctx_ref[...], agrad_ref[...], TN)
    size = ctx_ref.shape[1] // (outer * plane)
    for g in range(outer):
        for k in range(plane):
            first = (g * plane + k) * size
            for c in range(2):
                put(k, g, 3, c * size, full[first : first + size, c * cols : (c + 1) * cols])


def attn_wgrad(x_low, dqkv, ctx, agrad, dp, plane, recv=None):
    size = x_low.shape[1] // dp
    cols = dqkv.shape[2]
    outer = dp // plane
    extra = [] if recv is None else [recv]
    return pl.pallas_call(
        functools.partial(attn_wgrad_kernel, outer, plane, recv is not None),
        in_specs=[VMEM_SPEC] * (4 + len(extra)),
        out_specs=VMEM_SPEC,
        out_shape=jax.ShapeDtypeStruct((plane, outer, 4, size, cols), BF),
        compiler_params=params(40),
        name="attn_wgrad",
    )(x_low, dqkv, ctx, agrad, *extra)


def mid_kernel(
    pg_own_ref, pg_oth_ref, ograd_ref, normed_ref, inv_ref, wu_own_ref, wu_oth_ref, wo_own_ref, wo_oth_ref, ga_ref,
    migrad_ref, agrad_ref, cg_own_ref, cg_oth_ref, sums_ref,
):
    step = pl.program_id(0)
    e = mm(pg_own_ref[...], wu_own_ref[...], NT) + mm(pg_oth_ref[...], wu_oth_ref[...], NT) + ograd_ref[...]
    normed = normed_ref[...]
    migrad = normalize_back(e * ga_ref[...], normed, inv_ref[...])
    migrad_ref[...] = migrad
    agrad = migrad.astype(BF)
    agrad_ref[...] = agrad
    cg_own_ref[...] = mm(agrad, wo_own_ref[...], NT).astype(BF)
    cg_oth_ref[...] = mm(agrad, wo_oth_ref[...], NT).astype(BF)
    part = jnp.stack([fold8(e * normed), fold8(e), fold8(agrad.astype(F32))])

    @pl.when(step == 0)
    def _():
        sums_ref[...] = part

    @pl.when(step > 0)
    def _():
        sums_ref[...] += part


def mid_grads(pg_own, pg_oth, ograd, normed, inv, wu_own, wu_oth, wo_own, wo_oth, ga):
    rows, width = ograd.shape
    ff = pg_own.shape[1]
    cols = wo_own.shape[0]
    block = 256
    row_block = lambda n: pl.BlockSpec((block, n), lambda i: (i, 0))
    resident = (wu_own, wu_oth, wo_own, wo_oth, ga)
    sds = jax.ShapeDtypeStruct
    return pl.pallas_call(
        mid_kernel,
        grid=(rows // block,),
        in_specs=[row_block(ff), row_block(ff), row_block(width), row_block(width), row_block(1)]
        + [fixed(a.shape) for a in resident],
        out_specs=[row_block(width), row_block(width), row_block(cols), row_block(cols), fixed((3, 8, width))],
        out_shape=[
            sds((rows, width), F32), sds((rows, width), BF), sds((rows, cols), BF), sds((rows, cols), BF),
            sds((3, 8, width), F32),
        ],
        compiler_params=params(40),
        name="mid_grads",
    )(pg_own, pg_oth, ograd, normed, inv, *resident)


def attend_back_kernel(seqs, qkv_ref, prob_ref, cg_ref, dqkv_ref, sums_ref):
    scale_a, scale_b = half_masks(LEN, HD**-0.5)
    one_a, one_b = half_masks(LEN)
    sums = [[], []]
    for j in range(cg_ref.shape[1] // PAIR):
        cols = slice(j * PAIR, (j + 1) * PAIR)
        col_sums = [0.0, 0.0]
        for s in range(seqs):
            rows = slice(s * LEN, (s + 1) * LEN)
            q2, k2, v2, g2 = qkv_ref[0, rows, cols], qkv_ref[1, rows, cols], qkv_ref[2, rows, cols], cg_ref[rows, cols]
            qcat = jnp.concatenate([q2 * scale_a, q2 * scale_b], axis=0)
            kcat = jnp.concatenate([k2 * scale_a, k2 * scale_b], axis=0)
            vcat = jnp.concatenate([v2 * one_a, v2 * one_b], axis=0)
            gcat = jnp.concatenate([g2 * one_a, g2 * one_b], axis=0)
            probs = prob_ref[s, j]
            dprobs = mm(g2, vcat, NT)
            tall, flat = [], []
            for h in range(2):
                p = probs[:, h * LEN : (h + 1) * LEN]
                dp = dprobs[:, h * LEN : (h + 1) * LEN]
                ds = (p * (dp - jnp.sum(p * dp, axis=1, keepdims=True))).astype(BF)
                flat.append(ds)
                tall.append(p.astype(BF))
            dq = mm(jnp.concatenate(flat, axis=1), kcat).astype(BF)
            dk = mm(jnp.concatenate(flat, axis=0), qcat, TN).astype(BF)
            dv = mm(jnp.concatenate(tall, axis=0), gcat, TN).astype(BF)
            dqkv_ref[0, rows, cols] = dq
            dqkv_ref[1, rows, cols] = dk
            dqkv_ref[2, rows, cols] = dv
            col_sums[0] += fold8(dq.astype(F32))
            col_sums[1] += fold8(dv.astype(F32))
        sums[0].append(col_sums[0])
        sums[1].append(col_sums[1])
    part = jnp.stack([jnp.concatenate(sums[0], axis=1), jnp.concatenate(sums[1], axis=1)])
    step = pl.program_id(0)

    @pl.when(step == 0)
    def _():
        sums_ref[...] = part

    @pl.when(step > 0)
    def _():
        sums_ref[...] += part


def attend_back(qkv, probs, cgrad):
    rows, cols = cgrad.shape
    seqs = 2
    block = seqs * LEN
    pairs = cols // PAIR
    sds = jax.ShapeDtypeStruct
    spec3 = pl.BlockSpec((3, block, cols), lambda i: (0, i, 0))
    return pl.pallas_call(
        functools.partial(attend_back_kernel, seqs),
        grid=(rows // block,),
        in_specs=[
            spec3,
            pl.BlockSpec((seqs, pairs, LEN, 2 * LEN), lambda i: (i, 0, 0, 0)),
            pl.BlockSpec((block, cols), lambda i: (i, 0)),
        ],
        out_specs=[spec3, fixed((2, 8, cols))],
        out_shape=[sds((3, rows, cols), BF), sds((2, 8, cols), F32)],
        compiler_params=params(40),
        name="attend_back",
    )(qkv, probs, cgrad)


def token_kernel(own_ref, oth_ref, migrad_ref, w_own_ref, w_oth_ref, out_ref):
    total = migrad_ref[...]
    for d_ref, w_ref in ((own_ref, w_own_ref), (oth_ref, w_oth_ref)):
        for s in range(3):
            total = total + mm(d_ref[s], w_ref[s], NT)
    out_ref[...] = total


def token_grads(dqkv_own, dqkv_oth, migrad, w_own, w_oth):
    rows, width = migrad.shape
    cols = dqkv_own.shape[2]
    block = 256
    spec3 = pl.BlockSpec((3, block, cols), lambda i: (0, i, 0))
    row_spec = pl.BlockSpec((block, width), lambda i: (i, 0))
    return pl.pallas_call(
        token_kernel,
        grid=(rows // block,),
        in_specs=[spec3, spec3, row_spec, fixed(w_own.shape), fixed(w_oth.shape)],
        out_specs=row_spec,
        out_shape=jax.ShapeDtypeStruct((rows, width), F32),
        compiler_params=params(40),
        name="token_grads",
    )(dqkv_own, dqkv_oth, migrad, w_own, w_oth)


def per_device(
    tokens, timesteps, src_len, tgt_len, sample_weight, w_qkv, bias_qv, w_out, bias_out, gain_attn, shift_attn,
    w_up, bias_up, w_down, bias_down, gain_mlp, shift_mlp, cotangent,
):
    rows, width = tokens.shape
    dp = lax.axis_size("dp")
    mp_index = lax.axis_index("mp")
    seqs = rows // LEN
    cols = bias_qv.shape[1]
    ff = bias_up.shape[0]
    plane = 4

    def swap(value):
        return lax.ppermute(value, "mp", [(0, 1), (1, 0)])

    def mine(value):
        return lax.dynamic_slice_in_dim(value, mp_index * seqs, seqs)

    table = time_table(mine(timesteps), width)
    src = mine(src_len)
    lengths = src + mine(tgt_len)
    weight = mine(sample_weight)
    qkv_oth_w = swap(w_qkv)
    biases = jnp.concatenate([bias_qv.reshape(-1), bias_up])
    biases_oth = swap(biases)
    bqv_oth, bu_oth = biases_oth[: 2 * cols].reshape(2, cols), biases_oth[2 * cols :].reshape(1, ff)
    wo_oth = swap(w_out)
    wu_oth = swap(w_up)
    wd_oth = swap(w_down)
    row = lambda vec: vec.reshape(1, -1)

    qkv_own, prob_own, ctx_own, x_low = attend(tokens, table, lengths, w_qkv, bias_qv.astype(F32), True)
    qkv_oth, prob_oth, ctx_oth = attend(tokens, table, lengths, qkv_oth_w, bqv_oth.astype(F32), False)
    (normed, inv, mid_low, hid_own, hid_oth, dg_own, dg_oth, layer_out, ograd, mgrad, sums_mlp) = mlp(
        src, lengths, weight, tokens, table, ctx_own, ctx_oth, cotangent, w_out, wo_oth, row(bias_out),
        row(gain_attn), row(shift_attn), w_up, wu_oth, row(bias_up), bu_oth, w_down, wd_oth, row(bias_down),
        row(gain_mlp), row(shift_mlp),
    )
    down_recv = swap(wgrad(hid_oth, mgrad, dp, plane))
    pg_own, pg_oth, sum_up_own, sum_up_oth = pre_grads(mgrad, w_down, wd_oth, dg_own, dg_oth)
    down_part = wgrad(hid_own, mgrad, dp, plane, down_recv)
    up_recv = swap(wgrad(mid_low, pg_oth, dp, plane))
    migrad, agrad, cg_own, cg_oth, sums_mid = mid_grads(
        pg_own, pg_oth, ograd, normed, inv, w_up, wu_oth, w_out, wo_oth, row(gain_attn)
    )
    up_part = wgrad(mid_low, pg_own, dp, plane, up_recv)
    dqkv_oth, sum_qv_oth = attend_back(qkv_oth, prob_oth, cg_oth)
    attn_recv = swap(attn_wgrad(x_low, dqkv_oth, ctx_oth, agrad, dp, plane))
    dqkv_own, sum_qv_own = attend_back(qkv_own, prob_own, cg_own)
    attn_part = attn_wgrad(x_low, dqkv_own, ctx_own, agrad, dp, plane, attn_recv)
    tokens_grad = token_grads(dqkv_own, dqkv_oth, migrad, w_qkv, qkv_oth_w)

    in_plane = [[base + k for k in range(plane)] for base in range(0, dp, plane)]
    across = [[base * plane + k for base in range(dp // plane)] for k in range(plane)]

    def scatter(part):
        part = lax.psum_scatter(part, "dp", scatter_dimension=0, axis_index_groups=in_plane)
        return lax.psum_scatter(part, "dp", scatter_dimension=0, axis_index_groups=across).astype(F32)

    grad_w_down = scatter(down_part)
    grad_w_up = scatter(up_part)
    attn_out = scatter(attn_part)
    grad_w_qkv = attn_out[:3]
    half = attn_out.shape[1] // 2
    grad_w_out = jnp.concatenate([attn_out[3, :half], attn_out[3, half:]], axis=1)

    fold = lambda value: jnp.sum(value, axis=-2)
    shared = jnp.concatenate([fold(sums_mid), fold(sums_mlp)]).reshape(-1)
    oth = jnp.concatenate([fold(sum_up_oth), fold(sum_qv_oth).reshape(-1)])
    own = jnp.concatenate([fold(sum_up_own), fold(sum_qv_own).reshape(-1)])
    vec = jnp.concatenate([shared, own]) + swap(jnp.concatenate([shared, oth]))
    bit = 1
    while bit < dp:
        vec = vec + lax.ppermute(vec, "dp", [(i, i ^ bit) for i in range(dp)])
        bit *= 2
    shared = vec[: 6 * width].reshape(6, width)
    grad_rows = jnp.concatenate([shared[0:2], shared[3:6]])
    grad_bias_out = shared[2]
    grad_bias_up = vec[6 * width : 6 * width + ff]
    grad_bias_qv = vec[6 * width + ff :].reshape(2, cols)
    return (
        layer_out, tokens_grad, grad_w_qkv, grad_w_out, grad_w_up, grad_w_down,
        grad_bias_qv, grad_bias_up, grad_bias_out, grad_rows,
    )


def solution(mesh):
    in_specs = (
        P(("dp", "mp"), None), P("dp"), P("dp"), P("dp"), P("dp"),
        P(None, None, "mp"), P(None, "mp"), P("mp", None), P(), P(), P(),
        P(None, "mp"), P("mp"), P("mp", None), P(), P(), P(), P(("dp", "mp"), None),
    )
    out_specs = (
        P(("dp", "mp"), None), P(("dp", "mp"), None), P(None, "dp", "mp"), P(("mp", "dp"), None),
        P("dp", "mp"), P(("mp", "dp"), None), P(None, "mp"), P("mp"), P(), P(),
    )
    return jax.shard_map(per_device, mesh=mesh, in_specs=in_specs, out_specs=out_specs, check_vma=False)
```

```python
import functools
import math

import jax
import jax.numpy as jnp
from jax import lax
from jax.experimental import pallas as pl
from jax.experimental.pallas import tpu as pltpu
from jax.sharding import PartitionSpec as P

HD = 64
LEN = 128
PAIR = 2 * HD
NORM_EPS = 1e-05
MASK_FILL = -1e30
BF = jnp.bfloat16
F32 = jnp.float32
MIB = 1 << 20
ROWS = 16
SOFT = 32
BLOCK = 512
MLP_BLOCK = 512
AHEAD = 2

NN = (((1,), (0,)), ((), ()))
NT = (((1,), (1,)), ((), ()))
TN = (((0,), (0,)), ((), ()))

SPECS = {
    "v": pl.BlockSpec(memory_space=pltpu.VMEM),
    "s": pl.BlockSpec(memory_space=pltpu.SMEM),
    "h": pl.BlockSpec(memory_space=pltpu.HBM),
}


def mm(a, b, dims=NN):
    return lax.dot_general(a, b, dims, preferred_element_type=F32)


def params(mib):
    return pltpu.CompilerParams(vmem_limit_bytes=mib * MIB)


def local_call(kernel, out_shape, name, ins, outs, scratch=(), mib=16, flops=0):
    forced = {"v": pltpu.VMEM, "h": pltpu.HBM}

    def call(*args):
        args = [pltpu.with_memory_space_constraint(a, pltpu.HBM) if c == "h" else a for a, c in zip(args, ins)]
        return pl.pallas_call(
            kernel,
            in_specs=[SPECS[c] for c in ins],
            out_specs=[SPECS[c] for c in outs],
            out_shape=[forced[c](a.shape, a.dtype) for a, c in zip(out_shape, outs)],
            scratch_shapes=list(scratch),
            compiler_params=params(mib),
            cost_estimate=pl.CostEstimate(flops=flops, bytes_accessed=0, transcendentals=0) if flops else None,
            name=name,
        )(*args)

    return call


class Copies:
    def __init__(self, sems):
        self.sems = sems
        self.started = []
        self.waiting = {}

    def start(self, src, dst, key=None):
        copy = pltpu.make_async_copy(src, dst, self.sems.at[len(self.started)])
        copy.start()
        self.started.append(copy)
        self.waiting.setdefault(key, []).append(copy)

    def wait(self, key=None):
        for copy in self.waiting.pop(key, ()):
            copy.wait()

    def wait_all(self):
        for key in list(self.waiting):
            self.wait(key)


def time_table(timesteps, width):
    half_width = width // 2
    frequency = jnp.exp(-math.log(10000.0) * jnp.arange(half_width, dtype=F32) / half_width)
    angles = timesteps.astype(F32)[:, None] * frequency[None, :]
    return jnp.concatenate([jnp.sin(angles), jnp.cos(angles)], axis=1)


def half_masks(rows, value=1.0):
    lane = lax.broadcasted_iota(jnp.int32, (rows, PAIR), 1)
    first = jnp.where(lane < HD, value, 0.0).astype(BF)
    second = jnp.where(lane < HD, 0.0, value).astype(BF)
    return first, second


def fold8(value):
    rows, cols = value.shape
    return jnp.sum(value.reshape(rows // 8, 8, cols), axis=0)


def side_by_side(ref):
    return jnp.concatenate([ref[i] for i in range(ref.shape[0])], axis=1)


def attend_kernel(first, meta_ref, *refs):
    if first:
        (tok_hbm, table_ref, w_hbm, bias_ref, qkv_out, prob_out, ctx_ref, ctx_out, x_ref, x_out,
         qkv_ref, prob_ref, sems, tok_ref, w_ref) = refs
    else:
        x_ref, w_ref, bias_ref, qkv_out, prob_out, ctx_ref, ctx_out, qkv_ref, prob_ref, sems = refs
    copies = Copies(sems)
    seqs = x_ref.shape[0] // LEN
    cols = w_ref.shape[2]
    base = lax.axis_index("mp") * seqs
    if first:
        for i in range(3):
            copies.start(w_hbm.at[i], w_ref.at[i], "w")
        for start in range(0, x_ref.shape[0], BLOCK):
            rows = slice(start, start + BLOCK)
            copies.start(tok_hbm.at[rows, :], tok_ref.at[rows, :], start)
        copies.wait(0)
    bias_q = bias_ref[0:1, :].astype(F32)
    bias_v = bias_ref[1:2, :].astype(F32)
    scale_a, scale_b = half_masks(LEN, HD**-0.5)
    one_a, one_b = half_masks(LEN)
    key_pos = lax.broadcasted_iota(jnp.int32, (SOFT, LEN), 1)

    def project(start):
        if first:
            copies.wait(start)
            for s in range(start // LEN, (start + BLOCK) // LEN):
                row = table_ref[pl.ds(base + s, 1), :]
                for r in range(s * LEN, (s + 1) * LEN, ROWS):
                    x_ref[r : r + ROWS, :] = (tok_ref[r : r + ROWS, :].astype(F32) + row).astype(BF)
        rows = slice(start, start + BLOCK)
        full = mm(x_ref[rows, :], w)
        qkv_ref[rows, :cols] = (full[:, :cols] + bias_q).astype(BF)
        qkv_ref[rows, cols : 2 * cols] = full[:, cols : 2 * cols].astype(BF)
        qkv_ref[rows, 2 * cols :] = (full[:, 2 * cols :] + bias_v).astype(BF)
        copies.start(qkv_ref.at[rows, :], qkv_out.at[rows, :])
        if first:
            copies.start(x_ref.at[rows, :], x_out.at[rows, :])

    def score(unit):
        s, j = unit
        rows = slice(s * LEN, (s + 1) * LEN)
        q2 = qkv_ref[rows, j * PAIR : (j + 1) * PAIR]
        k2 = qkv_ref[rows, cols + j * PAIR : cols + (j + 1) * PAIR]
        return mm(q2, jnp.concatenate([k2 * scale_a, k2 * scale_b], axis=0), NT)

    def finish(unit, scores):
        s, j = unit
        rows = slice(s * LEN, (s + 1) * LEN)
        live = key_pos < meta_ref[1, base + s].astype(jnp.int32)
        low = []
        for r in range(0, LEN, SOFT):
            halves = []
            for h in range(2):
                part = jnp.where(live, scores[r : r + SOFT, h * LEN : (h + 1) * LEN], MASK_FILL)
                e = jnp.exp(part - jnp.max(part, axis=1, keepdims=True))
                halves.append(e * (1.0 / jnp.sum(e, axis=1, keepdims=True)))
            probs = jnp.concatenate(halves, axis=1)
            prob_ref[s, j, r : r + SOFT, :] = probs
            low.append(probs.astype(BF))
        v2 = qkv_ref[rows, 2 * cols + j * PAIR : 2 * cols + (j + 1) * PAIR]
        vcat = jnp.concatenate([v2 * one_a, v2 * one_b], axis=0)
        ctx_ref[rows, j * PAIR : (j + 1) * PAIR] = mm(jnp.concatenate(low, axis=0), vcat).astype(BF)

    count = x_ref.shape[0]
    copies.wait("w")
    w = side_by_side(w_ref)
    project(0)
    for start in range(0, count, BLOCK):
        if start + BLOCK < count:
            project(start + BLOCK)
        units = [(s, j) for s in range(start // LEN, (start + BLOCK) // LEN) for j in range(cols // PAIR)]
        pending = [score(u) for u in units[:AHEAD]]
        for i, unit in enumerate(units):
            if i + AHEAD < len(units):
                pending.append(score(units[i + AHEAD]))
            finish(unit, pending.pop(0))
            if unit[1] == cols // PAIR - 1:
                copies.start(prob_ref.at[unit[0]], prob_out.at[unit[0]])
        rows = slice(start, start + BLOCK)
        copies.start(ctx_ref.at[rows, :], ctx_out.at[rows, :])
    copies.wait_all()


def attend(meta, x_args, w_half, bias_half):
    first = len(x_args) == 2
    rows, width = x_args[0].shape
    cols = w_half.shape[2]
    sds = jax.ShapeDtypeStruct
    shapes = [
        sds((rows, 3 * cols), BF),
        sds((rows // LEN, cols // PAIR, LEN, 2 * LEN), F32),
        sds((rows, cols), BF),
        sds((rows, cols), BF),
        sds((rows, width), BF),
        sds((rows, width), BF),
    ]
    if not first:
        shapes = shapes[:4]
    scratch = [
        pltpu.VMEM(shapes[0].shape, BF),
        pltpu.VMEM(shapes[1].shape, F32),
        pltpu.SemaphoreType.DMA((4 * rows // BLOCK + rows // LEN + 3,)),
    ]
    if first:
        scratch += [pltpu.VMEM((rows, width), BF), pltpu.VMEM(w_half.shape, BF)]
    return local_call(
        functools.partial(attend_kernel, first), shapes, "attend",
        "shvhv" if first else "svvv", "hhvhvh"[: len(shapes)], scratch, 20,
    )(meta, *x_args, w_half, bias_half)


def normalize(value):
    centred = value - jnp.mean(value, axis=1, keepdims=True)
    inv_std = lax.rsqrt(jnp.mean(centred * centred, axis=1, keepdims=True) + NORM_EPS)
    return centred * inv_std, inv_std


def normalize_back(scaled, normed, inv_std):
    return inv_std * (
        scaled
        - jnp.mean(scaled, axis=1, keepdims=True)
        - normed * jnp.mean(scaled * normed, axis=1, keepdims=True)
    )


def gelu_pair(v):
    cdf = 0.5 + 0.5 * lax.erf(v * math.sqrt(0.5))
    return v * cdf, cdf + v * jnp.exp(v * v * -0.5) * (1.0 / math.sqrt(2.0 * math.pi))


def mlp_kernel(
    meta_ref, tok_ref, table_ref, ctx_own_ref, ctx_oth_ref, cot_hbm,
    wo_own_ref, wo_oth_ref, bo_ref, ga_ref, sa_ref,
    wu_own_ref, wu_oth_ref, bu_own_ref, bu_oth_ref, wd_own_ref, wd_oth_ref, bd_ref, gm_ref, sm_ref,
    normed_hbm, inv_ref, mid_ref, hid_own_ref, hid_oth_ref, dg_own_ref, dg_oth_ref,
    out_hbm, ograd_ref, mgrad_ref, sums_ref, normed_ref, out_ref, cot_ref, sems,
):
    count = tok_ref.shape[0]
    base = lax.axis_index("mp") * (count // LEN)
    copies = Copies(sems)
    for start in range(0, count, MLP_BLOCK):
        copies.start(cot_hbm.at[start : start + MLP_BLOCK, :], cot_ref.at[start : start + MLP_BLOCK, :], start)
    wo = jnp.concatenate([wo_own_ref[...], wo_oth_ref[...]], axis=0)
    halves = (
        (wu_own_ref, bu_own_ref, wd_own_ref, hid_own_ref, dg_own_ref),
        (wu_oth_ref, bu_oth_ref, wd_oth_ref, hid_oth_ref, dg_oth_ref),
    )

    def first_norm(start):
        rows = slice(start, start + MLP_BLOCK)
        attn_out = mm(jnp.concatenate([ctx_own_ref[rows, :], ctx_oth_ref[rows, :]], axis=1), wo)
        for r in range(0, MLP_BLOCK, ROWS):
            part = slice(start + r, start + r + ROWS)
            table_row = table_ref[pl.ds(base + (start + r) // LEN, 1), :]
            start_x = tok_ref[part, :].astype(F32) + table_row
            normed, inv = normalize(start_x + attn_out[r : r + ROWS] + bo_ref[...])
            normed_ref[part, :] = normed
            inv_ref[part, :] = inv
            mid_x = normed * ga_ref[...] + sa_ref[...]
            mid_ref[part, :] = mid_x.astype(BF)
        copies.start(normed_ref.at[rows, :], normed_hbm.at[rows, :])

    def up(unit):
        start, half = unit
        return mm(mid_ref[start : start + MLP_BLOCK, :], halves[half][0][...])

    def activate(unit, pre):
        start, half = unit
        _, bu_ref, wd_ref, hid_ref, dg_ref = halves[half]
        bias = jnp.concatenate([bu_ref[i : i + 1, :] for i in range(2, bu_ref.shape[0])], axis=1).astype(F32)
        for r in range(0, MLP_BLOCK, ROWS):
            part = slice(start + r, start + r + ROWS)
            hidden, slope = gelu_pair(pre[r : r + ROWS] + bias)
            hid_ref[part, :] = hidden.astype(BF)
            dg_ref[part, :] = slope.astype(BF)
        return mm(hid_ref[start : start + MLP_BLOCK, :], wd_ref[...])

    pos = lax.broadcasted_iota(jnp.int32, (ROWS, 1), 0)

    def second_norm(start, mlp_out, sums):
        copies.wait(start)
        for r in range(0, MLP_BLOCK, ROWS):
            part = slice(start + r, start + r + ROWS)
            seq = base + (start + r) // LEN
            mid_x = normed_ref[part, :] * ga_ref[...] + sa_ref[...]
            normed2, inv2 = normalize(mid_x + (mlp_out[r : r + ROWS] + bd_ref[...]))
            out_ref[part, :] = normed2 * gm_ref[...] + sm_ref[...]
            here = pos + (start + r) % LEN
            inside = (here >= meta_ref[0, seq].astype(jnp.int32)) & (here < meta_ref[1, seq].astype(jnp.int32))
            e = cot_ref[part, :].astype(F32) * jnp.where(inside, meta_ref[2, seq], 0.0)
            ograd = normalize_back(e * gm_ref[...], normed2, inv2)
            ograd_ref[part, :] = ograd
            mgrad = ograd.astype(BF)
            mgrad_ref[part, :] = mgrad
            new = [fold8(mgrad.astype(F32)), fold8(e * normed2), fold8(e)]
            sums = new if sums is None else [x + y for x, y in zip(sums, new)]
        rows = slice(start, start + MLP_BLOCK)
        copies.start(out_ref.at[rows, :], out_hbm.at[rows, :])
        return sums

    sums = None
    first_norm(0)
    units = [(start, half) for start in range(0, count, MLP_BLOCK) for half in range(2)]
    ready = up(units[0])
    waiting = None
    total = None
    for i, unit in enumerate(units):
        start, half = unit
        pre = ready
        if half == 0 and start + MLP_BLOCK < count:
            first_norm(start + MLP_BLOCK)
        if i + 1 < len(units):
            ready = up(units[i + 1])
        down = activate(unit, pre)
        if half == 0:
            if waiting is not None:
                sums = second_norm(*waiting, sums)
            total = down
        else:
            waiting = (start, total + down)
    sums = second_norm(*waiting, sums)
    sums_ref[...] = jnp.stack(sums)
    copies.wait_all()


def mlp(meta, tokens, table, ctx_own, ctx_oth, cot, wo_own, wo_oth, bo, ga, sa,
        wu_own, wu_oth, bu_own, bu_oth, wd_own, wd_oth, bd, gm, sm):
    rows, width = tokens.shape
    ff = wu_own.shape[1]
    sds = jax.ShapeDtypeStruct
    args = (meta, tokens, table, ctx_own, ctx_oth, cot, wo_own, wo_oth, bo, ga, sa,
            wu_own, wu_oth, bu_own, bu_oth, wd_own, wd_oth, bd, gm, sm)
    return local_call(
        mlp_kernel,
        [
            sds((rows, width), F32), sds((rows, 1), F32), sds((rows, width), BF),
            sds((rows, ff), BF), sds((rows, ff), BF), sds((rows, ff), BF), sds((rows, ff), BF),
            sds((rows, width), F32), sds((rows, width), F32), sds((rows, width), BF),
            sds((3, 8, width), F32),
        ],
        "mlp",
        "svvvvh" + "v" * 14,
        "hvvvvvvhvvv",
        [pltpu.VMEM((rows, width), F32)] * 2 + [pltpu.VMEM((rows, width), BF), pltpu.SemaphoreType.DMA((4 * rows // MLP_BLOCK,))],
        22,
    )(*args)


def pre_kernel(mgrad_ref, wd_own_ref, wd_oth_ref, dg_own_ref, dg_oth_ref, pg_own_ref, pg_oth_ref, sum_own_ref, sum_oth_ref):
    halves = ((wd_oth_ref, dg_oth_ref, pg_oth_ref, sum_oth_ref), (wd_own_ref, dg_own_ref, pg_own_ref, sum_own_ref))
    units = [(h, c) for h in halves for c in range(0, wd_own_ref.shape[0], 512)]

    def product(unit):
        (wd_ref, _, _, _), c = unit
        return mm(mgrad_ref[...], wd_ref[c : c + 512, :], NT)

    ready = product(units[0])
    for i, ((_, dg_ref, pg_ref, sum_ref), c) in enumerate(units):
        full = ready
        if i + 1 < len(units):
            ready = product(units[i + 1])
        sums = None
        for r in range(0, full.shape[0], 32):
            pg = (full[r : r + 32] * dg_ref[r : r + 32, c : c + 512].astype(F32)).astype(BF)
            pg_ref[r : r + 32, c : c + 512] = pg
            new = fold8(pg.astype(F32))
            sums = new if sums is None else sums + new
        sum_ref[:, c : c + 512] = sums


def pre_grads(mgrad, wd_own, wd_oth, dg_own, dg_oth):
    rows = mgrad.shape[0]
    ff = wd_own.shape[0]
    sds = jax.ShapeDtypeStruct
    return local_call(
        pre_kernel,
        [sds((rows, ff), BF), sds((rows, ff), BF), sds((8, ff), F32), sds((8, ff), F32)],
        "pre_grads", "vvvvv", "vvvv",
    )(mgrad, wd_own, wd_oth, dg_own, dg_oth)


def weight_pieces(lhs_ref, rhs_ref, size, chunk=384):
    m = lhs_ref.shape[1]
    ready = mm(lhs_ref[:, :chunk], rhs_ref[...], TN)
    for start in range(0, m, chunk):
        full = ready
        if start + chunk < m:
            ready = mm(lhs_ref[:, start + chunk : start + 2 * chunk], rhs_ref[...], TN)
        for first in range(0, chunk, size):
            yield (start + first) // size, full[first : first + size]


def attn_pieces(x_ref, dqkv_ref, ctx_ref, agrad_ref, size):
    cols = ctx_ref.shape[1]
    half = size // 2
    out_full = mm(ctx_ref[...], agrad_ref[...], TN)
    for index, qkv in weight_pieces(x_ref, dqkv_ref, size):
        rows = out_full[index * half : (index + 1) * half]
        blocks = [(0, qkv[:, i * cols : (i + 1) * cols], i) for i in range(3)]
        yield index, blocks + [(c * half, rows[:, c * cols : (c + 1) * cols], 3) for c in range(2)]


def send_kernel(attn, *refs):
    out_ref = refs[-1]
    plane, size = out_ref.shape[0], out_ref.shape[-2]
    if attn:
        for index, blocks in attn_pieces(*refs[:-1], size):
            for first, value, i in blocks:
                out_ref[index % plane, index // plane, i, first : first + value.shape[0], :] = value.astype(BF)
    else:
        for index, value in weight_pieces(*refs[:-1], size):
            out_ref[index % plane, index // plane] = value.astype(BF)


def own_sum(attn, recv_ref, index, held_ref, slot, value):
    plane = recv_ref.shape[0]
    k, g = index % plane, index // plane
    if attn:
        for first, block, i in value:
            rows = slice(first, first + block.shape[0])
            held_ref[slot, k, i, rows, :] = block
        held_ref[slot, k] = held_ref[slot, k] + recv_ref[k, g].astype(F32)
    else:
        held_ref[slot, k] = value + recv_ref[k, g].astype(F32)


def total_kernel(attn, *refs):
    *ins, recv_ref, out_ref, held_ref = refs
    plane, size = recv_ref.shape[0], recv_ref.shape[-2]
    source = attn_pieces(*ins, size) if attn else weight_pieces(*ins, size)
    for index, value in source:
        slot = (index // plane) % held_ref.shape[0]
        own_sum(attn, recv_ref, index, held_ref, slot, value)
        out_ref[index % plane, index // plane] = held_ref[slot, index % plane].astype(BF)


def split_kernel(attn, *refs):
    *ins, recv_ref, sa_ref, ka_ref, sb_ref, kb_ref, held_ref = refs
    plane, size = recv_ref.shape[0], recv_ref.shape[-2]
    me = lax.axis_index("dp") % plane
    source = attn_pieces(*ins, size) if attn else weight_pieces(*ins, size)
    for index, value in source:
        g = index // plane
        slot = g % held_ref.shape[0]
        own_sum(attn, recv_ref, index, held_ref, slot, value)
        if index % plane == plane - 1:
            for far in range(plane):
                y, x = divmod(far, 2)
                piece = held_ref[slot, me ^ far].astype(BF)
                if attn:
                    one, two = piece[:2], piece[2:]
                else:
                    half = piece.shape[1] // 2
                    one, two = piece[:, :half], piece[:, half:]
                (sa_ref if x else ka_ref)[y, g] = one
                (sb_ref if y else kb_ref)[x, g] = two


def weight_grad(ins, dp, plane, recv=None, split=False):
    attn = len(ins) == 4
    size = ins[0].shape[1] // dp
    outer = dp // plane
    piece = (4, size, ins[2].shape[1]) if attn else (size, ins[1].shape[1])
    half = (2,) + piece[1:] if attn else (size, piece[1] // 2)
    sds = jax.ShapeDtypeStruct
    held = [pltpu.VMEM((2, plane) + piece, F32)]
    if recv is None:
        kernel, shapes, scratch, args = send_kernel, [sds((plane, outer) + piece, BF)], [], ins
    elif split:
        kernel, shapes, scratch, args = split_kernel, [sds((2, outer) + half, BF)] * 4, held, (*ins, recv)
    else:
        kernel, shapes, scratch, args = total_kernel, [sds((plane, outer) + piece, BF)], held, (*ins, recv)
    return local_call(
        functools.partial(kernel, attn), shapes, "attn_wgrad" if attn else "wgrad", "v" * len(args), "v" * len(shapes), scratch
    )(*args)


def fold_kernel(ka_ref, ra_ref, kb_ref, rb_ref, sa_ref, ta_ref, sb_ref, tb_ref):
    for k_ref, r_ref, s_ref, t_ref in ((ka_ref, ra_ref, sa_ref, ta_ref), (kb_ref, rb_ref, sb_ref, tb_ref)):
        for g in range(k_ref.shape[1]):
            s_ref[g] = (k_ref[1, g].astype(F32) + r_ref[1, g].astype(F32)).astype(BF)
            t_ref[g] = (k_ref[0, g].astype(F32) + r_ref[0, g].astype(F32)).astype(BF)


def fold_first(ka, ra, kb, rb):
    shape = jax.ShapeDtypeStruct(ka.shape[1:], BF)
    return local_call(fold_kernel, [shape] * 4, "fold_first", "vvvv", "vvvv")(ka, ra, kb, rb)


def plane_kernel(plane, ka_ref, ra_ref, kb_ref, rb_ref, send_ref, keep_ref):
    me = lax.axis_index("dp") // plane
    for far in range(ka_ref.shape[0]):
        g = me ^ far
        out_ref = send_ref if far % 2 else keep_ref
        one = (ka_ref[g].astype(F32) + ra_ref[g].astype(F32)).astype(BF)
        two = (kb_ref[g].astype(F32) + rb_ref[g].astype(F32)).astype(BF)
        if len(out_ref.shape) == 4:
            out_ref[far // 2, : one.shape[0]] = one
            out_ref[far // 2, one.shape[0] :] = two
        else:
            out_ref[far // 2, :, : one.shape[1]] = one
            out_ref[far // 2, :, one.shape[1] :] = two


def fold_second(ka, ra, kb, rb, plane):
    shape = list(ka.shape)
    shape[0] //= 2
    shape[1 if len(shape) == 4 else -1] *= 2
    return local_call(
        functools.partial(plane_kernel, plane), [jax.ShapeDtypeStruct(tuple(shape), BF)] * 2, "fold_second", "vvvv", "vv"
    )(ka, ra, kb, rb)


def outer_kernel(keep_ref, arrived_ref, send_ref, own_ref):
    send_ref[...] = (keep_ref[1].astype(F32) + arrived_ref[1].astype(F32)).astype(BF)
    own_ref[...] = keep_ref[0].astype(F32) + arrived_ref[0].astype(F32)


def fold_outer(keep, arrived):
    shape = keep.shape[1:]
    sds = jax.ShapeDtypeStruct
    return local_call(outer_kernel, [sds(shape, BF), sds(shape, F32)], "fold_outer", "vv", "vv", flops=10**12)(keep, arrived)


def last_kernel(own_ref, *refs):
    arrived = refs[:1]
    if len(own_ref.shape) == 3:
        qkv_ref, out_ref = refs[1:]
        size, cols = own_ref.shape[1:]
        for i in range(4):
            total = own_ref[i]
            for ref in arrived:
                total = total + ref[i].astype(F32)
            if i < 3:
                qkv_ref[i] = total
            else:
                out_ref[:, :cols] = total[: size // 2]
                out_ref[:, cols:] = total[size // 2 :]
    else:
        total = own_ref[...]
        for ref in arrived:
            total = total + ref[...].astype(F32)
        refs[1][...] = total


def last_sum(own, *arrived):
    sds = jax.ShapeDtypeStruct
    if own.ndim == 3:
        _, size, cols = own.shape
        shapes = [sds((3, size, cols), F32), sds((size // 2, 2 * cols), F32)]
    else:
        shapes = [sds(own.shape, F32)]
    return local_call(last_kernel, shapes, "last_sum", "vv", "v" * len(shapes))(own, *arrived)


def pack_kernel(mid_ref, mlp_ref, up_own_ref, up_oth_ref, qv_own_ref, qv_oth_ref, keep_ref, send_ref):
    width = keep_ref.shape[1]
    cols = qv_own_ref.shape[2]
    row = lambda value: jnp.sum(value, axis=0, keepdims=True)
    for out_ref, up_ref, qv_ref in ((keep_ref, up_own_ref, qv_own_ref), (send_ref, up_oth_ref, qv_oth_ref)):
        for i in range(3):
            out_ref[i : i + 1, :] = row(mid_ref[i])
            out_ref[3 + i : 4 + i, :] = row(mlp_ref[i])
        for i in range(up_ref.shape[1] // width):
            out_ref[6 + i : 7 + i, :] = row(up_ref[:, i * width : (i + 1) * width])
        for i in range(2):
            out_ref[8:9, i * cols : (i + 1) * cols] = row(qv_ref[i])
        out_ref[9:, :] = jnp.zeros((out_ref.shape[0] - 9, width), F32)


def pack_sums(sums_mid, sums_mlp, up_own, up_oth, qv_own, qv_oth):
    shape = jax.ShapeDtypeStruct((16, sums_mid.shape[2]), F32)
    return local_call(pack_kernel, [shape] * 2, "pack_sums", "v" * 6, "vv")(sums_mid, sums_mlp, up_own, up_oth, qv_own, qv_oth)


def mid_kernel(
    pg_own_ref, pg_oth_ref, ograd_ref, normed_hbm, inv_ref, wu_own_ref, wu_oth_ref, wo_own_ref, wo_oth_ref, ga_ref,
    qkv_hbm, prob_hbm, migrad_hbm, agrad_ref, cg_own_ref, cg_oth_ref, sums_ref, qkv_ref, prob_ref, migrad_ref, normed_ref, sems,
):
    def product(first):
        rows = slice(first, first + BLOCK)
        return mm(pg_own_ref[rows, :], wu_own_ref[...], NT) + mm(pg_oth_ref[rows, :], wu_oth_ref[...], NT)

    sums = None
    count = ograd_ref.shape[0]
    copies = Copies(sems)
    for first in range(0, count, BLOCK):
        rows = slice(first, first + BLOCK)
        copies.start(normed_hbm.at[rows, :], normed_ref.at[rows, :], first)
    copies.start(qkv_hbm, qkv_ref)
    copies.start(prob_hbm, prob_ref)
    cols = cg_own_ref.shape[1]
    wo = jnp.concatenate([wo_own_ref[...], wo_oth_ref[...]], axis=0)
    ready = product(0)
    for first in range(0, count, BLOCK):
        back = ready
        if first + BLOCK < count:
            ready = product(first + BLOCK)
        copies.wait(first)
        for r in range(0, BLOCK, ROWS):
            part = slice(first + r, first + r + ROWS)
            e = back[r : r + ROWS] + ograd_ref[part, :]
            normed = normed_ref[part, :]
            migrad = normalize_back(e * ga_ref[...], normed, inv_ref[part, :])
            migrad_ref[part, :] = migrad
            agrad = migrad.astype(BF)
            agrad_ref[part, :] = agrad
            new = [fold8(e * normed), fold8(e), fold8(agrad.astype(F32))]
            sums = new if sums is None else [x + y for x, y in zip(sums, new)]
        rows = slice(first, first + BLOCK)
        copies.start(migrad_ref.at[rows, :], migrad_hbm.at[rows, :])
        cgrad = mm(agrad_ref[rows, :], wo, NT).astype(BF)
        cg_own_ref[rows, :] = cgrad[:, :cols]
        cg_oth_ref[rows, :] = cgrad[:, cols:]
    sums_ref[...] = jnp.stack(sums)
    copies.wait_all()


def mid_grads(pg_own, pg_oth, ograd, normed, inv, wu_own, wu_oth, wo_own, wo_oth, ga, qkv, probs):
    rows, width = ograd.shape
    cols = wo_own.shape[0]
    sds = jax.ShapeDtypeStruct
    return local_call(
        mid_kernel,
        [
            sds((rows, width), F32), sds((rows, width), BF), sds((rows, cols), BF), sds((rows, cols), BF),
            sds((3, 8, width), F32), sds(qkv.shape, BF), sds(probs.shape, F32),
        ],
        "mid_grads", "vvvhvvvvvvhh", "hvvvvvv",
        [pltpu.VMEM((rows, width), F32)] * 2 + [pltpu.SemaphoreType.DMA((2 * rows // BLOCK + 2,))], 24,
    )(pg_own, pg_oth, ograd, normed, inv, wu_own, wu_oth, wo_own, wo_oth, ga, qkv, probs)


def attend_back_kernel(qkv_ref, prob_ref, cg_ref, *refs):
    if len(refs) > 2:
        next_qkv_hbm, next_prob_hbm, dqkv_ref, sums_ref, next_qkv_ref, next_prob_ref, sems = refs
        copies = Copies(sems)
        copies.start(next_qkv_hbm, next_qkv_ref)
        copies.start(next_prob_hbm, next_prob_ref)
    else:
        dqkv_ref, sums_ref = refs
    rows_all, cols = cg_ref.shape
    scale_a, scale_b = half_masks(LEN, HD**-0.5)
    one_a, one_b = half_masks(LEN)
    units = [(s, j) for s in range(rows_all // LEN) for j in range(cols // PAIR)]
    sums = {}

    def load(unit, i):
        s, j = unit
        return qkv_ref[s * LEN : (s + 1) * LEN, i * cols + j * PAIR : i * cols + (j + 1) * PAIR]

    def grad_probs(unit):
        s, j = unit
        v2 = load(unit, 2)
        g2 = cg_ref[s * LEN : (s + 1) * LEN, j * PAIR : (j + 1) * PAIR]
        return mm(g2, jnp.concatenate([v2 * one_a, v2 * one_b], axis=0), NT)

    def finish(unit, dprobs):
        s, j = unit
        rows = slice(s * LEN, (s + 1) * LEN)
        tall, flat = [], []
        for h in range(2):
            lanes = slice(h * LEN, (h + 1) * LEN)
            ds, low = [], []
            for r in range(0, LEN, SOFT):
                p = prob_ref[s, j, r : r + SOFT, lanes]
                dp = dprobs[r : r + SOFT, lanes]
                ds.append((p * (dp - jnp.sum(p * dp, axis=1, keepdims=True))).astype(BF))
                low.append(p.astype(BF))
            flat.append(jnp.concatenate(ds, axis=0))
            tall.append(jnp.concatenate(low, axis=0))
        q2, k2 = load(unit, 0), load(unit, 1)
        g2 = cg_ref[rows, j * PAIR : (j + 1) * PAIR]
        qcat = jnp.concatenate([q2 * scale_a, q2 * scale_b], axis=0)
        kcat = jnp.concatenate([k2 * scale_a, k2 * scale_b], axis=0)
        gcat = jnp.concatenate([g2 * one_a, g2 * one_b], axis=0)
        dq = mm(jnp.concatenate(flat, axis=1), kcat).astype(BF)
        dk = mm(jnp.concatenate(flat, axis=0), qcat, TN).astype(BF)
        dv = mm(jnp.concatenate(tall, axis=0), gcat, TN).astype(BF)
        for i, value in enumerate((dq, dk, dv)):
            dqkv_ref[rows, i * cols + j * PAIR : i * cols + (j + 1) * PAIR] = value
        return fold8(dq.astype(F32)), fold8(dv.astype(F32))

    pending = [grad_probs(u) for u in units[:AHEAD]]
    for i, unit in enumerate(units):
        if i + AHEAD < len(units):
            pending.append(grad_probs(units[i + AHEAD]))
        new_q, new_v = finish(unit, pending.pop(0))
        j = unit[1]
        if j in sums:
            new_q, new_v = sums[j][0] + new_q, sums[j][1] + new_v
        sums[j] = (new_q, new_v)
    for j, (sum_q, sum_v) in sums.items():
        sums_ref[0, :, j * PAIR : (j + 1) * PAIR] = sum_q
        sums_ref[1, :, j * PAIR : (j + 1) * PAIR] = sum_v
    if len(refs) > 2:
        copies.wait_all()


def attend_back(qkv, probs, cgrad, *following):
    sds = jax.ShapeDtypeStruct
    shapes = [sds(qkv.shape, BF), sds((2, 8, cgrad.shape[1]), F32)] + [sds(a.shape, a.dtype) for a in following]
    return local_call(
        attend_back_kernel, shapes, "attend_back", "vvv" + "h" * len(following), "v" * len(shapes),
        [pltpu.SemaphoreType.DMA((2,))] if following else [], 12,
    )(qkv, probs, cgrad, *following)


def token_kernel(own_ref, oth_ref, migrad_hbm, w_own_ref, w_oth_ref, out_hbm, migrad_ref, out_ref, sems):
    copies = Copies(sems)
    blocks = [slice(start, start + BLOCK) for start in range(0, own_ref.shape[0], BLOCK)]
    for i, rows in enumerate(blocks):
        copies.start(migrad_hbm.at[rows, :], migrad_ref.at[rows, :], i)
    w = jnp.concatenate([side_by_side(w_own_ref), side_by_side(w_oth_ref)], axis=1)
    for i, rows in enumerate(blocks):
        grads = jnp.concatenate([own_ref[rows, :], oth_ref[rows, :]], axis=1)
        total = mm(grads, w, NT)
        copies.wait(i)
        out_ref[rows, :] = total + migrad_ref[rows, :]
        copies.start(out_ref.at[rows, :], out_hbm.at[rows, :])
    copies.wait_all()


def token_grads(dqkv_own, dqkv_oth, migrad, w_own, w_oth):
    return local_call(
        token_kernel, [jax.ShapeDtypeStruct(migrad.shape, F32)], "token_grads", "vvhvv", "h",
        [pltpu.VMEM(migrad.shape, F32)] * 2 + [pltpu.SemaphoreType.DMA((2 * migrad.shape[0] // BLOCK,))], 20, 10**12,
    )(dqkv_own, dqkv_oth, migrad, w_own, w_oth)[0]


def per_device(
    tokens, timesteps, src_len, tgt_len, sample_weight, w_qkv, bias_qv, w_out, bias_out, gain_attn, shift_attn,
    w_up, bias_up, w_down, bias_down, gain_mlp, shift_mlp, cotangent,
):
    rows, width = tokens.shape
    dp = lax.axis_size("dp")
    mp_index = lax.axis_index("mp")
    seqs = rows // LEN
    cols = bias_qv.shape[1]
    ff = bias_up.shape[0]
    plane = 4

    def swap(value):
        return lax.ppermute(value, "mp", [(0, 1), (1, 0)])

    def after(value, *earlier):
        return lax.optimization_barrier((value, *earlier))[0]

    table = time_table(timesteps, width)
    meta = jnp.stack([src_len.astype(F32), (src_len + tgt_len).astype(F32), sample_weight])
    qkv_oth_w = swap(w_qkv)
    biases = jnp.concatenate([bias_qv, bias_up.reshape(-1, cols)])
    biases_oth = swap(biases)
    wo_oth = swap(w_out)
    wu_oth = swap(w_up)
    wd_oth = swap(w_down)

    qkv_own, prob_own, ctx_own, ctx_own_h, x_low, x_low_h = attend(meta, (tokens, table), w_qkv, biases)
    qkv_oth, prob_oth, ctx_oth, ctx_oth_h = attend(meta, (x_low,), qkv_oth_w, biases_oth)
    (normed, inv, mid_low, hid_own, hid_oth, dg_own, dg_oth, layer_out, ograd, mgrad, sums_mlp) = mlp(
        meta, tokens, table, ctx_own, ctx_oth, cotangent, w_out, wo_oth, bias_out,
        gain_attn, shift_attn, w_up, wu_oth, biases, biases_oth, w_down, wd_oth, bias_down, gain_mlp, shift_mlp,
    )
    split = dp == 16
    in_plane = [[base + k for k in range(plane)] for base in range(0, dp, plane)]
    across = [[base * plane + k for base in range(dp // plane)] for k in range(plane)]

    def part(ins, recv):
        return weight_grad(ins, dp, plane, recv, split)

    def hop(value, bits):
        return lax.ppermute(value, "dp", [(i, i ^ bits) for i in range(dp)])

    def along(pieces):
        if not split:
            return pieces
        sa, ka, sb, kb = pieces
        return ka, hop(sa, 1), kb, hop(sb, 2)

    def across_it(pieces, *earlier):
        if not split:
            return pieces
        ka, ra, kb, rb = pieces
        sa, ta, sb, tb = fold_first(after(ka, *earlier), ra, kb, rb)
        return ta, hop(sa, 2), tb, hop(sb, 1)

    def out_of_plane(pieces, *earlier):
        if not split:
            return pieces
        ka, ra, kb, rb = pieces
        send, keep = fold_second(after(ka, *earlier), ra, kb, rb, plane)
        return keep, hop(send, plane)

    def farther(pieces, *earlier):
        if not split:
            return pieces
        keep, arrived = pieces
        send, own = fold_outer(after(keep, *earlier), arrived)
        return own, hop(send, 2 * plane)

    def finish(pieces, *earlier):
        if split:
            return last_sum(after(pieces[0], *earlier), *pieces[1:])
        value = lax.psum_scatter(pieces[0], "dp", scatter_dimension=0, axis_index_groups=in_plane)
        value = lax.psum_scatter(value, "dp", scatter_dimension=0, axis_index_groups=across).astype(F32)
        if value.ndim == 2:
            return [value]
        half = value.shape[1] // 2
        return [value[:3], jnp.concatenate([value[3, :half], value[3, half:]], axis=1)]

    (down_send,) = weight_grad((hid_oth, mgrad), dp, plane)
    down_recv = swap(down_send)
    pg_own, pg_oth, sum_up_own, sum_up_oth = pre_grads(after(mgrad, down_send), w_down, wd_oth, dg_own, dg_oth)
    down = along(part((hid_own, after(mgrad, pg_own)), down_recv))
    (up_send,) = weight_grad((after(mid_low, down[0]), pg_oth), dp, plane)
    up_recv = swap(up_send)
    migrad, agrad, cg_own, cg_oth, sums_mid, qkv_oth, prob_oth = mid_grads(
        pg_own, pg_oth, after(ograd, up_send), normed, inv, w_up, wu_oth, w_out, wo_oth, gain_attn, qkv_oth, prob_oth
    )
    down = across_it(down, agrad)
    up = along(part((after(mid_low, down[0]), pg_own), up_recv))
    dqkv_oth, sum_qv_oth, qkv_own, prob_own = attend_back(qkv_oth, prob_oth, after(cg_oth, up[0]), qkv_own, prob_own)
    dqkv_own, sum_qv_own = attend_back(qkv_own, prob_own, cg_own)
    keep, send = pack_sums(sums_mid, sums_mlp, sum_up_own, sum_up_oth, sum_qv_own, sum_qv_oth)
    (attn_send,) = weight_grad((x_low_h, dqkv_oth, ctx_oth_h, after(agrad, keep)), dp, plane)
    attn_recv = swap(attn_send)
    down = out_of_plane(down, attn_send)
    up = across_it(up, down[0])
    sums_recv = swap(send)
    tokens_grad = token_grads(dqkv_own, dqkv_oth, after(migrad, up[0]), w_qkv, qkv_oth_w)
    attn = along(part((x_low_h, dqkv_own, ctx_own_h, after(agrad, tokens_grad)), attn_recv))
    up = out_of_plane(up, attn[0])
    down = farther(down, up[0])
    sums = after(keep, down[0]) + sums_recv
    sums_far = hop(sums, 1)
    attn = across_it(attn, sums)
    up = farther(up, attn[0])
    sums = after(sums, up[0]) + sums_far
    sums_far = hop(sums, 2)
    (grad_w_down,) = finish(down, sums)
    attn = out_of_plane(attn, grad_w_down)
    sums = after(sums, attn[0]) + sums_far
    sums_far = hop(sums, 4)
    (grad_w_up,) = finish(up, sums)
    attn = farther(attn, grad_w_up)
    sums = after(sums, attn[0]) + sums_far
    bit = 8
    while bit < dp:
        sums_far = hop(sums, bit)
        if bit == 8:
            grad_w_qkv, grad_w_out = finish(attn, sums)
            sums = after(sums, grad_w_out)
        sums = sums + sums_far
        bit *= 2
    grad_rows = jnp.concatenate([sums[0:2], sums[3:6]])
    grad_bias_out = sums[2]
    grad_bias_up = sums[6:8].reshape(-1)
    grad_bias_qv = sums[8].reshape(2, cols)
    return (
        layer_out, tokens_grad, grad_w_qkv, grad_w_out, grad_w_up, grad_w_down,
        grad_bias_qv, grad_bias_up, grad_bias_out, grad_rows,
    )


def solution(mesh):
    in_specs = (
        P(("dp", "mp"), None), P("dp"), P("dp"), P("dp"), P("dp"),
        P(None, None, "mp"), P(None, "mp"), P("mp", None), P(), P(), P(),
        P(None, "mp"), P("mp"), P("mp", None), P(), P(), P(), P(("dp", "mp"), None),
    )
    out_specs = (
        P(("dp", "mp"), None), P(("dp", "mp"), None), P(None, "dp", "mp"), P(("mp", "dp"), None),
        P("dp", "mp"), P(("mp", "dp"), None), P(None, "mp"), P("mp"), P(), P(),
    )
    return jax.shard_map(per_device, mesh=mesh, in_specs=in_specs, out_specs=out_specs, check_vma=False)
```

```python
import functools
import math

import jax
import jax.numpy as jnp
from jax import lax
from jax.experimental import pallas as pl
from jax.experimental.pallas import tpu as pltpu
from jax.sharding import PartitionSpec as P

HD = 64
LEN = 128
PAIR = 2 * HD
NORM_EPS = 1e-05
MASK_FILL = -1e30
BF = jnp.bfloat16
F32 = jnp.float32
MIB = 1 << 20
ROWS = 16
SOFT = 32
BLOCK = 512
MLP_BLOCK = 256
MLP_ROWS = 32
AHEAD = 2

NN = (((1,), (0,)), ((), ()))
NT = (((1,), (1,)), ((), ()))
TN = (((0,), (0,)), ((), ()))

SPECS = {
    "v": pl.BlockSpec(memory_space=pltpu.VMEM),
    "h": pl.BlockSpec(memory_space=pltpu.HBM),
    "w": pl.BlockSpec(memory_space=pltpu.VMEM),
}
AHEAD_FLOPS = 3 * 10**10


def mm(a, b, dims=NN):
    return lax.dot_general(a, b, dims, preferred_element_type=F32)


def params(mib):
    return pltpu.CompilerParams(vmem_limit_bytes=mib * MIB)


def local_call(kernel, out_shape, name, ins, outs, scratch=(), mib=16, flops=0):
    forced = {"v": pltpu.VMEM, "h": pltpu.HBM, "w": pltpu.HBM}

    def call(*args):
        args = [pltpu.with_memory_space_constraint(a, pltpu.HBM) if c in "hw" else a for a, c in zip(args, ins)]
        return pl.pallas_call(
            kernel,
            in_specs=[SPECS[c] for c in ins],
            out_specs=[SPECS[c] for c in outs],
            out_shape=[forced[c](a.shape, a.dtype) for a, c in zip(out_shape, outs)],
            scratch_shapes=list(scratch),
            compiler_params=params(mib),
            cost_estimate=pl.CostEstimate(flops=flops, bytes_accessed=0, transcendentals=0) if flops else None,
            name=name,
        )(*args)

    return call


class Copies:
    def __init__(self, sems):
        self.sems = sems
        self.started = []
        self.waiting = {}

    def start(self, src, dst, key=None):
        copy = pltpu.make_async_copy(src, dst, self.sems.at[len(self.started)])
        copy.start()
        self.started.append(copy)
        self.waiting.setdefault(key, []).append(copy)

    def wait(self, key=None):
        for copy in self.waiting.pop(key, ()):
            copy.wait()

    def wait_all(self):
        for key in list(self.waiting):
            self.wait(key)


def prepare_kernel(steps_hbm, bqv_ref, bu_ref, table_ref, bias_ref, steps_ref, sems):
    copies = Copies(sems)
    copies.start(steps_hbm, steps_ref)
    seqs, width = table_ref.shape
    half = width // 2
    cols = bqv_ref.shape[1]
    up = bu_ref[...].astype(F32).reshape(1, -1)
    rows = [bqv_ref[...].astype(F32)]
    rows += [up[:, i * cols : (i + 1) * cols] for i in range(up.shape[1] // cols)]
    rows += [jnp.zeros((bias_ref.shape[0] - 1 - len(rows), cols), F32)]
    bias_ref[...] = jnp.concatenate(rows, axis=0).astype(BF)
    lane = lax.broadcasted_iota(jnp.int32, (seqs, half), 1).astype(F32)
    frequency = jnp.exp(-math.log(10000.0) * lane / half)
    row = lax.broadcasted_iota(jnp.int32, (seqs, half), 0)
    base = lax.axis_index("mp") * seqs
    copies.wait()
    angles = jnp.zeros((seqs, half), F32)
    for s in range(seqs):
        angles = jnp.where(row == s, steps_ref[base + s].astype(F32), angles)
    angles = angles * frequency
    table_ref[:, :half] = jnp.sin(angles)
    table_ref[:, half:] = jnp.cos(angles)


def prepare(timesteps, bias_qv, bias_up, seqs, width):
    cols = bias_qv.shape[1]
    sds = jax.ShapeDtypeStruct
    rows = -(-(2 + bias_up.shape[0] // cols) // 8) * 8
    return local_call(
        prepare_kernel, [sds((seqs, width), F32), sds((rows, cols), BF)], "prepare", "hww", "vv",
        [pltpu.SMEM(timesteps.shape, jnp.int32), pltpu.SemaphoreType.DMA((1,))],
    )(timesteps, bias_qv, bias_up)


def half_masks(rows, value=1.0):
    lane = lax.broadcasted_iota(jnp.int32, (rows, PAIR), 1)
    first = jnp.where(lane < HD, value, 0.0).astype(BF)
    second = jnp.where(lane < HD, 0.0, value).astype(BF)
    return first, second


def fold8(value):
    rows, cols = value.shape
    return jnp.sum(value.reshape(rows // 8, 8, cols), axis=0)


def side_by_side(ref):
    return jnp.concatenate([ref[i] for i in range(ref.shape[0])], axis=1)


def attend_kernel(first, src_hbm, tgt_hbm, *refs):
    if first:
        (tok_hbm, table_ref, w_hbm, bias_ref, qkv_out, prob_out, ctx_ref, ctx_out, x_ref, x_out,
         src_ref, tgt_ref, qkv_ref, prob_ref, sems, tok_ref, w_ref) = refs
    else:
        (x_ref, w_ref, bias_ref, next_hbm, qkv_out, prob_out, ctx_ref, ctx_out, next_ref,
         src_ref, tgt_ref, qkv_ref, prob_ref, sems) = refs
    copies = Copies(sems)
    copies.start(src_hbm, src_ref, "m")
    copies.start(tgt_hbm, tgt_ref, "m")
    seqs = x_ref.shape[0] // LEN
    cols = w_ref.shape[2]
    base = lax.axis_index("mp") * seqs
    if first:
        for i in range(3):
            copies.start(w_hbm.at[i], w_ref.at[i], "w")
        for start in range(0, x_ref.shape[0], BLOCK):
            rows = slice(start, start + BLOCK)
            copies.start(tok_hbm.at[rows, :], tok_ref.at[rows, :], start)
    else:
        copies.start(next_hbm, next_ref)
    bias_q = bias_ref[0:1, :].astype(F32)
    bias_v = bias_ref[1:2, :].astype(F32)
    scale_a, scale_b = half_masks(LEN, HD**-0.5)
    one_a, one_b = half_masks(LEN)
    key_pos = lax.broadcasted_iota(jnp.int32, (SOFT, LEN), 1)

    def project(start):
        if first:
            copies.wait(start)
            for s in range(start // LEN, (start + BLOCK) // LEN):
                row = table_ref[s : s + 1, :]
                for r in range(s * LEN, (s + 1) * LEN, ROWS):
                    x_ref[r : r + ROWS, :] = (tok_ref[r : r + ROWS, :].astype(F32) + row).astype(BF)
        rows = slice(start, start + BLOCK)
        full = mm(x_ref[rows, :], w)
        qkv_ref[rows, :cols] = (full[:, :cols] + bias_q).astype(BF)
        qkv_ref[rows, cols : 2 * cols] = full[:, cols : 2 * cols].astype(BF)
        qkv_ref[rows, 2 * cols :] = (full[:, 2 * cols :] + bias_v).astype(BF)
        copies.start(qkv_ref.at[rows, :], qkv_out.at[rows, :])
        if first:
            copies.start(x_ref.at[rows, :], x_out.at[rows, :])

    def score(unit):
        s, j = unit
        rows = slice(s * LEN, (s + 1) * LEN)
        q2 = qkv_ref[rows, j * PAIR : (j + 1) * PAIR]
        k2 = qkv_ref[rows, cols + j * PAIR : cols + (j + 1) * PAIR]
        return mm(q2, jnp.concatenate([k2 * scale_a, k2 * scale_b], axis=0), NT)

    def finish(unit, scores):
        s, j = unit
        rows = slice(s * LEN, (s + 1) * LEN)
        live = key_pos < src_ref[base + s] + tgt_ref[base + s]
        low = []
        for r in range(0, LEN, SOFT):
            halves = []
            for h in range(2):
                part = jnp.where(live, scores[r : r + SOFT, h * LEN : (h + 1) * LEN], MASK_FILL)
                e = jnp.exp(part - jnp.max(part, axis=1, keepdims=True))
                halves.append(e * (1.0 / jnp.sum(e, axis=1, keepdims=True)))
            low.append(jnp.concatenate(halves, axis=1).astype(BF))
            prob_ref[s, j, r : r + SOFT, :] = low[-1]
        v2 = qkv_ref[rows, 2 * cols + j * PAIR : 2 * cols + (j + 1) * PAIR]
        vcat = jnp.concatenate([v2 * one_a, v2 * one_b], axis=0)
        ctx_ref[rows, j * PAIR : (j + 1) * PAIR] = mm(jnp.concatenate(low, axis=0), vcat).astype(BF)

    count = x_ref.shape[0]
    copies.wait("w")
    w = side_by_side(w_ref)
    project(0)
    copies.wait("m")
    for start in range(0, count, BLOCK):
        if start + BLOCK < count:
            project(start + BLOCK)
        units = [(s, j) for s in range(start // LEN, (start + BLOCK) // LEN) for j in range(cols // PAIR)]
        pending = [score(u) for u in units[:AHEAD]]
        for i, unit in enumerate(units):
            if i + AHEAD < len(units):
                pending.append(score(units[i + AHEAD]))
            finish(unit, pending.pop(0))
            if unit[1] == cols // PAIR - 1:
                copies.start(prob_ref.at[unit[0]], prob_out.at[unit[0]])
        rows = slice(start, start + BLOCK)
        copies.start(ctx_ref.at[rows, :], ctx_out.at[rows, :])
    copies.wait_all()


def attend(src, tgt, x_args, w_half, bias_half, following=None):
    first = len(x_args) == 2
    rows, width = x_args[0].shape
    cols = w_half.shape[2]
    sds = jax.ShapeDtypeStruct
    shapes = [
        sds((rows, 3 * cols), BF),
        sds((rows // LEN, cols // PAIR, LEN, 2 * LEN), BF),
        sds((rows, cols), BF),
        sds((rows, cols), BF),
        sds((rows, width), BF),
        sds((rows, width), BF),
    ]
    if not first:
        shapes = shapes[:4] + [sds(following.shape, BF)]
    scratch = [
        pltpu.SMEM(src.shape, jnp.int32),
        pltpu.SMEM(tgt.shape, jnp.int32),
        pltpu.VMEM(shapes[0].shape, BF),
        pltpu.VMEM(shapes[1].shape, BF),
        pltpu.SemaphoreType.DMA((4 * rows // BLOCK + rows // LEN + 5,)),
    ]
    if first:
        scratch += [pltpu.VMEM((rows, width), BF), pltpu.VMEM(w_half.shape, BF)]
    return local_call(
        functools.partial(attend_kernel, first), shapes, "attend",
        "hhhvhv" if first else "hhvvvh", "hhvhvh"[: len(shapes)], scratch, 20,
    )(src, tgt, *x_args, w_half, bias_half, *(() if first else (following,)))


def normalize(value):
    centred = value - jnp.mean(value, axis=1, keepdims=True)
    inv_std = lax.rsqrt(jnp.mean(centred * centred, axis=1, keepdims=True) + NORM_EPS)
    return centred * inv_std, inv_std


def normalize_back(scaled, normed, inv_std):
    return inv_std * (
        scaled
        - jnp.mean(scaled, axis=1, keepdims=True)
        - normed * jnp.mean(scaled * normed, axis=1, keepdims=True)
    )


def gelu_pair(v):
    cdf = 0.5 + 0.5 * lax.erf(v * math.sqrt(0.5))
    return v * cdf, cdf + v * jnp.exp(v * v * -0.5) * (1.0 / math.sqrt(2.0 * math.pi))


def mlp_kernel(
    src_hbm, tgt_hbm, weight_hbm, tok_ref, table_ref, ctx_own_ref, ctx_oth_ref, cot_hbm,
    wo_own_ref, wo_oth_ref, bo_ref, ga_ref, sa_ref,
    wu_own_ref, wu_oth_ref, bu_own_ref, bu_oth_ref, wd_own_ref, wd_oth_ref, bd_ref, gm_ref, sm_ref,
    normed_ref, inv_ref, mid_ref, hid_own_ref, hid_oth_ref, dg_own_ref, dg_oth_ref,
    out_hbm, mgrad_ref, sums_ref, normed_f32, out_ref, cot_ref, src_ref, tgt_ref, weight_ref, sems,
):
    count = tok_ref.shape[0]
    base = lax.axis_index("mp") * (count // LEN)
    copies = Copies(sems)
    for hbm, smem in ((src_hbm, src_ref), (tgt_hbm, tgt_ref), (weight_hbm, weight_ref)):
        copies.start(hbm, smem, 0)
    for start in range(0, count, MLP_BLOCK):
        copies.start(cot_hbm.at[start : start + MLP_BLOCK, :], cot_ref.at[start : start + MLP_BLOCK, :], start)
    wo = jnp.concatenate([wo_own_ref[...], wo_oth_ref[...]], axis=0)
    halves = (
        (wu_own_ref, bu_own_ref, wd_own_ref, hid_own_ref, dg_own_ref),
        (wu_oth_ref, bu_oth_ref, wd_oth_ref, hid_oth_ref, dg_oth_ref),
    )

    def first_norm(start):
        rows = slice(start, start + MLP_BLOCK)
        attn_out = mm(jnp.concatenate([ctx_own_ref[rows, :], ctx_oth_ref[rows, :]], axis=1), wo)
        for r in range(0, MLP_BLOCK, MLP_ROWS):
            part = slice(start + r, start + r + MLP_ROWS)
            table_row = table_ref[(start + r) // LEN : (start + r) // LEN + 1, :]
            start_x = tok_ref[part, :].astype(F32) + table_row
            normed, inv = normalize(start_x + attn_out[r : r + MLP_ROWS] + bo_ref[...])
            normed_f32[part, :] = normed
            normed_ref[part, :] = normed.astype(BF)
            inv_ref[part, :] = inv
            mid_x = normed * ga_ref[...] + sa_ref[...]
            mid_ref[part, :] = mid_x.astype(BF)

    def up(unit):
        start, half = unit
        return mm(mid_ref[start : start + MLP_BLOCK, :], halves[half][0][...])

    def activate(unit, pre):
        start, half = unit
        _, bu_ref, wd_ref, hid_ref, dg_ref = halves[half]
        bias = jnp.concatenate([bu_ref[i : i + 1, :] for i in range(2, 2 + wd_ref.shape[0] // bu_ref.shape[1])], axis=1).astype(F32)
        for r in range(0, MLP_BLOCK, MLP_ROWS):
            part = slice(start + r, start + r + MLP_ROWS)
            hidden, slope = gelu_pair(pre[r : r + MLP_ROWS] + bias)
            hid_ref[part, :] = hidden.astype(BF)
            dg_ref[part, :] = slope.astype(BF)
        return mm(hid_ref[start : start + MLP_BLOCK, :], wd_ref[...])

    pos = lax.broadcasted_iota(jnp.int32, (MLP_ROWS, 1), 0)

    def second_norm(start, mlp_out, sums):
        copies.wait(start)
        for r in range(0, MLP_BLOCK, MLP_ROWS):
            part = slice(start + r, start + r + MLP_ROWS)
            seq = base + (start + r) // LEN
            mid_x = normed_f32[part, :] * ga_ref[...] + sa_ref[...]
            normed2, inv2 = normalize(mid_x + (mlp_out[r : r + MLP_ROWS] + bd_ref[...]))
            out_ref[part, :] = normed2 * gm_ref[...] + sm_ref[...]
            here = pos + (start + r) % LEN
            inside = (here >= src_ref[seq]) & (here < src_ref[seq] + tgt_ref[seq])
            e = cot_ref[part, :].astype(F32) * jnp.where(inside, weight_ref[seq], 0.0)
            mgrad = normalize_back(e * gm_ref[...], normed2, inv2).astype(BF)
            mgrad_ref[part, :] = mgrad
            new = [fold8(mgrad.astype(F32)), fold8(e * normed2), fold8(e)]
            sums = new if sums is None else [x + y for x, y in zip(sums, new)]
        rows = slice(start, start + MLP_BLOCK)
        copies.start(out_ref.at[rows, :], out_hbm.at[rows, :])
        return sums

    sums = None
    first_norm(0)
    units = [(start, half) for start in range(0, count, MLP_BLOCK) for half in range(2)]
    ready = up(units[0])
    waiting = None
    total = None
    for i, unit in enumerate(units):
        start, half = unit
        pre = ready
        if half == 0 and start + MLP_BLOCK < count:
            first_norm(start + MLP_BLOCK)
        if i + 1 < len(units):
            ready = up(units[i + 1])
        down = activate(unit, pre)
        if half == 0:
            if waiting is not None:
                sums = second_norm(*waiting, sums)
            total = down
        else:
            waiting = (start, total + down)
    sums = second_norm(*waiting, sums)
    sums_ref[...] = jnp.stack(sums)
    copies.wait_all()


def mlp(src, tgt, weight, tokens, table, ctx_own, ctx_oth, cot, wo_own, wo_oth, bo, ga, sa,
        wu_own, wu_oth, bu_own, bu_oth, wd_own, wd_oth, bd, gm, sm):
    rows, width = tokens.shape
    ff = wu_own.shape[1]
    sds = jax.ShapeDtypeStruct
    args = (src, tgt, weight, tokens, table, ctx_own, ctx_oth, cot, wo_own, wo_oth, bo, ga, sa,
            wu_own, wu_oth, bu_own, bu_oth, wd_own, wd_oth, bd, gm, sm)
    return local_call(
        mlp_kernel,
        [
            sds((rows, width), BF), sds((rows, 1), F32), sds((rows, width), BF),
            sds((rows, ff), BF), sds((rows, ff), BF), sds((rows, ff), BF), sds((rows, ff), BF),
            sds((rows, width), F32), sds((rows, width), BF), sds((3, 8, width), F32),
        ],
        "mlp",
        "hhhvvvvh" + "v" * 14,
        "vvvvvvvhvv",
        [pltpu.VMEM((rows, width), F32)] * 2 + [
            pltpu.VMEM((rows, width), BF), pltpu.SMEM(src.shape, jnp.int32), pltpu.SMEM(tgt.shape, jnp.int32),
            pltpu.SMEM(weight.shape, F32), pltpu.SemaphoreType.DMA((4 * rows // MLP_BLOCK + 3,)),
        ],
        22,
    )(*args)


def pre_kernel(mgrad_ref, wd_own_ref, wd_oth_ref, dg_own_ref, dg_oth_ref, pg_own_ref, pg_oth_ref, sum_own_ref, sum_oth_ref):
    halves = ((wd_oth_ref, dg_oth_ref, pg_oth_ref, sum_oth_ref), (wd_own_ref, dg_own_ref, pg_own_ref, sum_own_ref))
    units = [(h, c) for h in halves for c in range(0, wd_own_ref.shape[0], 512)]

    def product(unit):
        (wd_ref, _, _, _), c = unit
        return mm(mgrad_ref[...], wd_ref[c : c + 512, :], NT)

    ready = product(units[0])
    for i, ((_, dg_ref, pg_ref, sum_ref), c) in enumerate(units):
        full = ready
        if i + 1 < len(units):
            ready = product(units[i + 1])
        sums = None
        for r in range(0, full.shape[0], 32):
            pg = (full[r : r + 32] * dg_ref[r : r + 32, c : c + 512].astype(F32)).astype(BF)
            pg_ref[r : r + 32, c : c + 512] = pg
            new = fold8(pg.astype(F32))
            sums = new if sums is None else sums + new
        sum_ref[:, c : c + 512] = sums


def pre_grads(mgrad, wd_own, wd_oth, dg_own, dg_oth):
    rows = mgrad.shape[0]
    ff = wd_own.shape[0]
    sds = jax.ShapeDtypeStruct
    return local_call(
        pre_kernel,
        [sds((rows, ff), BF), sds((rows, ff), BF), sds((8, ff), F32), sds((8, ff), F32)],
        "pre_grads", "vvvvv", "vvvv", mib=16,
    )(mgrad, wd_own, wd_oth, dg_own, dg_oth)


def weight_pieces(lhs_ref, rhs_ref, size, chunk=384):
    m = lhs_ref.shape[1]
    ready = mm(lhs_ref[:, :chunk], rhs_ref[...], TN)
    for start in range(0, m, chunk):
        full = ready
        if start + chunk < m:
            ready = mm(lhs_ref[:, start + chunk : start + 2 * chunk], rhs_ref[...], TN)
        for first in range(0, chunk, size):
            yield (start + first) // size, full[first : first + size]


def attn_pieces(x_ref, dqkv_ref, ctx_ref, agrad_ref, size):
    cols = ctx_ref.shape[1]
    half = size // 2
    out_full = mm(ctx_ref[...], agrad_ref[...], TN)
    for index, qkv in weight_pieces(x_ref, dqkv_ref, size):
        rows = out_full[index * half : (index + 1) * half]
        blocks = [(0, qkv[:, i * cols : (i + 1) * cols], i) for i in range(3)]
        yield index, blocks + [(c * half, rows[:, c * cols : (c + 1) * cols], 3) for c in range(2)]


def coded(sums):
    high = sums.astype(BF).astype(F32)
    return jnp.concatenate([high, sums - high], axis=0).astype(BF)


def decoded(block):
    value = block.astype(F32)
    half = value.shape[0] // 2
    return value[:half] + value[half:]


def send_kernel(lhs_ref, rhs_ref, out_ref):
    plane, _, size, _ = out_ref.shape
    for index, value in weight_pieces(lhs_ref, rhs_ref, size):
        out_ref[index % plane, index // plane] = value.astype(BF)


def total_kernel(lhs_ref, rhs_ref, recv_ref, out_ref):
    plane, _, size, _ = out_ref.shape
    for index, value in weight_pieces(lhs_ref, rhs_ref, size):
        k, g = index % plane, index // plane
        out_ref[k, g] = (value + recv_ref[k, g].astype(F32)).astype(BF)


def split_kernel(lhs_ref, rhs_ref, recv_ref, sa_ref, ka_ref, sb_ref, kb_ref, held_ref):
    plane, size = held_ref.shape[1], held_ref.shape[2]
    me = lax.axis_index("dp") % plane
    for index, value in weight_pieces(lhs_ref, rhs_ref, size):
        k, g = index % plane, index // plane
        slot = g % held_ref.shape[0]
        held_ref[slot, k] = value + recv_ref[k, g].astype(F32)
        if k == plane - 1:
            for far in range(plane):
                y, x = divmod(far, 2)
                piece = held_ref[slot, me ^ far].astype(BF)
                half = piece.shape[1] // 2
                (sa_ref if x else ka_ref)[y, g] = piece[:, :half]
                (sb_ref if y else kb_ref)[x, g] = piece[:, half:]


def weight_grad(lhs, rhs, dp, plane, recv=None, split=False):
    size, n = lhs.shape[1] // dp, rhs.shape[1]
    outer = dp // plane
    sds = jax.ShapeDtypeStruct
    scratch = ()
    if recv is None:
        kernel, shapes, args = send_kernel, [sds((plane, outer, size, n), BF)], (lhs, rhs)
    elif split:
        kernel, shapes, args = split_kernel, [sds((2, outer, size, n // 2), BF)] * 4, (lhs, rhs, recv)
        scratch = [pltpu.VMEM((2, plane, size, n), F32)]
    else:
        kernel, shapes, args = total_kernel, [sds((plane, outer, size, n), BF)], (lhs, rhs, recv)
    return local_call(kernel, shapes, "wgrad", "v" * len(args), "v" * len(shapes), scratch, 16)(*args)


def attn_send_kernel(x_ref, dqkv_ref, ctx_ref, agrad_ref, *refs):
    *sums_refs, out_ref = refs
    _, size, cols = out_ref.shape
    outer = out_ref.shape[0] // 16
    for index, blocks in attn_pieces(x_ref, dqkv_ref, ctx_ref, agrad_ref, size):
        k, g = index % 4, index // 4
        for first, value, i in blocks:
            out_ref[(k * outer + g) * 4 + i, first : first + value.shape[0], :] = value.astype(BF)
    for sums_ref in sums_refs:
        out_ref[16 * outer] = coded(sums_ref[...])


def attn_hold(recv_ref, index, blocks, held_ref, slot, outer):
    k, g = index % 4, index // 4
    for first, value, i in blocks:
        held_ref[slot, k, i, first : first + value.shape[0], :] = value
    for i in range(4):
        arrived = recv_ref[(k * outer + g) * 4 + i]
        held_ref[slot, k, i] = held_ref[slot, k, i] + arrived.astype(F32)
    return k, g


def attn_total_kernel(x_ref, dqkv_ref, ctx_ref, agrad_ref, recv_ref, out_ref, held_ref):
    plane, outer, _, size, _ = out_ref.shape
    for index, blocks in attn_pieces(x_ref, dqkv_ref, ctx_ref, agrad_ref, size):
        slot = (index // plane) % 2
        k, g = attn_hold(recv_ref, index, blocks, held_ref, slot, outer)
        out_ref[k, g] = held_ref[slot, k].astype(BF)


def attn_split_kernel(
    x_ref, dqkv_ref, ctx_ref, agrad_ref, keep_ref, recv_ref,
    sa_ref, ka_ref, sb_ref, kb_ref, sums_ref, held_ref,
):
    plane, size = held_ref.shape[1], held_ref.shape[3]
    outer = kb_ref.shape[0] // 4
    me = lax.axis_index("dp") % plane
    sums = decoded(coded(keep_ref[...])) + decoded(recv_ref[16 * outer])
    sums_ref[...] = sums
    sa_ref[4 * outer] = coded(sums)
    for index, blocks in attn_pieces(x_ref, dqkv_ref, ctx_ref, agrad_ref, size):
        slot = (index // plane) % 2
        k, g = attn_hold(recv_ref, index, blocks, held_ref, slot, outer)
        if k == plane - 1:
            for far in range(plane):
                y, x = divmod(far, 2)
                piece = held_ref[slot, me ^ far].astype(BF)
                a, b = (y * outer + g) * 2, (x * outer + g) * 2
                (sa_ref if x else ka_ref)[a : a + 2] = piece[:2]
                (sb_ref if y else kb_ref)[b : b + 2] = piece[2:]


def attn_grad(x_low, dqkv, ctx, agrad, dp, sums=None, recv=None):
    size, cols = x_low.shape[1] // dp, ctx.shape[1]
    outer = dp // 4
    sds = jax.ShapeDtypeStruct
    block = lambda n: sds((n, size, cols), BF)
    args = (x_low, dqkv, ctx, agrad) + (() if sums is None else (sums,))
    scratch = ()
    if recv is None:
        kernel, shapes = attn_send_kernel, [block(16 * outer + (sums is not None))]
    else:
        args += (recv,)
        scratch = [pltpu.VMEM((2, 4, 4, size, cols), F32)]
        if sums is None:
            kernel, shapes = attn_total_kernel, [sds((4, outer, 4, size, cols), BF)]
        else:
            kernel = attn_split_kernel
            shapes = [block(4 * outer + 1)] + [block(4 * outer)] * 3 + [sds(sums.shape, F32)]
    return local_call(kernel, shapes, "attn_wgrad", "v" * len(args), "v" * len(shapes), scratch, 16)(*args)


def add_low(one, two):
    return (one.astype(F32) + two.astype(F32)).astype(BF)


def fold_kernel(ka_ref, ra_ref, kb_ref, rb_ref, sa_ref, ta_ref, sb_ref, tb_ref):
    for k_ref, r_ref, s_ref, t_ref in ((ka_ref, ra_ref, sa_ref, ta_ref), (kb_ref, rb_ref, sb_ref, tb_ref)):
        for g in range(k_ref.shape[1]):
            s_ref[g] = add_low(k_ref[1, g], r_ref[1, g])
            t_ref[g] = add_low(k_ref[0, g], r_ref[0, g])


def fold_first(ka, ra, kb, rb):
    shape = jax.ShapeDtypeStruct(ka.shape[1:], BF)
    return local_call(fold_kernel, [shape] * 4, "fold_first", "vvvv", "vvvv")(ka, ra, kb, rb)


def attn_fold_kernel(ka_ref, ra_ref, kb_ref, rb_ref, old_ref, sa_ref, ta_ref, sb_ref, tb_ref, sums_ref):
    count = ta_ref.shape[0]
    for k_ref, r_ref, s_ref, t_ref in ((ka_ref, ra_ref, sa_ref, ta_ref), (kb_ref, rb_ref, sb_ref, tb_ref)):
        for g in range(count):
            s_ref[g] = add_low(k_ref[count + g], r_ref[count + g])
            t_ref[g] = add_low(k_ref[g], r_ref[g])
    sums = decoded(coded(old_ref[...])) + decoded(ra_ref[2 * count])
    sums_ref[...] = sums
    sa_ref[count] = coded(sums)


def attn_fold_first(ka, ra, kb, rb, sums):
    sds = jax.ShapeDtypeStruct
    count = ka.shape[0] // 2
    block = lambda n: sds((n,) + ka.shape[1:], BF)
    return local_call(
        attn_fold_kernel, [block(count + 1)] + [block(count)] * 3 + [sds(sums.shape, F32)], "fold_first", "vvvvv", "vvvvv"
    )(ka, ra, kb, rb, sums)


def plane_kernel(plane, ka_ref, ra_ref, kb_ref, rb_ref, send_ref, keep_ref):
    me = lax.axis_index("dp") // plane
    for far in range(ka_ref.shape[0]):
        g = me ^ far
        out_ref = send_ref if far % 2 else keep_ref
        half = ka_ref.shape[2]
        out_ref[far // 2, :, :half] = add_low(ka_ref[g], ra_ref[g])
        out_ref[far // 2, :, half:] = add_low(kb_ref[g], rb_ref[g])


def fold_second(ka, ra, kb, rb, plane):
    outer, size, n = ka.shape
    return local_call(
        functools.partial(plane_kernel, plane), [jax.ShapeDtypeStruct((outer // 2, size, 2 * n), BF)] * 2,
        "fold_second", "vvvv", "vv", flops=AHEAD_FLOPS,
    )(ka, ra, kb, rb)


def attn_plane_kernel(ka_ref, ra_ref, kb_ref, rb_ref, old_ref, send_ref, keep_ref, sums_ref):
    me = lax.axis_index("dp") // 4
    outer = ka_ref.shape[0] // 2
    for far in range(outer):
        here = pl.ds((me ^ far) * 2, 2)
        out_ref = send_ref if far % 2 else keep_ref
        first = (far // 2) * 4
        out_ref[first : first + 2] = add_low(ka_ref[here], ra_ref[here])
        out_ref[first + 2 : first + 4] = add_low(kb_ref[here], rb_ref[here])
    sums = decoded(coded(old_ref[...])) + decoded(ra_ref[2 * outer])
    sums_ref[...] = sums
    send_ref[2 * outer] = coded(sums)


def attn_fold_second(ka, ra, kb, rb, sums):
    sds = jax.ShapeDtypeStruct
    outer = ka.shape[0] // 2
    block = lambda n: sds((n,) + ka.shape[1:], BF)
    return local_call(
        attn_plane_kernel, [block(2 * outer + 1), block(2 * outer), sds(sums.shape, F32)], "fold_second", "vvvvv", "vvv",
        flops=AHEAD_FLOPS,
    )(ka, ra, kb, rb, sums)


def outer_kernel(keep_ref, arrived_ref, send_ref, own_ref):
    send_ref[...] = add_low(keep_ref[1], arrived_ref[1])
    own_ref[...] = keep_ref[0].astype(F32) + arrived_ref[0].astype(F32)


def fold_outer(keep, arrived):
    shape = keep.shape[1:]
    sds = jax.ShapeDtypeStruct
    return local_call(outer_kernel, [sds(shape, BF), sds(shape, F32)], "fold_outer", "vv", "vv")(keep, arrived)


def attn_outer_kernel(keep_ref, arrived_ref, old_ref, send_ref, own_ref, sums_ref):
    for i in range(4):
        send_ref[i] = add_low(keep_ref[4 + i], arrived_ref[4 + i])
        own_ref[i] = keep_ref[i].astype(F32) + arrived_ref[i].astype(F32)
    sums = decoded(coded(old_ref[...])) + decoded(arrived_ref[8])
    sums_ref[...] = sums
    send_ref[4] = coded(sums)


def attn_fold_outer(keep, arrived, sums):
    sds = jax.ShapeDtypeStruct
    tile = keep.shape[1:]
    return local_call(
        attn_outer_kernel, [sds((5,) + tile, BF), sds((4,) + tile, F32), sds(sums.shape, F32)], "fold_outer", "vvv", "vvv"
    )(keep, arrived, sums)


def last_kernel(own_ref, arrived_ref, out_ref):
    out_ref[...] = own_ref[...] + arrived_ref[...].astype(F32)


def last_sum(own, arrived):
    return local_call(last_kernel, [jax.ShapeDtypeStruct(own.shape, F32)], "last_sum", "vv", "w")(own, arrived)[0]


SUM_ROWS = 24


def unpack(sums, rows_ref, out_bias_ref, up_ref, qv_ref):
    whole = jnp.concatenate([sums[0:9], sums[9:18]], axis=1)
    width = whole.shape[1]
    rows_ref[...] = whole[0:5]
    out_bias_ref[...] = whole[5]
    up_ref[:width] = whole[6]
    up_ref[width:] = whole[7]
    qv_ref[0:1, :] = sums[8:9]
    qv_ref[1:2, :] = sums[17:18]


def attn_last_kernel(own_ref, arrived_ref, old_ref, qkv_ref, out_ref, *sum_refs):
    _, size, cols = own_ref.shape
    for i in range(3):
        qkv_ref[i] = own_ref[i] + arrived_ref[i].astype(F32)
    total = own_ref[3] + arrived_ref[3].astype(F32)
    out_ref[:, :cols] = total[: size // 2]
    out_ref[:, cols:] = total[size // 2 :]
    unpack(decoded(coded(old_ref[...])) + decoded(arrived_ref[4]), *sum_refs)


def attn_last(own, arrived, sums):
    sds = jax.ShapeDtypeStruct
    _, size, cols = own.shape
    width = 2 * cols
    shapes = [
        sds((3, size, cols), F32), sds((size // 2, width), F32), sds((5, width), F32), sds((width,), F32),
        sds((2 * width,), F32), sds((2, cols), F32),
    ]
    return local_call(attn_last_kernel, shapes, "last_sum", "vvv", "w" * 6)(own, arrived, sums)


def pack_kernel(mid_ref, mlp_ref, up_own_ref, up_oth_ref, qv_own_ref, qv_oth_ref, keep_ref, send_ref):
    cols = keep_ref.shape[1]
    row = lambda value: jnp.sum(value, axis=0, keepdims=True)
    for out_ref, up_ref, qv_ref in ((keep_ref, up_own_ref, qv_own_ref), (send_ref, up_oth_ref, qv_oth_ref)):
        rows = [row(mid_ref[0]), row(mid_ref[1])] + [row(mlp_ref[i]) for i in range(3)] + [row(mid_ref[2])]
        rows += [row(up_ref[:, i * 2 * cols : (i + 1) * 2 * cols]) for i in range(2)]
        rows.append(jnp.concatenate([row(qv_ref[0]), row(qv_ref[1])], axis=1))
        for i, value in enumerate(rows):
            out_ref[i : i + 1, :] = value[:, :cols]
            out_ref[9 + i : 10 + i, :] = value[:, cols:]
        out_ref[18:, :] = jnp.zeros((SUM_ROWS - 18, cols), F32)


def pack_sums(sums_mid, sums_mlp, up_own, up_oth, qv_own, qv_oth):
    shape = jax.ShapeDtypeStruct((SUM_ROWS, qv_own.shape[2]), F32)
    return local_call(pack_kernel, [shape] * 2, "pack_sums", "v" * 6, "vv")(sums_mid, sums_mlp, up_own, up_oth, qv_own, qv_oth)


def mid_kernel(
    pg_own_ref, pg_oth_ref, mgrad_ref, normed_ref, inv_ref, wu_own_ref, wu_oth_ref, wo_own_ref, wo_oth_ref, ga_ref,
    qkv_hbm, prob_hbm, migrad_hbm, agrad_ref, cg_own_ref, cg_oth_ref, sums_ref, qkv_ref, prob_ref, migrad_ref, sems,
):
    def product(first):
        rows = slice(first, first + BLOCK)
        return mm(pg_own_ref[rows, :], wu_own_ref[...], NT) + mm(pg_oth_ref[rows, :], wu_oth_ref[...], NT)

    sums = None
    count = mgrad_ref.shape[0]
    copies = Copies(sems)
    copies.start(qkv_hbm, qkv_ref)
    copies.start(prob_hbm, prob_ref)
    cols = cg_own_ref.shape[1]
    wo = jnp.concatenate([wo_own_ref[...], wo_oth_ref[...]], axis=0)
    ready = product(0)
    for first in range(0, count, BLOCK):
        back = ready
        if first + BLOCK < count:
            ready = product(first + BLOCK)
        for r in range(0, BLOCK, ROWS):
            part = slice(first + r, first + r + ROWS)
            e = back[r : r + ROWS] + mgrad_ref[part, :].astype(F32)
            normed = normed_ref[part, :].astype(F32)
            migrad = normalize_back(e * ga_ref[...], normed, inv_ref[part, :])
            migrad_ref[part, :] = migrad
            agrad = migrad.astype(BF)
            agrad_ref[part, :] = agrad
            new = [fold8(e * normed), fold8(e), fold8(agrad.astype(F32))]
            sums = new if sums is None else [x + y for x, y in zip(sums, new)]
        rows = slice(first, first + BLOCK)
        copies.start(migrad_ref.at[rows, :], migrad_hbm.at[rows, :])
        cgrad = mm(agrad_ref[rows, :], wo, NT).astype(BF)
        cg_own_ref[rows, :] = cgrad[:, :cols]
        cg_oth_ref[rows, :] = cgrad[:, cols:]
    sums_ref[...] = jnp.stack(sums)
    copies.wait_all()


def mid_grads(pg_own, pg_oth, mgrad, normed, inv, wu_own, wu_oth, wo_own, wo_oth, ga, qkv, probs):
    rows, width = mgrad.shape
    cols = wo_own.shape[0]
    sds = jax.ShapeDtypeStruct
    return local_call(
        mid_kernel,
        [
            sds((rows, width), F32), sds((rows, width), BF), sds((rows, cols), BF), sds((rows, cols), BF),
            sds((3, 8, width), F32), sds(qkv.shape, BF), sds(probs.shape, BF),
        ],
        "mid_grads", "vvvvvvvvvvhh", "hvvvvvv",
        [pltpu.VMEM((rows, width), F32)] + [pltpu.SemaphoreType.DMA((rows // BLOCK + 2,))], 20,
    )(pg_own, pg_oth, mgrad, normed, inv, wu_own, wu_oth, wo_own, wo_oth, ga, qkv, probs)


def attend_back_kernel(qkv_ref, prob_ref, cg_ref, *refs):
    if len(refs) > 2:
        next_qkv_hbm, next_prob_hbm, dqkv_ref, sums_ref, next_qkv_ref, next_prob_ref, sems = refs
        copies = Copies(sems)
        copies.start(next_qkv_hbm, next_qkv_ref)
        copies.start(next_prob_hbm, next_prob_ref)
    else:
        dqkv_ref, sums_ref = refs
    rows_all, cols = cg_ref.shape
    scale_a, scale_b = half_masks(LEN, HD**-0.5)
    one_a, one_b = half_masks(LEN)
    units = [(s, j) for s in range(rows_all // LEN) for j in range(cols // PAIR)]
    sums = {}

    def load(unit, i):
        s, j = unit
        return qkv_ref[s * LEN : (s + 1) * LEN, i * cols + j * PAIR : i * cols + (j + 1) * PAIR]

    def grad_probs(unit):
        s, j = unit
        v2 = load(unit, 2)
        g2 = cg_ref[s * LEN : (s + 1) * LEN, j * PAIR : (j + 1) * PAIR]
        return mm(g2, jnp.concatenate([v2 * one_a, v2 * one_b], axis=0), NT)

    def finish(unit, dprobs):
        s, j = unit
        rows = slice(s * LEN, (s + 1) * LEN)
        tall, flat = [], []
        for h in range(2):
            lanes = slice(h * LEN, (h + 1) * LEN)
            ds, low = [], []
            for r in range(0, LEN, SOFT):
                low.append(prob_ref[s, j, r : r + SOFT, lanes])
                p = low[-1].astype(F32)
                dp = dprobs[r : r + SOFT, lanes]
                ds.append((p * (dp - jnp.sum(p * dp, axis=1, keepdims=True))).astype(BF))
            flat.append(jnp.concatenate(ds, axis=0))
            tall.append(jnp.concatenate(low, axis=0))
        q2, k2 = load(unit, 0), load(unit, 1)
        g2 = cg_ref[rows, j * PAIR : (j + 1) * PAIR]
        qcat = jnp.concatenate([q2 * scale_a, q2 * scale_b], axis=0)
        kcat = jnp.concatenate([k2 * scale_a, k2 * scale_b], axis=0)
        gcat = jnp.concatenate([g2 * one_a, g2 * one_b], axis=0)
        dq = mm(jnp.concatenate(flat, axis=1), kcat).astype(BF)
        dk = mm(jnp.concatenate(flat, axis=0), qcat, TN).astype(BF)
        dv = mm(jnp.concatenate(tall, axis=0), gcat, TN).astype(BF)
        for i, value in enumerate((dq, dk, dv)):
            dqkv_ref[rows, i * cols + j * PAIR : i * cols + (j + 1) * PAIR] = value
        return fold8(dq.astype(F32)), fold8(dv.astype(F32))

    pending = [grad_probs(u) for u in units[:AHEAD]]
    for i, unit in enumerate(units):
        if i + AHEAD < len(units):
            pending.append(grad_probs(units[i + AHEAD]))
        new_q, new_v = finish(unit, pending.pop(0))
        j = unit[1]
        if j in sums:
            new_q, new_v = sums[j][0] + new_q, sums[j][1] + new_v
        sums[j] = (new_q, new_v)
    for j, (sum_q, sum_v) in sums.items():
        sums_ref[0, :, j * PAIR : (j + 1) * PAIR] = sum_q
        sums_ref[1, :, j * PAIR : (j + 1) * PAIR] = sum_v
    if len(refs) > 2:
        copies.wait_all()


def attend_back(qkv, probs, cgrad, *following):
    sds = jax.ShapeDtypeStruct
    shapes = [sds(qkv.shape, BF), sds((2, 8, cgrad.shape[1]), F32)] + [sds(a.shape, a.dtype) for a in following]
    return local_call(
        attend_back_kernel, shapes, "attend_back", "vvv" + "h" * len(following), "v" * len(shapes),
        [pltpu.SemaphoreType.DMA((2,))] if following else [], 12,
    )(qkv, probs, cgrad, *following)


def token_kernel(own_ref, oth_ref, migrad_hbm, w_own_ref, w_oth_ref, out_hbm, migrad_ref, out_ref, sems):
    copies = Copies(sems)
    blocks = [slice(start, start + BLOCK) for start in range(0, own_ref.shape[0], BLOCK)]
    for i, rows in enumerate(blocks):
        copies.start(migrad_hbm.at[rows, :], migrad_ref.at[rows, :], i)
    w = jnp.concatenate([side_by_side(w_own_ref), side_by_side(w_oth_ref)], axis=1)
    for i, rows in enumerate(blocks):
        grads = jnp.concatenate([own_ref[rows, :], oth_ref[rows, :]], axis=1)
        total = mm(grads, w, NT)
        copies.wait(i)
        out_ref[rows, :] = total + migrad_ref[rows, :]
        copies.start(out_ref.at[rows, :], out_hbm.at[rows, :])
    copies.wait_all()


def token_grads(dqkv_own, dqkv_oth, migrad, w_own, w_oth):
    return local_call(
        token_kernel, [jax.ShapeDtypeStruct(migrad.shape, F32)], "token_grads", "vvhvv", "h",
        [pltpu.VMEM(migrad.shape, F32)] * 2 + [pltpu.SemaphoreType.DMA((2 * migrad.shape[0] // BLOCK,))], 20,
    )(dqkv_own, dqkv_oth, migrad, w_own, w_oth)[0]


def per_device(
    tokens, timesteps, src_len, tgt_len, sample_weight, w_qkv, bias_qv, w_out, bias_out, gain_attn, shift_attn,
    w_up, bias_up, w_down, bias_down, gain_mlp, shift_mlp, cotangent,
):
    rows, width = tokens.shape
    dp = lax.axis_size("dp")
    mp_index = lax.axis_index("mp")
    seqs = rows // LEN
    cols = bias_qv.shape[1]
    ff = bias_up.shape[0]
    plane = 4

    def swap(value):
        return lax.ppermute(value, "mp", [(0, 1), (1, 0)])

    def after(value, *earlier):
        return lax.optimization_barrier((value, *earlier))[0]

    qkv_oth_w = swap(w_qkv)
    wo_oth = swap(w_out)
    wu_oth = swap(w_up)
    wd_oth = swap(w_down)
    table, biases = prepare(timesteps, bias_qv, bias_up, seqs, width)
    biases_oth = swap(biases)

    qkv_own, prob_own, ctx_own, ctx_own_h, x_low, x_low_h = attend(src_len, tgt_len, (tokens, table), w_qkv, biases)
    qkv_oth, prob_oth, ctx_oth, ctx_oth_h, wo_own = attend(src_len, tgt_len, (x_low,), qkv_oth_w, biases_oth, w_out)
    (normed, inv, mid_low, hid_own, hid_oth, dg_own, dg_oth, layer_out, mgrad, sums_mlp) = mlp(
        src_len, tgt_len, sample_weight, tokens, table, ctx_own, ctx_oth, cotangent, wo_own, wo_oth, bias_out,
        gain_attn, shift_attn, w_up, wu_oth, biases, biases_oth, w_down, wd_oth, bias_down, gain_mlp, shift_mlp,
    )
    split = dp == 16
    in_plane = [[base + k for k in range(plane)] for base in range(0, dp, plane)]
    across = [[base * plane + k for base in range(dp // plane)] for k in range(plane)]

    def hop(value, bits):
        return lax.ppermute(value, "dp", [(i, i ^ bits) for i in range(dp)])

    def along(sa, ka, sb, kb):
        return ka, hop(sa, 1), kb, hop(sb, 2)

    def across(sa, ta, sb, tb):
        return ta, hop(sa, 2), tb, hop(sb, 1)

    (down_send,) = weight_grad(hid_oth, mgrad, dp, plane)
    down_recv = swap(down_send)
    pg_own, pg_oth, sum_up_own, sum_up_oth = pre_grads(after(mgrad, down_send), w_down, wd_oth, dg_own, dg_oth)
    down = weight_grad(hid_own, after(mgrad, pg_own), dp, plane, down_recv, split)
    if split:
        down = along(*down)
    (up_send,) = weight_grad(after(mid_low, down[0]), pg_oth, dp, plane)
    up_recv = swap(up_send)
    migrad, agrad, cg_own, cg_oth, sums_mid, qkv_oth, prob_oth = mid_grads(
        pg_own, pg_oth, after(mgrad, up_send), normed, inv, w_up, wu_oth, wo_own, wo_oth, gain_attn, qkv_oth, prob_oth
    )
    up = weight_grad(after(mid_low, agrad), pg_own, dp, plane, up_recv, split)
    if split:
        up = along(*up)
        down = across(*fold_first(after(down[0], up[0]), *down[1:]))
    dqkv_oth, sum_qv_oth, qkv_own, prob_own = attend_back(
        qkv_oth, prob_oth, after(cg_oth, up[0], down[0]), qkv_own, prob_own
    )
    dqkv_own, sum_qv_own = attend_back(qkv_own, prob_own, cg_own)
    keep, send = pack_sums(sums_mid, sums_mlp, sum_up_own, sum_up_oth, sum_qv_own, sum_qv_oth)
    attn_args = (x_low_h, dqkv_oth, ctx_oth_h, after(agrad, keep), dp)
    (attn_send,) = attn_grad(*attn_args, send) if split else attn_grad(*attn_args)
    attn_recv = swap(attn_send)
    attn_args = (x_low_h, dqkv_own, ctx_own_h)
    if split:
        up = across(*fold_first(after(up[0], attn_send), *up[1:]))
        send, keep_down = fold_second(after(down[0], up[0]), *down[1:], plane)
        down = keep_down, hop(send, plane)
        sa, ka, sb, kb, sums = attn_grad(*attn_args, after(agrad, keep_down), dp, keep, attn_recv)
        attn = along(sa, ka, sb, kb)
        send, keep_up = fold_second(after(up[0], ka), *up[1:], plane)
        up = keep_up, hop(send, plane)
        send, own = fold_outer(after(down[0], keep_up), down[1])
        down = own, hop(send, 2 * plane)
        tokens_grad = token_grads(dqkv_own, dqkv_oth, after(migrad, own), w_qkv, qkv_oth_w)
        grad_w_down = last_sum(after(down[0], tokens_grad), down[1])
        *folded, sums = attn_fold_first(after(attn[0], grad_w_down), *attn[1:], sums)
        attn = across(*folded)
        send, own = fold_outer(after(up[0], attn[0]), up[1])
        up = own, hop(send, 2 * plane)
        grad_w_up = last_sum(after(up[0], own), up[1])
        send, keep, sums = attn_fold_second(after(attn[0], grad_w_up), *attn[1:], sums)
        send, own, sums = attn_fold_outer(keep, hop(send, plane), sums)
        grad_w_qkv, grad_w_out, grad_rows, grad_bias_out, grad_bias_up, grad_bias_qv = attn_last(
            own, hop(send, 2 * plane), sums
        )
    else:
        in_plane = [[base + k for k in range(plane)] for base in range(0, dp, plane)]
        outside = [[base * plane + k for base in range(dp // plane)] for k in range(plane)]

        def scatter(value):
            value = lax.psum_scatter(value, "dp", scatter_dimension=0, axis_index_groups=in_plane)
            return lax.psum_scatter(value, "dp", scatter_dimension=0, axis_index_groups=outside).astype(F32)

        (attn,) = attn_grad(*attn_args, agrad, dp, None, attn_recv)
        tokens_grad = token_grads(dqkv_own, dqkv_oth, after(migrad, attn), w_qkv, qkv_oth_w)
        grad_w_down, grad_w_up, attn = scatter(down[0]), scatter(up[0]), scatter(attn)
        half = attn.shape[1] // 2
        grad_w_qkv, grad_w_out = attn[:3], jnp.concatenate([attn[3, :half], attn[3, half:]], axis=1)
        sums = lax.psum(keep + swap(send), "dp")
        whole = jnp.concatenate([sums[0:9], sums[9:18]], axis=1)
        grad_rows, grad_bias_out, grad_bias_up = whole[0:5], whole[5], whole[6:8].reshape(-1)
        grad_bias_qv = jnp.stack([sums[8], sums[17]])
    return (
        layer_out, tokens_grad, grad_w_qkv, grad_w_out, grad_w_up, grad_w_down,
        grad_bias_qv, grad_bias_up, grad_bias_out, grad_rows,
    )


def solution(mesh):
    in_specs = (
        P(("dp", "mp"), None), P("dp"), P("dp"), P("dp"), P("dp"),
        P(None, None, "mp"), P(None, "mp"), P("mp", None), P(), P(), P(),
        P(None, "mp"), P("mp"), P("mp", None), P(), P(), P(), P(("dp", "mp"), None),
    )
    out_specs = (
        P(("dp", "mp"), None), P(("dp", "mp"), None), P(None, "dp", "mp"), P(("mp", "dp"), None),
        P("dp", "mp"), P(("mp", "dp"), None), P(None, "mp"), P("mp"), P(), P(),
    )
    return jax.shard_map(per_device, mesh=mesh, in_specs=in_specs, out_specs=out_specs, check_vma=False)
```

```python
import functools
import math

import jax
import jax.numpy as jnp
from jax import lax
from jax.experimental import pallas as pl
from jax.experimental.pallas import tpu as pltpu
from jax.sharding import PartitionSpec as P

HD = 64
LEN = 128
PAIR = 2 * HD
NORM_EPS = 1e-05
MASK_FILL = -1e30
BF = jnp.bfloat16
F32 = jnp.float32
MIB = 1 << 20
ROWS = 16
SOFT = 32
BLOCK = 512
MLP_BLOCK = 256
MLP_ROWS = 32
AHEAD = 2

NN = (((1,), (0,)), ((), ()))
NT = (((1,), (1,)), ((), ()))
TN = (((0,), (0,)), ((), ()))

SPECS = {
    "v": pl.BlockSpec(memory_space=pltpu.VMEM),
    "h": pl.BlockSpec(memory_space=pltpu.HBM),
    "w": pl.BlockSpec(memory_space=pltpu.VMEM),
}
AHEAD_FLOPS = 3 * 10**10
LATE_FLOPS = 10**9


def mm(a, b, dims=NN):
    return lax.dot_general(a, b, dims, preferred_element_type=F32)


def params(mib):
    return pltpu.CompilerParams(vmem_limit_bytes=mib * MIB)


def local_call(kernel, out_shape, name, ins, outs, scratch=(), mib=16, flops=0, aliases=None):
    forced = {"v": pltpu.VMEM, "h": pltpu.HBM, "w": pltpu.HBM}

    def call(*args):
        args = [pltpu.with_memory_space_constraint(a, pltpu.HBM) if c in "hw" else a for a, c in zip(args, ins)]
        return pl.pallas_call(
            kernel,
            in_specs=[SPECS[c] for c in ins],
            out_specs=[SPECS[c] for c in outs],
            out_shape=[forced[c](a.shape, a.dtype) for a, c in zip(out_shape, outs)],
            scratch_shapes=list(scratch),
            input_output_aliases=aliases or {},
            compiler_params=params(mib),
            cost_estimate=pl.CostEstimate(flops=flops, bytes_accessed=0, transcendentals=0) if flops else None,
            name=name,
        )(*args)

    return call


class Copies:
    def __init__(self, sems):
        self.sems = sems
        self.started = []
        self.waiting = {}

    def start(self, src, dst, key=None):
        copy = pltpu.make_async_copy(src, dst, self.sems.at[len(self.started)])
        copy.start()
        self.started.append(copy)
        self.waiting.setdefault(key, []).append(copy)

    def wait(self, key=None):
        for copy in self.waiting.pop(key, ()):
            copy.wait()

    def wait_all(self):
        for key in list(self.waiting):
            self.wait(key)


def prepare_kernel(bqv_ref, bu_ref, bias_ref):
    cols = bqv_ref.shape[1]
    up = bu_ref[...].astype(F32).reshape(1, -1)
    rows = [bqv_ref[...].astype(F32)]
    rows += [up[:, i * cols : (i + 1) * cols] for i in range(up.shape[1] // cols)]
    rows += [jnp.zeros((bias_ref.shape[0] - 1 - len(rows), cols), F32)]
    bias_ref[...] = jnp.concatenate(rows, axis=0).astype(BF)


def prepare(bias_qv, bias_up):
    cols = bias_qv.shape[1]
    rows = -(-(2 + bias_up.shape[0] // cols) // 8) * 8
    return local_call(prepare_kernel, [jax.ShapeDtypeStruct((rows, cols), BF)], "prepare", "ww", "v")(bias_qv, bias_up)[0]


def fill_table(table_ref, steps_ref, base):
    seqs, width = table_ref.shape
    half = width // 2
    lane = lax.broadcasted_iota(jnp.int32, (seqs, half), 1).astype(F32)
    frequency = jnp.exp(-math.log(10000.0) * lane / half)
    row = lax.broadcasted_iota(jnp.int32, (seqs, half), 0)
    angles = jnp.zeros((seqs, half), F32)
    for s in range(seqs):
        angles = jnp.where(row == s, steps_ref[base + s].astype(F32), angles)
    angles = angles * frequency
    table_ref[:, :half] = jnp.sin(angles)
    table_ref[:, half:] = jnp.cos(angles)


def half_masks(rows, value=1.0):
    lane = lax.broadcasted_iota(jnp.int32, (rows, PAIR), 1)
    first = jnp.where(lane < HD, value, 0.0).astype(BF)
    second = jnp.where(lane < HD, 0.0, value).astype(BF)
    return first, second


def fold8(value):
    rows, cols = value.shape
    return jnp.sum(value.reshape(rows // 8, 8, cols), axis=0)


def side_by_side(ref):
    return jnp.concatenate([ref[i] for i in range(ref.shape[0])], axis=1)


def attend_kernel(first, src_hbm, tgt_hbm, *refs):
    if first:
        (tok_hbm, steps_hbm, w_hbm, bias_ref, qkv_out, prob_out, ctx_ref, ctx_out, x_ref, x_out, table_ref,
         src_ref, tgt_ref, qkv_ref, prob_ref, sems, steps_ref, tok_ref, w_ref) = refs
    else:
        (x_ref, w_ref, bias_ref, next_hbm, qkv_out, prob_out, ctx_ref, ctx_out, next_ref,
         src_ref, tgt_ref, qkv_ref, prob_ref, sems) = refs
    copies = Copies(sems)
    copies.start(src_hbm, src_ref, "m")
    copies.start(tgt_hbm, tgt_ref, "m")
    seqs = x_ref.shape[0] // LEN
    cols = w_ref.shape[2]
    base = lax.axis_index("mp") * seqs
    if first:
        copies.start(steps_hbm, steps_ref, "t")
        blocks = [slice(start, start + BLOCK) for start in range(0, x_ref.shape[0], BLOCK)]
        copies.start(tok_hbm.at[blocks[0], :], tok_ref.at[blocks[0], :], 0)
        for i in range(3):
            copies.start(w_hbm.at[i], w_ref.at[i], "w")
        for rows in blocks[1:]:
            copies.start(tok_hbm.at[rows, :], tok_ref.at[rows, :], rows.start)
        copies.wait("t")
        fill_table(table_ref, steps_ref, base)
    else:
        copies.start(next_hbm, next_ref)
    bias_q = bias_ref[0:1, :].astype(F32)
    bias_v = bias_ref[1:2, :].astype(F32)
    scale_a, scale_b = half_masks(LEN, HD**-0.5)
    one_a, one_b = half_masks(LEN)
    key_pos = lax.broadcasted_iota(jnp.int32, (SOFT, LEN), 1)

    def project(start):
        if first:
            copies.wait(start)
            for s in range(start // LEN, (start + BLOCK) // LEN):
                row = table_ref[s : s + 1, :]
                for r in range(s * LEN, (s + 1) * LEN, ROWS):
                    x_ref[r : r + ROWS, :] = (tok_ref[r : r + ROWS, :].astype(F32) + row).astype(BF)
        rows = slice(start, start + BLOCK)
        full = mm(x_ref[rows, :], w)
        qkv_ref[rows, :cols] = (full[:, :cols] + bias_q).astype(BF)
        qkv_ref[rows, cols : 2 * cols] = full[:, cols : 2 * cols].astype(BF)
        qkv_ref[rows, 2 * cols :] = (full[:, 2 * cols :] + bias_v).astype(BF)
        copies.start(qkv_ref.at[rows, :], qkv_out.at[rows, :])
        if first:
            copies.start(x_ref.at[rows, :], x_out.at[rows, :])

    def score(unit):
        s, j = unit
        rows = slice(s * LEN, (s + 1) * LEN)
        q2 = qkv_ref[rows, j * PAIR : (j + 1) * PAIR]
        k2 = qkv_ref[rows, cols + j * PAIR : cols + (j + 1) * PAIR]
        return mm(q2, jnp.concatenate([k2 * scale_a, k2 * scale_b], axis=0), NT)

    def finish(unit, scores):
        s, j = unit
        rows = slice(s * LEN, (s + 1) * LEN)
        live = key_pos < src_ref[base + s] + tgt_ref[base + s]
        low = []
        for r in range(0, LEN, SOFT):
            halves = []
            for h in range(2):
                part = jnp.where(live, scores[r : r + SOFT, h * LEN : (h + 1) * LEN], MASK_FILL)
                e = jnp.exp(part - jnp.max(part, axis=1, keepdims=True))
                halves.append(e * (1.0 / jnp.sum(e, axis=1, keepdims=True)))
            low.append(jnp.concatenate(halves, axis=1).astype(BF))
            prob_ref[s, j, r : r + SOFT, :] = low[-1]
        v2 = qkv_ref[rows, 2 * cols + j * PAIR : 2 * cols + (j + 1) * PAIR]
        vcat = jnp.concatenate([v2 * one_a, v2 * one_b], axis=0)
        ctx_ref[rows, j * PAIR : (j + 1) * PAIR] = mm(jnp.concatenate(low, axis=0), vcat).astype(BF)

    count = x_ref.shape[0]
    if first:
        copies.wait(0)
        copies.wait("w")
    w = side_by_side(w_ref)
    project(0)
    copies.wait("m")
    for start in range(0, count, BLOCK):
        if start + BLOCK < count:
            project(start + BLOCK)
        units = [(s, j) for s in range(start // LEN, (start + BLOCK) // LEN) for j in range(cols // PAIR)]
        pending = [score(u) for u in units[:AHEAD]]
        for i, unit in enumerate(units):
            if i + AHEAD < len(units):
                pending.append(score(units[i + AHEAD]))
            finish(unit, pending.pop(0))
            if unit[1] == cols // PAIR - 1:
                copies.start(prob_ref.at[unit[0]], prob_out.at[unit[0]])
        rows = slice(start, start + BLOCK)
        copies.start(ctx_ref.at[rows, :], ctx_out.at[rows, :])
    copies.wait_all()


def attend(src, tgt, x_args, w_half, bias_half, following=None):
    first = len(x_args) == 2
    rows, width = x_args[0].shape
    cols = w_half.shape[2]
    sds = jax.ShapeDtypeStruct
    shapes = [
        sds((rows, 3 * cols), BF),
        sds((rows // LEN, cols // PAIR, LEN, 2 * LEN), BF),
        sds((rows, cols), BF),
        sds((rows, cols), BF),
        sds((rows, width), BF),
        sds((rows, width), BF),
        sds((rows // LEN, width), F32),
    ]
    if not first:
        shapes = shapes[:4] + [sds(following.shape, BF)]
    scratch = [
        pltpu.SMEM(src.shape, jnp.int32),
        pltpu.SMEM(tgt.shape, jnp.int32),
        pltpu.VMEM(shapes[0].shape, BF),
        pltpu.VMEM(shapes[1].shape, BF),
        pltpu.SemaphoreType.DMA((4 * rows // BLOCK + rows // LEN + 6,)),
    ]
    if first:
        scratch += [pltpu.SMEM(x_args[1].shape, jnp.int32), pltpu.VMEM((rows, width), BF), pltpu.VMEM(w_half.shape, BF)]
    return local_call(
        functools.partial(attend_kernel, first), shapes, "attend",
        "hhhhhv" if first else "hhvvvh", "hhvhvhv" if first else "hhvhv", scratch, 20,
    )(src, tgt, *x_args, w_half, bias_half, *(() if first else (following,)))


def normalize(value):
    centred = value - jnp.mean(value, axis=1, keepdims=True)
    inv_std = lax.rsqrt(jnp.mean(centred * centred, axis=1, keepdims=True) + NORM_EPS)
    return centred * inv_std, inv_std


def normalize_back(scaled, normed, inv_std):
    return inv_std * (
        scaled
        - jnp.mean(scaled, axis=1, keepdims=True)
        - normed * jnp.mean(scaled * normed, axis=1, keepdims=True)
    )


def gelu_pair(v):
    cdf = 0.5 + 0.5 * lax.erf(v * math.sqrt(0.5))
    return v * cdf, cdf + v * jnp.exp2(v * v * (-0.5 * math.log2(math.e))) * (1.0 / math.sqrt(2.0 * math.pi))


def mlp_kernel(
    src_hbm, tgt_hbm, weight_hbm, tok_ref, table_ref, ctx_own_ref, ctx_oth_ref, cot_hbm,
    wo_own_ref, wo_oth_ref, bo_ref, ga_ref, sa_ref,
    wu_own_ref, wu_oth_ref, bu_own_ref, bu_oth_ref, wd_own_ref, wd_oth_ref, bd_ref, gm_ref, sm_ref,
    normed_ref, inv_ref, mid_ref, hid_own_ref, hid_oth_ref, dg_own_ref, dg_oth_ref,
    out_hbm, mgrad_ref, sums_ref, normed_f32, out_ref, cot_ref, src_ref, tgt_ref, weight_ref, sems,
):
    count = tok_ref.shape[0]
    base = lax.axis_index("mp") * (count // LEN)
    copies = Copies(sems)
    for hbm, smem in ((src_hbm, src_ref), (tgt_hbm, tgt_ref), (weight_hbm, weight_ref)):
        copies.start(hbm, smem, 0)
    for start in range(0, count, MLP_BLOCK):
        copies.start(cot_hbm.at[start : start + MLP_BLOCK, :], cot_ref.at[start : start + MLP_BLOCK, :], start)
    wo = jnp.concatenate([wo_own_ref[...], wo_oth_ref[...]], axis=0)
    halves = (
        (wu_own_ref, bu_own_ref, wd_own_ref, hid_own_ref, dg_own_ref),
        (wu_oth_ref, bu_oth_ref, wd_oth_ref, hid_oth_ref, dg_oth_ref),
    )

    def first_norm(start):
        rows = slice(start, start + MLP_BLOCK)
        attn_out = mm(jnp.concatenate([ctx_own_ref[rows, :], ctx_oth_ref[rows, :]], axis=1), wo)
        for r in range(0, MLP_BLOCK, MLP_ROWS):
            part = slice(start + r, start + r + MLP_ROWS)
            table_row = table_ref[(start + r) // LEN : (start + r) // LEN + 1, :]
            start_x = tok_ref[part, :].astype(F32) + table_row
            normed, inv = normalize(start_x + attn_out[r : r + MLP_ROWS] + bo_ref[...])
            normed_f32[part, :] = normed
            normed_ref[part, :] = normed.astype(BF)
            inv_ref[part, :] = inv
            mid_x = normed * ga_ref[...] + sa_ref[...]
            mid_ref[part, :] = mid_x.astype(BF)

    def up(unit):
        start, half = unit
        return mm(mid_ref[start : start + MLP_BLOCK, :], halves[half][0][...])

    def activate(unit, pre):
        start, half = unit
        _, bu_ref, wd_ref, hid_ref, dg_ref = halves[half]
        bias = jnp.concatenate([bu_ref[i : i + 1, :] for i in range(2, 2 + wd_ref.shape[0] // bu_ref.shape[1])], axis=1).astype(F32)
        for r in range(0, MLP_BLOCK, MLP_ROWS):
            part = slice(start + r, start + r + MLP_ROWS)
            hidden, slope = gelu_pair(pre[r : r + MLP_ROWS] + bias)
            hid_ref[part, :] = hidden.astype(BF)
            dg_ref[part, :] = slope.astype(BF)
        return mm(hid_ref[start : start + MLP_BLOCK, :], wd_ref[...])

    pos = lax.broadcasted_iota(jnp.int32, (MLP_ROWS, 1), 0)

    def second_norm(start, mlp_out, sums):
        copies.wait(start)
        for r in range(0, MLP_BLOCK, MLP_ROWS):
            part = slice(start + r, start + r + MLP_ROWS)
            seq = base + (start + r) // LEN
            mid_x = normed_f32[part, :] * ga_ref[...] + sa_ref[...]
            normed2, inv2 = normalize(mid_x + (mlp_out[r : r + MLP_ROWS] + bd_ref[...]))
            out_ref[part, :] = normed2 * gm_ref[...] + sm_ref[...]
            here = pos + (start + r) % LEN
            inside = (here >= src_ref[seq]) & (here < src_ref[seq] + tgt_ref[seq])
            e = cot_ref[part, :].astype(F32) * jnp.where(inside, weight_ref[seq], 0.0)
            mgrad = normalize_back(e * gm_ref[...], normed2, inv2).astype(BF)
            mgrad_ref[part, :] = mgrad
            new = [fold8(mgrad.astype(F32)), fold8(e * normed2), fold8(e)]
            sums = new if sums is None else [x + y for x, y in zip(sums, new)]
        rows = slice(start, start + MLP_BLOCK)
        copies.start(out_ref.at[rows, :], out_hbm.at[rows, :])
        return sums

    sums = None
    first_norm(0)
    units = [(start, half) for start in range(0, count, MLP_BLOCK) for half in range(2)]
    ready = up(units[0])
    waiting = None
    total = None
    for i, unit in enumerate(units):
        start, half = unit
        pre = ready
        if half == 0 and start + MLP_BLOCK < count:
            first_norm(start + MLP_BLOCK)
        if i + 1 < len(units):
            ready = up(units[i + 1])
        down = activate(unit, pre)
        if half == 0:
            if waiting is not None:
                sums = second_norm(*waiting, sums)
            total = down
        else:
            waiting = (start, total + down)
    sums = second_norm(*waiting, sums)
    sums_ref[...] = jnp.stack(sums)
    copies.wait_all()


def mlp(src, tgt, weight, tokens, table, ctx_own, ctx_oth, cot, wo_own, wo_oth, bo, ga, sa,
        wu_own, wu_oth, bu_own, bu_oth, wd_own, wd_oth, bd, gm, sm):
    rows, width = tokens.shape
    ff = wu_own.shape[1]
    sds = jax.ShapeDtypeStruct
    args = (src, tgt, weight, tokens, table, ctx_own, ctx_oth, cot, wo_own, wo_oth, bo, ga, sa,
            wu_own, wu_oth, bu_own, bu_oth, wd_own, wd_oth, bd, gm, sm)
    return local_call(
        mlp_kernel,
        [
            sds((rows, width), BF), sds((rows, 1), F32), sds((rows, width), BF),
            sds((rows, ff), BF), sds((rows, ff), BF), sds((rows, ff), BF), sds((rows, ff), BF),
            sds((rows, width), F32), sds((rows, width), BF), sds((3, 8, width), F32),
        ],
        "mlp",
        "hhhvvvvh" + "v" * 14,
        "vvvvvvvhvv",
        [pltpu.VMEM((rows, width), F32)] * 2 + [
            pltpu.VMEM((rows, width), BF), pltpu.SMEM(src.shape, jnp.int32), pltpu.SMEM(tgt.shape, jnp.int32),
            pltpu.SMEM(weight.shape, F32), pltpu.SemaphoreType.DMA((4 * rows // MLP_BLOCK + 3,)),
        ],
        20,
    )(*args)


def pre_kernel(mgrad_ref, wd_own_ref, wd_oth_ref, dg_own_ref, dg_oth_ref, pg_own_ref, pg_oth_ref, sum_own_ref, sum_oth_ref):
    halves = ((wd_oth_ref, dg_oth_ref, pg_oth_ref, sum_oth_ref), (wd_own_ref, dg_own_ref, pg_own_ref, sum_own_ref))
    units = [(h, c) for h in halves for c in range(0, wd_own_ref.shape[0], 512)]

    def product(unit):
        (wd_ref, _, _, _), c = unit
        return mm(mgrad_ref[...], wd_ref[c : c + 512, :], NT)

    ready = product(units[0])
    for i, ((_, dg_ref, pg_ref, sum_ref), c) in enumerate(units):
        full = ready
        if i + 1 < len(units):
            ready = product(units[i + 1])
        sums = None
        for r in range(0, full.shape[0], 32):
            pg = (full[r : r + 32] * dg_ref[r : r + 32, c : c + 512].astype(F32)).astype(BF)
            pg_ref[r : r + 32, c : c + 512] = pg
            new = fold8(pg.astype(F32))
            sums = new if sums is None else sums + new
        sum_ref[:, c : c + 512] = sums


def pre_grads(mgrad, wd_own, wd_oth, dg_own, dg_oth):
    rows = mgrad.shape[0]
    ff = wd_own.shape[0]
    sds = jax.ShapeDtypeStruct
    return local_call(
        pre_kernel,
        [sds((rows, ff), BF), sds((rows, ff), BF), sds((8, ff), F32), sds((8, ff), F32)],
        "pre_grads", "vvvvv", "vvvv", mib=12,
    )(mgrad, wd_own, wd_oth, dg_own, dg_oth)


def weight_pieces(lhs_ref, rhs_ref, size, chunk=384):
    m = lhs_ref.shape[1]
    ready = mm(lhs_ref[:, :chunk], rhs_ref[...], TN)
    for start in range(0, m, chunk):
        full = ready
        if start + chunk < m:
            ready = mm(lhs_ref[:, start + chunk : start + 2 * chunk], rhs_ref[...], TN)
        for first in range(0, chunk, size):
            yield (start + first) // size, full[first : first + size]


def attn_pieces(x_ref, dqkv_ref, ctx_ref, agrad_ref, size):
    cols = ctx_ref.shape[1]
    half = size // 2
    out_full = mm(ctx_ref[...], agrad_ref[...], TN)
    for index, qkv in weight_pieces(x_ref, dqkv_ref, size):
        rows = out_full[index * half : (index + 1) * half]
        blocks = [(0, qkv[:, i * cols : (i + 1) * cols], i) for i in range(3)]
        yield index, blocks + [(c * half, rows[:, c * cols : (c + 1) * cols], 3) for c in range(2)]


def coded(sums):
    high = sums.astype(BF).astype(F32)
    return jnp.concatenate([high, sums - high], axis=0).astype(BF)


def decoded(block):
    value = block.astype(F32)
    half = value.shape[0] // 2
    return value[:half] + value[half:]


def send_kernel(lhs_ref, rhs_ref, out_ref):
    plane, _, size, _ = out_ref.shape
    for index, value in weight_pieces(lhs_ref, rhs_ref, size):
        out_ref[index % plane, index // plane] = value.astype(BF)


def total_kernel(lhs_ref, rhs_ref, recv_ref, out_ref):
    plane, _, size, _ = out_ref.shape
    for index, value in weight_pieces(lhs_ref, rhs_ref, size):
        k, g = index % plane, index // plane
        out_ref[k, g] = (value + recv_ref[k, g].astype(F32)).astype(BF)


def split_kernel(lhs_ref, rhs_ref, recv_ref, sa_ref, ka_ref, sb_ref, kb_ref, held_ref):
    plane, size = held_ref.shape[1], held_ref.shape[2]
    me = lax.axis_index("dp") % plane
    for index, value in weight_pieces(lhs_ref, rhs_ref, size):
        k, g = index % plane, index // plane
        slot = g % held_ref.shape[0]
        held_ref[slot, k] = value + recv_ref[k, g].astype(F32)
        if k == plane - 1:
            for far in range(plane):
                y, x = divmod(far, 2)
                piece = held_ref[slot, me ^ far].astype(BF)
                half = piece.shape[1] // 2
                (sa_ref if x else ka_ref)[y, g] = piece[:, :half]
                (sb_ref if y else kb_ref)[x, g] = piece[:, half:]


def weight_grad(lhs, rhs, dp, plane, recv=None, split=False):
    size, n = lhs.shape[1] // dp, rhs.shape[1]
    outer = dp // plane
    sds = jax.ShapeDtypeStruct
    scratch = ()
    if recv is None:
        kernel, shapes, args = send_kernel, [sds((plane, outer, size, n), BF)], (lhs, rhs)
    elif split:
        kernel, shapes, args = split_kernel, [sds((2, outer, size, n // 2), BF)] * 4, (lhs, rhs, recv)
        scratch = [pltpu.VMEM((2, plane, size, n), F32)]
    else:
        kernel, shapes, args = total_kernel, [sds((plane, outer, size, n), BF)], (lhs, rhs, recv)
    return local_call(kernel, shapes, "wgrad", "v" * len(args), "v" * len(shapes), scratch, 12)(*args)


def attn_send_kernel(x_ref, dqkv_ref, ctx_ref, agrad_ref, *refs):
    *sums_refs, out_ref = refs
    _, size, cols = out_ref.shape
    outer = out_ref.shape[0] // 16
    for index, blocks in attn_pieces(x_ref, dqkv_ref, ctx_ref, agrad_ref, size):
        k, g = index % 4, index // 4
        for first, value, i in blocks:
            out_ref[(k * outer + g) * 4 + i, first : first + value.shape[0], :] = value.astype(BF)
    for sums_ref in sums_refs:
        out_ref[16 * outer] = coded(sums_ref[...])


def attn_hold(recv_ref, index, blocks, held_ref, slot, outer):
    k, g = index % 4, index // 4
    for first, value, i in blocks:
        held_ref[slot, k, i, first : first + value.shape[0], :] = value
    for i in range(4):
        arrived = recv_ref[(k * outer + g) * 4 + i]
        held_ref[slot, k, i] = held_ref[slot, k, i] + arrived.astype(F32)
    return k, g


def attn_total_kernel(x_ref, dqkv_ref, ctx_ref, agrad_ref, recv_ref, out_ref, held_ref):
    plane, outer, _, size, _ = out_ref.shape
    for index, blocks in attn_pieces(x_ref, dqkv_ref, ctx_ref, agrad_ref, size):
        slot = (index // plane) % 2
        k, g = attn_hold(recv_ref, index, blocks, held_ref, slot, outer)
        out_ref[k, g] = held_ref[slot, k].astype(BF)


def attn_split_kernel(
    x_ref, dqkv_ref, ctx_ref, agrad_ref, keep_ref, recv_ref,
    sa_ref, ka_ref, sb_ref, kb_ref, sa2_ref, ka2_ref, sb2_ref, kb2_ref, sums_ref, held_ref,
):
    plane = held_ref.shape[1]
    outer = kb_ref.shape[0] // 2
    me = lax.axis_index("dp") % plane
    sums = decoded(coded(keep_ref[...])) + decoded(recv_ref[16 * outer])
    sums_ref[...] = sums
    sa_ref[2 * outer] = coded(sums)
    for index, blocks in attn_pieces(x_ref, dqkv_ref, ctx_ref, agrad_ref, held_ref.shape[3]):
        slot = (index // plane) % 2
        k, g = attn_hold(recv_ref, index, blocks, held_ref, slot, outer)
        if k == plane - 1:
            for far in range(plane):
                y, x = divmod(far, 2)
                piece = held_ref[slot, me ^ far].astype(BF)
                (sa_ref if x else ka_ref)[y * outer + g] = piece[0]
                (sb_ref if y else kb_ref)[x * outer + g] = piece[2]
                (sa2_ref if x else ka2_ref)[y, g] = piece[1]
                (sb2_ref if y else kb2_ref)[x, g] = piece[3]


def attn_grad(x_low, dqkv, ctx, agrad, dp, sums=None, recv=None):
    size, cols = x_low.shape[1] // dp, ctx.shape[1]
    outer = dp // 4
    sds = jax.ShapeDtypeStruct
    block = lambda n: sds((n, size, cols), BF)
    args = (x_low, dqkv, ctx, agrad) + (() if sums is None else (sums,))
    scratch = ()
    if recv is None:
        kernel, shapes = attn_send_kernel, [block(16 * outer + (sums is not None))]
    else:
        args += (recv,)
        scratch = [pltpu.VMEM((2, 4, 4, size, cols), F32)]
        if sums is None:
            kernel, shapes = attn_total_kernel, [sds((4, outer, 4, size, cols), BF)]
        else:
            kernel = attn_split_kernel
            shapes = [block(2 * outer + 1)] + [block(2 * outer)] * 3
            shapes += [sds((2, outer, size, cols), BF)] * 4 + [sds(sums.shape, F32)]
    return local_call(kernel, shapes, "attn_wgrad", "v" * len(args), "v" * len(shapes), scratch, 16)(*args)


def add_low(one, two):
    return (one.astype(F32) + two.astype(F32)).astype(BF)


def fold_kernel(ka_ref, ra_ref, kb_ref, rb_ref, sa_ref, ta_ref, sb_ref, tb_ref):
    for k_ref, r_ref, s_ref, t_ref in ((ka_ref, ra_ref, sa_ref, ta_ref), (kb_ref, rb_ref, sb_ref, tb_ref)):
        for g in range(k_ref.shape[1]):
            s_ref[g] = add_low(k_ref[1, g], r_ref[1, g])
            t_ref[g] = add_low(k_ref[0, g], r_ref[0, g])


def fold_first(ka, ra, kb, rb):
    shape = jax.ShapeDtypeStruct(ka.shape[1:], BF)
    return local_call(fold_kernel, [shape] * 4, "fold_first", "vvvv", "vvvv")(ka, ra, kb, rb)


def attn_fold_kernel(ka_ref, ra_ref, kb_ref, rb_ref, old_ref, sa_ref, ta_ref, sb_ref, tb_ref, sums_ref):
    count = ta_ref.shape[0]
    for k_ref, r_ref, s_ref, t_ref in ((ka_ref, ra_ref, sa_ref, ta_ref), (kb_ref, rb_ref, sb_ref, tb_ref)):
        for g in range(count):
            s_ref[g] = add_low(k_ref[count + g], r_ref[count + g])
            t_ref[g] = add_low(k_ref[g], r_ref[g])
    sums = decoded(coded(old_ref[...])) + decoded(ra_ref[2 * count])
    sums_ref[...] = sums
    sa_ref[count] = coded(sums)


def attn_fold_first(ka, ra, kb, rb, sums):
    sds = jax.ShapeDtypeStruct
    count = ka.shape[0] // 2
    block = lambda n: sds((n,) + ka.shape[1:], BF)
    return local_call(
        attn_fold_kernel, [block(count + 1)] + [block(count)] * 3 + [sds(sums.shape, F32)], "fold_first", "vvvvv", "vvvvv"
    )(ka, ra, kb, rb, sums)


def plane_kernel(plane, ka_ref, ra_ref, kb_ref, rb_ref, send_ref, keep_ref):
    me = lax.axis_index("dp") // plane
    for far in range(ka_ref.shape[0]):
        g = me ^ far
        out_ref = send_ref if far % 2 else keep_ref
        half = ka_ref.shape[2]
        out_ref[far // 2, :, :half] = add_low(ka_ref[g], ra_ref[g])
        out_ref[far // 2, :, half:] = add_low(kb_ref[g], rb_ref[g])


def fold_second(ka, ra, kb, rb, plane, flops=AHEAD_FLOPS):
    outer, size, n = ka.shape
    return local_call(
        functools.partial(plane_kernel, plane), [jax.ShapeDtypeStruct((outer // 2, size, 2 * n), BF)] * 2,
        "fold_second", "vvvv", "vv", flops=flops,
    )(ka, ra, kb, rb)


def attn_plane_kernel(ka_ref, ra_ref, kb_ref, rb_ref, old_ref, send_ref, keep_ref, sums_ref):
    me = lax.axis_index("dp") // 4
    outer = ka_ref.shape[0]
    for far in range(outer):
        g = me ^ far
        out_ref = send_ref if far % 2 else keep_ref
        first = (far // 2) * 2
        out_ref[first] = add_low(ka_ref[g], ra_ref[g])
        out_ref[first + 1] = add_low(kb_ref[g], rb_ref[g])
    sums = decoded(coded(old_ref[...])) + decoded(ra_ref[outer])
    sums_ref[...] = sums
    send_ref[outer] = coded(sums)


def attn_fold_second(ka, ra, kb, rb, sums):
    sds = jax.ShapeDtypeStruct
    outer = ka.shape[0]
    block = lambda n: sds((n,) + ka.shape[1:], BF)
    return local_call(
        attn_plane_kernel, [block(outer + 1), block(outer), sds(sums.shape, F32)], "fold_second", "vvvvv", "vvv",
    )(ka, ra, kb, rb, sums)


def outer_kernel(keep_ref, arrived_ref, send_ref, own_ref):
    send_ref[...] = add_low(keep_ref[1], arrived_ref[1])
    own_ref[...] = keep_ref[0].astype(F32) + arrived_ref[0].astype(F32)


def fold_outer(keep, arrived):
    shape = keep.shape[1:]
    sds = jax.ShapeDtypeStruct
    return local_call(outer_kernel, [sds(shape, BF), sds(shape, F32)], "fold_outer", "vv", "vv")(keep, arrived)


def outer_pair_kernel(down_ref, ku_ref, ru_ref, send_ref, up_ref):
    size, width = ku_ref.shape[1], down_ref.shape[1]
    send_ref[0] = down_ref[...]
    for i in range(ku_ref.shape[2] // width):
        cols = slice(i * width, (i + 1) * width)
        send_ref[1, i * size : (i + 1) * size, :] = add_low(ku_ref[1, :, cols], ru_ref[1, :, cols])
    up_ref[...] = ku_ref[0].astype(F32) + ru_ref[0].astype(F32)


def fold_outer_pair(down, ku, ru):
    sds = jax.ShapeDtypeStruct
    shapes = [sds((2,) + down.shape, BF), sds(ku.shape[1:], F32)]
    return local_call(outer_pair_kernel, shapes, "fold_outer", "vvv", "vv")(down, ku, ru)


def last_pair_kernel(down_ref, up_ref, arrived_ref, down_out_ref, up_out_ref):
    size, width = up_ref.shape[0], down_ref.shape[1]
    down_out_ref[...] = down_ref[...] + arrived_ref[0].astype(F32)
    for i in range(up_ref.shape[1] // width):
        cols = slice(i * width, (i + 1) * width)
        up_out_ref[:, cols] = up_ref[:, cols] + arrived_ref[1, i * size : (i + 1) * size, :].astype(F32)


def last_pair(down, up, arrived):
    sds = jax.ShapeDtypeStruct
    return local_call(
        last_pair_kernel, [sds(down.shape, F32), sds(up.shape, F32)], "last_sum", "vvv", "ww"
    )(down, up, arrived)


def attn_outer_kernel(keep_ref, arrived_ref, old_ref, send_ref, own_ref, sums_ref):
    for i in range(2):
        send_ref[i] = add_low(keep_ref[2 + i], arrived_ref[2 + i])
        own_ref[i] = keep_ref[i].astype(F32) + arrived_ref[i].astype(F32)
    sums = decoded(coded(old_ref[...])) + decoded(arrived_ref[4])
    sums_ref[...] = sums
    send_ref[2] = coded(sums)


def attn_fold_outer(keep, arrived, sums):
    sds = jax.ShapeDtypeStruct
    tile = keep.shape[1:]
    return local_call(
        attn_outer_kernel, [sds((3,) + tile, BF), sds((2,) + tile, F32), sds(sums.shape, F32)], "fold_outer", "vvv", "vvv"
    )(keep, arrived, sums)


SUM_ROWS = 24


def unpack(sums, rows_ref, out_bias_ref, up_ref, qv_ref):
    whole = jnp.concatenate([sums[0:9], sums[9:18]], axis=1)
    width = whole.shape[1]
    rows_ref[...] = whole[0:5]
    out_bias_ref[...] = whole[5]
    up_ref[:width] = whole[6]
    up_ref[width:] = whole[7]
    qv_ref[0:1, :] = sums[8:9]
    qv_ref[1:2, :] = sums[17:18]


def attn_last_kernel(one_ref, arrived_ref, old_ref, two_ref, arrived2_ref, qkv_ref, out_ref, *sum_refs):
    _, size, cols = one_ref.shape
    qkv_ref[0] = one_ref[0] + arrived_ref[0].astype(F32)
    qkv_ref[2] = one_ref[1] + arrived_ref[1].astype(F32)
    total = two_ref[...] + arrived2_ref[...].astype(F32)
    qkv_ref[1] = total[:, :cols]
    out_ref[:, :cols] = total[: size // 2, cols:]
    out_ref[:, cols:] = total[size // 2 :, cols:]
    unpack(decoded(coded(old_ref[...])) + decoded(arrived_ref[2]), *sum_refs)


def attn_last(one, arrived, sums, two, arrived2):
    sds = jax.ShapeDtypeStruct
    _, size, cols = one.shape
    width = 2 * cols
    shapes = [
        sds((3, size, cols), F32), sds((size // 2, width), F32), sds((5, width), F32), sds((width,), F32),
        sds((2 * width,), F32), sds((2, cols), F32),
    ]
    return local_call(attn_last_kernel, shapes, "last_sum", "vvvvv", "w" * 6)(one, arrived, sums, two, arrived2)


def pack_kernel(mid_ref, mlp_ref, up_own_ref, up_oth_ref, qv_own_ref, qv_oth_ref, keep_ref, send_ref):
    cols = keep_ref.shape[1]
    row = lambda value: jnp.sum(value, axis=0, keepdims=True)
    for out_ref, up_ref, qv_ref in ((keep_ref, up_own_ref, qv_own_ref), (send_ref, up_oth_ref, qv_oth_ref)):
        rows = [row(mid_ref[0]), row(mid_ref[1])] + [row(mlp_ref[i]) for i in range(3)] + [row(mid_ref[2])]
        rows += [row(up_ref[:, i * 2 * cols : (i + 1) * 2 * cols]) for i in range(2)]
        rows.append(jnp.concatenate([row(qv_ref[0]), row(qv_ref[1])], axis=1))
        for i, value in enumerate(rows):
            out_ref[i : i + 1, :] = value[:, :cols]
            out_ref[9 + i : 10 + i, :] = value[:, cols:]
        out_ref[18:, :] = jnp.zeros((SUM_ROWS - 18, cols), F32)


def pack_sums(sums_mid, sums_mlp, up_own, up_oth, qv_own, qv_oth):
    shape = jax.ShapeDtypeStruct((SUM_ROWS, qv_own.shape[2]), F32)
    return local_call(pack_kernel, [shape] * 2, "pack_sums", "v" * 6, "vv")(sums_mid, sums_mlp, up_own, up_oth, qv_own, qv_oth)


def mid_kernel(
    pg_own_ref, pg_oth_ref, mgrad_ref, normed_ref, inv_ref, wu_own_ref, wu_oth_ref, wo_own_ref, wo_oth_ref, ga_ref,
    qkv_hbm, prob_hbm, migrad_hbm, agrad_ref, cg_own_ref, cg_oth_ref, sums_ref, qkv_ref, prob_ref, migrad_ref, sems,
):
    def product(first):
        rows = slice(first, first + BLOCK)
        return mm(pg_own_ref[rows, :], wu_own_ref[...], NT) + mm(pg_oth_ref[rows, :], wu_oth_ref[...], NT)

    sums = None
    count = mgrad_ref.shape[0]
    copies = Copies(sems)
    copies.start(qkv_hbm, qkv_ref)
    copies.start(prob_hbm, prob_ref)
    cols = cg_own_ref.shape[1]
    wo = jnp.concatenate([wo_own_ref[...], wo_oth_ref[...]], axis=0)
    ready = product(0)
    for first in range(0, count, BLOCK):
        back = ready
        if first + BLOCK < count:
            ready = product(first + BLOCK)
        for r in range(0, BLOCK, ROWS):
            part = slice(first + r, first + r + ROWS)
            e = back[r : r + ROWS] + mgrad_ref[part, :].astype(F32)
            normed = normed_ref[part, :].astype(F32)
            migrad = normalize_back(e * ga_ref[...], normed, inv_ref[part, :])
            migrad_ref[part, :] = migrad
            agrad = migrad.astype(BF)
            agrad_ref[part, :] = agrad
            new = [fold8(e * normed), fold8(e), fold8(agrad.astype(F32))]
            sums = new if sums is None else [x + y for x, y in zip(sums, new)]
        rows = slice(first, first + BLOCK)
        copies.start(migrad_ref.at[rows, :], migrad_hbm.at[rows, :])
        cgrad = mm(agrad_ref[rows, :], wo, NT).astype(BF)
        cg_own_ref[rows, :] = cgrad[:, :cols]
        cg_oth_ref[rows, :] = cgrad[:, cols:]
    sums_ref[...] = jnp.stack(sums)
    copies.wait_all()


def mid_grads(pg_own, pg_oth, mgrad, normed, inv, wu_own, wu_oth, wo_own, wo_oth, ga, qkv, probs):
    rows, width = mgrad.shape
    cols = wo_own.shape[0]
    sds = jax.ShapeDtypeStruct
    return local_call(
        mid_kernel,
        [
            sds((rows, width), F32), sds((rows, width), BF), sds((rows, cols), BF), sds((rows, cols), BF),
            sds((3, 8, width), F32), sds(qkv.shape, BF), sds(probs.shape, BF),
        ],
        "mid_grads", "vvvvvvvvvvhh", "hvvvvvv",
        [pltpu.VMEM((rows, width), F32)] + [pltpu.SemaphoreType.DMA((rows // BLOCK + 2,))], 20,
    )(pg_own, pg_oth, mgrad, normed, inv, wu_own, wu_oth, wo_own, wo_oth, ga, qkv, probs)


def attend_back_kernel(qkv_ref, prob_ref, cg_ref, *refs):
    if len(refs) > 2:
        next_qkv_hbm, next_prob_hbm, dqkv_ref, sums_ref, next_qkv_ref, next_prob_ref, sems = refs
        copies = Copies(sems)
        copies.start(next_qkv_hbm, next_qkv_ref)
        copies.start(next_prob_hbm, next_prob_ref)
    else:
        dqkv_ref, sums_ref = refs
    rows_all, cols = cg_ref.shape
    scale_a, scale_b = half_masks(LEN, HD**-0.5)
    one_a, one_b = half_masks(LEN)
    units = [(s, j) for s in range(rows_all // LEN) for j in range(cols // PAIR)]
    sums = {}

    def load(unit, i):
        s, j = unit
        return qkv_ref[s * LEN : (s + 1) * LEN, i * cols + j * PAIR : i * cols + (j + 1) * PAIR]

    def grad_probs(unit):
        s, j = unit
        v2 = load(unit, 2)
        g2 = cg_ref[s * LEN : (s + 1) * LEN, j * PAIR : (j + 1) * PAIR]
        return mm(g2, jnp.concatenate([v2 * one_a, v2 * one_b], axis=0), NT)

    def finish(unit, dprobs):
        s, j = unit
        rows = slice(s * LEN, (s + 1) * LEN)
        tall, flat = [], []
        for h in range(2):
            lanes = slice(h * LEN, (h + 1) * LEN)
            ds, low = [], []
            for r in range(0, LEN, SOFT):
                low.append(prob_ref[s, j, r : r + SOFT, lanes])
                p = low[-1].astype(F32)
                dp = dprobs[r : r + SOFT, lanes]
                ds.append((p * (dp - jnp.sum(p * dp, axis=1, keepdims=True))).astype(BF))
            flat.append(jnp.concatenate(ds, axis=0))
            tall.append(jnp.concatenate(low, axis=0))
        q2, k2 = load(unit, 0), load(unit, 1)
        g2 = cg_ref[rows, j * PAIR : (j + 1) * PAIR]
        qcat = jnp.concatenate([q2 * scale_a, q2 * scale_b], axis=0)
        kcat = jnp.concatenate([k2 * scale_a, k2 * scale_b], axis=0)
        gcat = jnp.concatenate([g2 * one_a, g2 * one_b], axis=0)
        dq = mm(jnp.concatenate(flat, axis=1), kcat).astype(BF)
        dk = mm(jnp.concatenate(flat, axis=0), qcat, TN).astype(BF)
        dv = mm(jnp.concatenate(tall, axis=0), gcat, TN).astype(BF)
        for i, value in enumerate((dq, dk, dv)):
            dqkv_ref[rows, i * cols + j * PAIR : i * cols + (j + 1) * PAIR] = value
        return fold8(dq.astype(F32)), fold8(dv.astype(F32))

    pending = [grad_probs(u) for u in units[:AHEAD]]
    for i, unit in enumerate(units):
        if i + AHEAD < len(units):
            pending.append(grad_probs(units[i + AHEAD]))
        new_q, new_v = finish(unit, pending.pop(0))
        j = unit[1]
        if j in sums:
            new_q, new_v = sums[j][0] + new_q, sums[j][1] + new_v
        sums[j] = (new_q, new_v)
    for j, (sum_q, sum_v) in sums.items():
        sums_ref[0, :, j * PAIR : (j + 1) * PAIR] = sum_q
        sums_ref[1, :, j * PAIR : (j + 1) * PAIR] = sum_v
    if len(refs) > 2:
        copies.wait_all()


def attend_back(qkv, probs, cgrad, *following):
    sds = jax.ShapeDtypeStruct
    shapes = [sds(qkv.shape, BF), sds((2, 8, cgrad.shape[1]), F32)] + [sds(a.shape, a.dtype) for a in following]
    return local_call(
        attend_back_kernel, shapes, "attend_back", "vvv" + "h" * len(following), "v" * len(shapes),
        [pltpu.SemaphoreType.DMA((2,))] if following else [], 12,
    )(qkv, probs, cgrad, *following)


def token_kernel(first, own_ref, oth_ref, migrad_hbm, w_own_ref, w_oth_ref, *refs):
    out_hbm, migrad_ref, out_ref, sems = refs[-4:]
    copies = Copies(sems)
    count = migrad_ref.shape[0]
    rows = slice(first, first + count)
    copies.start(migrad_hbm.at[rows, :], migrad_ref, "in")
    w = jnp.concatenate([side_by_side(w_own_ref), side_by_side(w_oth_ref)], axis=1)
    copies.wait("in")
    for r in range(0, count, 256):
        part = slice(first + r, first + r + 256)
        grads = jnp.concatenate([own_ref[part, :], oth_ref[part, :]], axis=1)
        out_ref[r : r + 256, :] = mm(grads, w, NT) + migrad_ref[r : r + 256, :]
        copies.start(out_ref.at[r : r + 256, :], out_hbm.at[part, :])
    copies.wait_all()


def token_grads(dqkv_own, dqkv_oth, migrad, w_own, w_oth, begun=None):
    rows, width = migrad.shape
    half = rows // 2
    extra = () if begun is None else (begun,)
    return local_call(
        functools.partial(token_kernel, half * len(extra)), [jax.ShapeDtypeStruct(migrad.shape, F32)], "token_grads",
        "vvhvv" + "h" * len(extra), "h",
        [pltpu.VMEM((half, width), F32)] * 2 + [pltpu.SemaphoreType.DMA((1 + half // 256,))], 16,
        aliases={5: 0} if extra else None,
    )(dqkv_own, dqkv_oth, migrad, w_own, w_oth, *extra)[0]


def per_device(
    tokens, timesteps, src_len, tgt_len, sample_weight, w_qkv, bias_qv, w_out, bias_out, gain_attn, shift_attn,
    w_up, bias_up, w_down, bias_down, gain_mlp, shift_mlp, cotangent,
):
    rows, width = tokens.shape
    dp = lax.axis_size("dp")
    mp_index = lax.axis_index("mp")
    cols = bias_qv.shape[1]
    ff = bias_up.shape[0]
    plane = 4

    def swap(value):
        return lax.ppermute(value, "mp", [(0, 1), (1, 0)])

    def after(value, *earlier):
        return lax.optimization_barrier((value, *earlier))[0]

    qkv_oth_w = swap(w_qkv)
    wo_oth = swap(w_out)
    wu_oth = swap(w_up)
    wd_oth = swap(w_down)
    biases = prepare(bias_qv, bias_up)
    biases_oth = swap(biases)

    qkv_own, prob_own, ctx_own, ctx_own_h, x_low, x_low_h, table = attend(
        src_len, tgt_len, (tokens, timesteps), w_qkv, biases
    )
    qkv_oth, prob_oth, ctx_oth, ctx_oth_h, wo_own = attend(src_len, tgt_len, (x_low,), qkv_oth_w, biases_oth, w_out)
    (normed, inv, mid_low, hid_own, hid_oth, dg_own, dg_oth, layer_out, mgrad, sums_mlp) = mlp(
        src_len, tgt_len, sample_weight, tokens, table, ctx_own, ctx_oth, cotangent, wo_own, wo_oth, bias_out,
        gain_attn, shift_attn, w_up, wu_oth, biases, biases_oth, w_down, wd_oth, bias_down, gain_mlp, shift_mlp,
    )
    split = dp == 16
    in_plane = [[base + k for k in range(plane)] for base in range(0, dp, plane)]
    across = [[base * plane + k for base in range(dp // plane)] for k in range(plane)]

    def hop(value, bits):
        return lax.ppermute(value, "dp", [(i, i ^ bits) for i in range(dp)])

    def along(sa, ka, sb, kb):
        return ka, hop(sa, 1), kb, hop(sb, 2)

    def across(sa, ta, sb, tb):
        return ta, hop(sa, 2), tb, hop(sb, 1)

    (down_send,) = weight_grad(hid_oth, mgrad, dp, plane)
    down_recv = swap(down_send)
    pg_own, pg_oth, sum_up_own, sum_up_oth = pre_grads(after(mgrad, down_send), w_down, wd_oth, dg_own, dg_oth)
    down = weight_grad(hid_own, after(mgrad, pg_own), dp, plane, down_recv, split)
    if split:
        down = along(*down)
    (up_send,) = weight_grad(after(mid_low, down[0]), pg_oth, dp, plane)
    up_recv = swap(up_send)
    migrad, agrad, cg_own, cg_oth, sums_mid, qkv_oth, prob_oth = mid_grads(
        pg_own, pg_oth, after(mgrad, up_send), normed, inv, w_up, wu_oth, wo_own, wo_oth, gain_attn, qkv_oth, prob_oth
    )
    up = weight_grad(after(mid_low, agrad), pg_own, dp, plane, up_recv, split)
    if split:
        up = along(*up)
        down = across(*fold_first(after(down[0], up[0]), *down[1:]))
    dqkv_oth, sum_qv_oth, qkv_own, prob_own = attend_back(
        qkv_oth, prob_oth, after(cg_oth, up[0], down[0]), qkv_own, prob_own
    )
    dqkv_own, sum_qv_own = attend_back(qkv_own, prob_own, cg_own)
    keep, send = pack_sums(sums_mid, sums_mlp, sum_up_own, sum_up_oth, sum_qv_own, sum_qv_oth)
    attn_args = (x_low_h, dqkv_oth, ctx_oth_h, after(agrad, keep), dp)
    (attn_send,) = attn_grad(*attn_args, send) if split else attn_grad(*attn_args)
    attn_recv = swap(attn_send)
    attn_args = (x_low_h, dqkv_own, ctx_own_h)
    if split:
        up = across(*fold_first(after(up[0], attn_send), *up[1:]))
        send, keep_down = fold_second(after(down[0], up[0]), *down[1:], plane)
        down = keep_down, hop(send, plane)
        *parts, sums = attn_grad(*attn_args, after(agrad, keep_down), dp, keep, attn_recv)
        one = along(*parts[:4])
        send, keep_up = fold_second(after(up[0], one[0]), *up[1:], plane)
        up = keep_up, hop(send, plane)
        send_down, own_down = fold_outer(after(down[0], keep_up), down[1])
        two = along(*parts[4:])
        token_args = dqkv_own, dqkv_oth, after(migrad, own_down), w_qkv, qkv_oth_w
        begun = token_grads(*token_args)
        *folded, sums = attn_fold_first(after(one[0], begun), *one[1:], sums)
        one = across(*folded)
        send, own_up = fold_outer_pair(after(send_down, one[0]), *up)
        arrived = hop(send, 2 * plane)
        tokens_grad = token_grads(*token_args[:3], w_qkv, qkv_oth_w, after(begun, own_up))
        two = across(*fold_first(after(two[0], tokens_grad), *two[1:]))
        send, keep_one, sums = attn_fold_second(after(one[0], two[0]), *one[1:], sums)
        one = keep_one, hop(send, plane)
        grad_w_down, grad_w_up = last_pair(after(own_down, keep_one), own_up, arrived)
        send, keep_two = fold_second(after(two[0], grad_w_up), *two[1:], plane, LATE_FLOPS)
        two = keep_two, hop(send, plane)
        send, own_one, sums = attn_fold_outer(after(one[0], keep_two), one[1], sums)
        one = own_one, hop(send, 2 * plane)
        send, own_two = fold_outer(after(two[0], own_one), two[1])
        two = own_two, hop(send, 2 * plane)
        grad_w_qkv, grad_w_out, grad_rows, grad_bias_out, grad_bias_up, grad_bias_qv = attn_last(*one, sums, *two)
    else:
        in_plane = [[base + k for k in range(plane)] for base in range(0, dp, plane)]
        outside = [[base * plane + k for base in range(dp // plane)] for k in range(plane)]

        def scatter(value):
            value = lax.psum_scatter(value, "dp", scatter_dimension=0, axis_index_groups=in_plane)
            return lax.psum_scatter(value, "dp", scatter_dimension=0, axis_index_groups=outside).astype(F32)

        (attn,) = attn_grad(*attn_args, agrad, dp, None, attn_recv)
        tokens_grad = token_grads(dqkv_own, dqkv_oth, after(migrad, attn), w_qkv, qkv_oth_w)
        grad_w_down, grad_w_up, attn = scatter(down[0]), scatter(up[0]), scatter(attn)
        half = attn.shape[1] // 2
        grad_w_qkv, grad_w_out = attn[:3], jnp.concatenate([attn[3, :half], attn[3, half:]], axis=1)
        sums = lax.psum(keep + swap(send), "dp")
        whole = jnp.concatenate([sums[0:9], sums[9:18]], axis=1)
        grad_rows, grad_bias_out, grad_bias_up = whole[0:5], whole[5], whole[6:8].reshape(-1)
        grad_bias_qv = jnp.stack([sums[8], sums[17]])
    return (
        layer_out, tokens_grad, grad_w_qkv, grad_w_out, grad_w_up, grad_w_down,
        grad_bias_qv, grad_bias_up, grad_bias_out, grad_rows,
    )


def solution(mesh):
    in_specs = (
        P(("dp", "mp"), None), P("dp"), P("dp"), P("dp"), P("dp"),
        P(None, None, "mp"), P(None, "mp"), P("mp", None), P(), P(), P(),
        P(None, "mp"), P("mp"), P("mp", None), P(), P(), P(), P(("dp", "mp"), None),
    )
    out_specs = (
        P(("dp", "mp"), None), P(("dp", "mp"), None), P(None, "dp", "mp"), P(("mp", "dp"), None),
        P("dp", "mp"), P(("mp", "dp"), None), P(None, "mp"), P("mp"), P(), P(),
    )
    return jax.shard_map(per_device, mesh=mesh, in_specs=in_specs, out_specs=out_specs, check_vma=False)
```

```python
import functools
import math

import jax
import jax.numpy as jnp
from jax import lax
from jax.experimental import pallas as pl
from jax.experimental.pallas import tpu as pltpu
from jax.sharding import PartitionSpec as P

HD = 64
LEN = 128
PAIR = 2 * HD
NORM_EPS = 1e-05
MASK_FILL = -1e30
BF = jnp.bfloat16
F32 = jnp.float32
MIB = 1 << 20
ROWS = 16
SOFT = 32
BLOCK = 512
MLP_BLOCK = 256
MLP_ROWS = 32
AHEAD = 2

NN = (((1,), (0,)), ((), ()))
NT = (((1,), (1,)), ((), ()))
TN = (((0,), (0,)), ((), ()))

SPECS = {
    "v": pl.BlockSpec(memory_space=pltpu.VMEM),
    "h": pl.BlockSpec(memory_space=pltpu.HBM),
    "w": pl.BlockSpec(memory_space=pltpu.VMEM),
}
AHEAD_FLOPS = 3 * 10**10
LATE_FLOPS = 10**9


def mm(a, b, dims=NN):
    return lax.dot_general(a, b, dims, preferred_element_type=F32)


def params(mib):
    return pltpu.CompilerParams(vmem_limit_bytes=mib * MIB)


def local_call(kernel, out_shape, name, ins, outs, scratch=(), mib=16, flops=0, aliases=None):
    forced = {"v": pltpu.VMEM, "h": pltpu.HBM, "w": pltpu.HBM}

    def call(*args):
        args = [pltpu.with_memory_space_constraint(a, pltpu.HBM) if c in "hw" else a for a, c in zip(args, ins)]
        return pl.pallas_call(
            kernel,
            in_specs=[SPECS[c] for c in ins],
            out_specs=[SPECS[c] for c in outs],
            out_shape=[forced[c](a.shape, a.dtype) for a, c in zip(out_shape, outs)],
            scratch_shapes=list(scratch),
            input_output_aliases=aliases or {},
            compiler_params=params(mib),
            cost_estimate=pl.CostEstimate(flops=flops, bytes_accessed=0, transcendentals=0) if flops else None,
            name=name,
        )(*args)

    return call


class Copies:
    def __init__(self, sems):
        self.sems = sems
        self.started = []
        self.waiting = {}

    def start(self, src, dst, key=None):
        copy = pltpu.make_async_copy(src, dst, self.sems.at[len(self.started)])
        copy.start()
        self.started.append(copy)
        self.waiting.setdefault(key, []).append(copy)

    def wait(self, key=None):
        for copy in self.waiting.pop(key, ()):
            copy.wait()

    def wait_all(self):
        for key in list(self.waiting):
            self.wait(key)


def prepare_kernel(bqv_ref, bu_ref, bias_ref):
    cols = bqv_ref.shape[1]
    up = bu_ref[...].astype(F32).reshape(1, -1)
    rows = [bqv_ref[...].astype(F32)]
    rows += [up[:, i * cols : (i + 1) * cols] for i in range(up.shape[1] // cols)]
    rows += [jnp.zeros((bias_ref.shape[0] - 1 - len(rows), cols), F32)]
    bias_ref[...] = jnp.concatenate(rows, axis=0).astype(BF)


def prepare(bias_qv, bias_up):
    cols = bias_qv.shape[1]
    rows = -(-(2 + bias_up.shape[0] // cols) // 8) * 8
    return local_call(prepare_kernel, [jax.ShapeDtypeStruct((rows, cols), BF)], "prepare", "ww", "v")(bias_qv, bias_up)[0]


def fill_table(table_ref, steps_ref, base):
    seqs, width = table_ref.shape
    half = width // 2
    lane = lax.broadcasted_iota(jnp.int32, (seqs, half), 1).astype(F32)
    frequency = jnp.exp(-math.log(10000.0) * lane / half)
    row = lax.broadcasted_iota(jnp.int32, (seqs, half), 0)
    angles = jnp.zeros((seqs, half), F32)
    for s in range(seqs):
        angles = jnp.where(row == s, steps_ref[base + s].astype(F32), angles)
    angles = angles * frequency
    table_ref[:, :half] = jnp.sin(angles)
    table_ref[:, half:] = jnp.cos(angles)


def half_masks(rows, value=1.0):
    lane = lax.broadcasted_iota(jnp.int32, (rows, PAIR), 1)
    first = jnp.where(lane < HD, value, 0.0).astype(BF)
    second = jnp.where(lane < HD, 0.0, value).astype(BF)
    return first, second


def fold8(value):
    rows, cols = value.shape
    return jnp.sum(value.reshape(rows // 8, 8, cols), axis=0)


def side_by_side(ref):
    return jnp.concatenate([ref[i] for i in range(ref.shape[0])], axis=1)


def attend_kernel(first, src_hbm, tgt_hbm, *refs):
    if first:
        (tok_hbm, steps_hbm, w_hbm, bias_ref, qkv_out, prob_out, ctx_ref, ctx_out, x_ref, x_out, table_ref,
         src_ref, tgt_ref, qkv_ref, prob_ref, sems, steps_ref, tok_ref, w_ref) = refs
    else:
        (x_ref, w_ref, bias_ref, next_hbm, qkv_out, prob_out, ctx_ref, ctx_out, next_ref,
         src_ref, tgt_ref, qkv_ref, prob_ref, sems) = refs
    copies = Copies(sems)
    copies.start(src_hbm, src_ref, "m")
    copies.start(tgt_hbm, tgt_ref, "m")
    seqs = x_ref.shape[0] // LEN
    cols = w_ref.shape[2]
    base = lax.axis_index("mp") * seqs
    if first:
        copies.start(steps_hbm, steps_ref, "t")
        blocks = [slice(start, start + BLOCK) for start in range(0, x_ref.shape[0], BLOCK)]
        copies.start(tok_hbm.at[blocks[0], :], tok_ref.at[blocks[0], :], 0)
        for i in range(3):
            copies.start(w_hbm.at[i], w_ref.at[i], "w")
        for rows in blocks[1:]:
            copies.start(tok_hbm.at[rows, :], tok_ref.at[rows, :], rows.start)
        copies.wait("t")
        fill_table(table_ref, steps_ref, base)
    else:
        copies.start(next_hbm, next_ref)
    bias_q = bias_ref[0:1, :].astype(F32)
    bias_v = bias_ref[1:2, :].astype(F32)
    scale_a, scale_b = half_masks(LEN, HD**-0.5)
    one_a, one_b = half_masks(LEN)
    key_pos = lax.broadcasted_iota(jnp.int32, (SOFT, LEN), 1)

    def project(start):
        if first:
            copies.wait(start)
            for s in range(start // LEN, (start + BLOCK) // LEN):
                row = table_ref[s : s + 1, :]
                for r in range(s * LEN, (s + 1) * LEN, ROWS):
                    x_ref[r : r + ROWS, :] = (tok_ref[r : r + ROWS, :].astype(F32) + row).astype(BF)
        rows = slice(start, start + BLOCK)
        full = mm(x_ref[rows, :], w)
        qkv_ref[rows, :cols] = (full[:, :cols] + bias_q).astype(BF)
        qkv_ref[rows, cols : 2 * cols] = full[:, cols : 2 * cols].astype(BF)
        qkv_ref[rows, 2 * cols :] = (full[:, 2 * cols :] + bias_v).astype(BF)
        copies.start(qkv_ref.at[rows, :], qkv_out.at[rows, :])
        if first:
            copies.start(x_ref.at[rows, :], x_out.at[rows, :])

    def score(unit):
        s, j = unit
        rows = slice(s * LEN, (s + 1) * LEN)
        q2 = qkv_ref[rows, j * PAIR : (j + 1) * PAIR]
        k2 = qkv_ref[rows, cols + j * PAIR : cols + (j + 1) * PAIR]
        return mm(q2, jnp.concatenate([k2 * scale_a, k2 * scale_b], axis=0), NT)

    def finish(unit, scores):
        s, j = unit
        rows = slice(s * LEN, (s + 1) * LEN)
        live = key_pos < src_ref[base + s] + tgt_ref[base + s]
        low = []
        for r in range(0, LEN, SOFT):
            halves = []
            for h in range(2):
                part = jnp.where(live, scores[r : r + SOFT, h * LEN : (h + 1) * LEN], MASK_FILL)
                e = jnp.exp(part - jnp.max(part, axis=1, keepdims=True))
                halves.append(e * (1.0 / jnp.sum(e, axis=1, keepdims=True)))
            low.append(jnp.concatenate(halves, axis=1).astype(BF))
            prob_ref[s, j, r : r + SOFT, :] = low[-1]
        v2 = qkv_ref[rows, 2 * cols + j * PAIR : 2 * cols + (j + 1) * PAIR]
        vcat = jnp.concatenate([v2 * one_a, v2 * one_b], axis=0)
        ctx_ref[rows, j * PAIR : (j + 1) * PAIR] = mm(jnp.concatenate(low, axis=0), vcat).astype(BF)

    count = x_ref.shape[0]
    if first:
        copies.wait(0)
        copies.wait("w")
    w = side_by_side(w_ref)
    project(0)
    copies.wait("m")
    for start in range(0, count, BLOCK):
        if start + BLOCK < count:
            project(start + BLOCK)
        units = [(s, j) for s in range(start // LEN, (start + BLOCK) // LEN) for j in range(cols // PAIR)]
        pending = [score(u) for u in units[:AHEAD]]
        for i, unit in enumerate(units):
            if i + AHEAD < len(units):
                pending.append(score(units[i + AHEAD]))
            finish(unit, pending.pop(0))
            if unit[1] == cols // PAIR - 1:
                copies.start(prob_ref.at[unit[0]], prob_out.at[unit[0]])
        rows = slice(start, start + BLOCK)
        copies.start(ctx_ref.at[rows, :], ctx_out.at[rows, :])
    copies.wait_all()


def attend(src, tgt, x_args, w_half, bias_half, following=None):
    first = len(x_args) == 2
    rows, width = x_args[0].shape
    cols = w_half.shape[2]
    sds = jax.ShapeDtypeStruct
    shapes = [
        sds((rows, 3 * cols), BF),
        sds((rows // LEN, cols // PAIR, LEN, 2 * LEN), BF),
        sds((rows, cols), BF),
        sds((rows, cols), BF),
        sds((rows, width), BF),
        sds((rows, width), BF),
        sds((rows // LEN, width), F32),
    ]
    if not first:
        shapes = shapes[:4] + [sds(following.shape, BF)]
    scratch = [
        pltpu.SMEM(src.shape, jnp.int32),
        pltpu.SMEM(tgt.shape, jnp.int32),
        pltpu.VMEM(shapes[0].shape, BF),
        pltpu.VMEM(shapes[1].shape, BF),
        pltpu.SemaphoreType.DMA((4 * rows // BLOCK + rows // LEN + 6,)),
    ]
    if first:
        scratch += [pltpu.SMEM(x_args[1].shape, jnp.int32), pltpu.VMEM((rows, width), BF), pltpu.VMEM(w_half.shape, BF)]
    return local_call(
        functools.partial(attend_kernel, first), shapes, "attend",
        "hhhhhv" if first else "hhvvvh", "hhvhvhv" if first else "hhvhv", scratch, 20,
    )(src, tgt, *x_args, w_half, bias_half, *(() if first else (following,)))


def normalize(value):
    centred = value - jnp.mean(value, axis=1, keepdims=True)
    inv_std = lax.rsqrt(jnp.mean(centred * centred, axis=1, keepdims=True) + NORM_EPS)
    return centred * inv_std, inv_std


def normalize_back(scaled, normed, inv_std):
    return inv_std * (
        scaled
        - jnp.mean(scaled, axis=1, keepdims=True)
        - normed * jnp.mean(scaled * normed, axis=1, keepdims=True)
    )


def gelu_pair(v):
    cdf = 0.5 + 0.5 * lax.erf(v * math.sqrt(0.5))
    return v * cdf, cdf + v * jnp.exp2(v * v * (-0.5 * math.log2(math.e))) * (1.0 / math.sqrt(2.0 * math.pi))


def mlp_kernel(
    src_hbm, tgt_hbm, weight_hbm, tok_ref, table_ref, ctx_own_ref, ctx_oth_ref, cot_hbm,
    wo_own_ref, wo_oth_ref, bo_ref, ga_ref, sa_ref,
    wu_own_ref, wu_oth_ref, bu_own_ref, bu_oth_ref, wd_own_ref, wd_oth_ref, bd_ref, gm_ref, sm_ref,
    normed_ref, inv_ref, mid_ref, hid_own_ref, hid_oth_ref, dg_own_ref, dg_oth_ref,
    out_hbm, mgrad_ref, sums_ref, normed_f32, out_ref, cot_ref, src_ref, tgt_ref, weight_ref, sems,
):
    count = tok_ref.shape[0]
    base = lax.axis_index("mp") * (count // LEN)
    copies = Copies(sems)
    for hbm, smem in ((src_hbm, src_ref), (tgt_hbm, tgt_ref), (weight_hbm, weight_ref)):
        copies.start(hbm, smem, 0)
    for start in range(0, count, MLP_BLOCK):
        copies.start(cot_hbm.at[start : start + MLP_BLOCK, :], cot_ref.at[start : start + MLP_BLOCK, :], start)
    wo = jnp.concatenate([wo_own_ref[...], wo_oth_ref[...]], axis=0)
    halves = (
        (wu_own_ref, bu_own_ref, wd_own_ref, hid_own_ref, dg_own_ref),
        (wu_oth_ref, bu_oth_ref, wd_oth_ref, hid_oth_ref, dg_oth_ref),
    )

    def first_norm(start):
        rows = slice(start, start + MLP_BLOCK)
        attn_out = mm(jnp.concatenate([ctx_own_ref[rows, :], ctx_oth_ref[rows, :]], axis=1), wo)
        for r in range(0, MLP_BLOCK, MLP_ROWS):
            part = slice(start + r, start + r + MLP_ROWS)
            table_row = table_ref[(start + r) // LEN : (start + r) // LEN + 1, :]
            start_x = tok_ref[part, :].astype(F32) + table_row
            normed, inv = normalize(start_x + attn_out[r : r + MLP_ROWS] + bo_ref[...])
            normed_f32[part, :] = normed
            normed_ref[part, :] = normed.astype(BF)
            inv_ref[part, :] = inv
            mid_x = normed * ga_ref[...] + sa_ref[...]
            mid_ref[part, :] = mid_x.astype(BF)

    def up(unit):
        start, half = unit
        return mm(mid_ref[start : start + MLP_BLOCK, :], halves[half][0][...])

    def activate(unit, pre):
        start, half = unit
        _, bu_ref, wd_ref, hid_ref, dg_ref = halves[half]
        bias = jnp.concatenate([bu_ref[i : i + 1, :] for i in range(2, 2 + wd_ref.shape[0] // bu_ref.shape[1])], axis=1).astype(F32)
        for r in range(0, MLP_BLOCK, MLP_ROWS):
            part = slice(start + r, start + r + MLP_ROWS)
            hidden, slope = gelu_pair(pre[r : r + MLP_ROWS] + bias)
            hid_ref[part, :] = hidden.astype(BF)
            dg_ref[part, :] = slope.astype(BF)
        return mm(hid_ref[start : start + MLP_BLOCK, :], wd_ref[...])

    pos = lax.broadcasted_iota(jnp.int32, (MLP_ROWS, 1), 0)

    def second_norm(start, mlp_out, sums):
        for r in range(0, MLP_BLOCK, MLP_ROWS):
            part = slice(start + r, start + r + MLP_ROWS)
            seq = base + (start + r) // LEN
            mid_x = normed_f32[part, :] * ga_ref[...] + sa_ref[...]
            normed2, inv2 = normalize(mid_x + (mlp_out[r : r + MLP_ROWS] + bd_ref[...]))
            out_ref[part, :] = normed2 * gm_ref[...] + sm_ref[...]
            here = pos + (start + r) % LEN
            inside = (here >= src_ref[seq]) & (here < src_ref[seq] + tgt_ref[seq])
            e = cot_ref[part, :].astype(F32) * jnp.where(inside, weight_ref[seq], 0.0)
            mgrad = normalize_back(e * gm_ref[...], normed2, inv2).astype(BF)
            mgrad_ref[part, :] = mgrad
            new = [fold8(mgrad.astype(F32)), fold8(e * normed2), fold8(e)]
            sums = new if sums is None else [x + y for x, y in zip(sums, new)]
        return sums

    sums = None
    first_norm(0)
    for start in range(0, count, MLP_BLOCK):
        copies.wait(start)
    units = [(start, half) for start in range(0, count, MLP_BLOCK) for half in range(2)]
    ready = up(units[0])
    waiting = None
    total = None
    for i, unit in enumerate(units):
        start, half = unit
        pre = ready
        if half == 0 and start + MLP_BLOCK < count:
            first_norm(start + MLP_BLOCK)
        if i + 1 < len(units):
            ready = up(units[i + 1])
        down = activate(unit, pre)
        if half == 0:
            if waiting is not None:
                sums = second_norm(*waiting, sums)
            total = down
        else:
            waiting = (start, total + down)
    done = slice(0, count - MLP_BLOCK)
    copies.start(out_ref.at[done, :], out_hbm.at[done, :])
    sums = second_norm(*waiting, sums)
    sums_ref[...] = jnp.stack(sums)
    done = slice(count - MLP_BLOCK, count)
    copies.start(out_ref.at[done, :], out_hbm.at[done, :])
    copies.wait_all()


def mlp(src, tgt, weight, tokens, table, ctx_own, ctx_oth, cot, wo_own, wo_oth, bo, ga, sa,
        wu_own, wu_oth, bu_own, bu_oth, wd_own, wd_oth, bd, gm, sm):
    rows, width = tokens.shape
    ff = wu_own.shape[1]
    sds = jax.ShapeDtypeStruct
    args = (src, tgt, weight, tokens, table, ctx_own, ctx_oth, cot, wo_own, wo_oth, bo, ga, sa,
            wu_own, wu_oth, bu_own, bu_oth, wd_own, wd_oth, bd, gm, sm)
    return local_call(
        mlp_kernel,
        [
            sds((rows, width), BF), sds((rows, 1), F32), sds((rows, width), BF),
            sds((rows, ff), BF), sds((rows, ff), BF), sds((rows, ff), BF), sds((rows, ff), BF),
            sds((rows, width), F32), sds((rows, width), BF), sds((3, 8, width), F32),
        ],
        "mlp",
        "hhhvvvvh" + "v" * 14,
        "vvvvvvvhvv",
        [pltpu.VMEM((rows, width), F32)] * 2 + [
            pltpu.VMEM((rows, width), BF), pltpu.SMEM(src.shape, jnp.int32), pltpu.SMEM(tgt.shape, jnp.int32),
            pltpu.SMEM(weight.shape, F32), pltpu.SemaphoreType.DMA((4 * rows // MLP_BLOCK + 3,)),
        ],
        20,
    )(*args)


def pre_kernel(mgrad_ref, wd_own_ref, wd_oth_ref, dg_own_ref, dg_oth_ref, pg_own_ref, pg_oth_ref, sum_own_ref, sum_oth_ref):
    halves = ((wd_oth_ref, dg_oth_ref, pg_oth_ref, sum_oth_ref), (wd_own_ref, dg_own_ref, pg_own_ref, sum_own_ref))
    units = [(h, c) for h in halves for c in range(0, wd_own_ref.shape[0], 512)]

    def product(unit):
        (wd_ref, _, _, _), c = unit
        return mm(mgrad_ref[...], wd_ref[c : c + 512, :], NT)

    ready = product(units[0])
    for i, ((_, dg_ref, pg_ref, sum_ref), c) in enumerate(units):
        full = ready
        if i + 1 < len(units):
            ready = product(units[i + 1])
        sums = None
        for r in range(0, full.shape[0], 32):
            pg = (full[r : r + 32] * dg_ref[r : r + 32, c : c + 512].astype(F32)).astype(BF)
            pg_ref[r : r + 32, c : c + 512] = pg
            new = fold8(pg.astype(F32))
            sums = new if sums is None else sums + new
        sum_ref[:, c : c + 512] = sums


def pre_grads(mgrad, wd_own, wd_oth, dg_own, dg_oth):
    rows = mgrad.shape[0]
    ff = wd_own.shape[0]
    sds = jax.ShapeDtypeStruct
    return local_call(
        pre_kernel,
        [sds((rows, ff), BF), sds((rows, ff), BF), sds((8, ff), F32), sds((8, ff), F32)],
        "pre_grads", "vvvvv", "vvvv", mib=12,
    )(mgrad, wd_own, wd_oth, dg_own, dg_oth)


def weight_pieces(lhs_ref, rhs_ref, size, chunk=384):
    m = lhs_ref.shape[1]
    ready = mm(lhs_ref[:, :chunk], rhs_ref[...], TN)
    for start in range(0, m, chunk):
        full = ready
        if start + chunk < m:
            ready = mm(lhs_ref[:, start + chunk : start + 2 * chunk], rhs_ref[...], TN)
        for first in range(0, chunk, size):
            yield (start + first) // size, full[first : first + size]


def attn_pieces(x_ref, dqkv_ref, ctx_ref, agrad_ref, size):
    cols = ctx_ref.shape[1]
    half = size // 2
    out_full = mm(ctx_ref[...], agrad_ref[...], TN)
    for index, qkv in weight_pieces(x_ref, dqkv_ref, size):
        rows = out_full[index * half : (index + 1) * half]
        blocks = [(0, qkv[:, i * cols : (i + 1) * cols], i) for i in range(3)]
        yield index, blocks + [(c * half, rows[:, c * cols : (c + 1) * cols], 3) for c in range(2)]


def coded(sums):
    high = sums.astype(BF).astype(F32)
    return jnp.concatenate([high, sums - high], axis=0).astype(BF)


def decoded(block):
    value = block.astype(F32)
    half = value.shape[0] // 2
    return value[:half] + value[half:]


def send_kernel(lhs_ref, rhs_ref, out_ref):
    plane, _, size, _ = out_ref.shape
    for index, value in weight_pieces(lhs_ref, rhs_ref, size):
        out_ref[index % plane, index // plane] = value.astype(BF)


def total_kernel(lhs_ref, rhs_ref, recv_ref, out_ref):
    plane, _, size, _ = out_ref.shape
    for index, value in weight_pieces(lhs_ref, rhs_ref, size):
        k, g = index % plane, index // plane
        out_ref[k, g] = (value + recv_ref[k, g].astype(F32)).astype(BF)


def split_kernel(lhs_ref, rhs_ref, recv_ref, sa_ref, ka_ref, sb_ref, kb_ref, held_ref):
    plane, size = held_ref.shape[1], held_ref.shape[2]
    me = lax.axis_index("dp") % plane
    for index, value in weight_pieces(lhs_ref, rhs_ref, size):
        k, g = index % plane, index // plane
        slot = g % held_ref.shape[0]
        held_ref[slot, k] = value + recv_ref[k, g].astype(F32)
        if k == plane - 1:
            for far in range(plane):
                y, x = divmod(far, 2)
                piece = held_ref[slot, me ^ far].astype(BF)
                half = piece.shape[1] // 2
                (sa_ref if x else ka_ref)[y, g] = piece[:, :half]
                (sb_ref if y else kb_ref)[x, g] = piece[:, half:]


def weight_grad(lhs, rhs, dp, plane, recv=None, split=False):
    size, n = lhs.shape[1] // dp, rhs.shape[1]
    outer = dp // plane
    sds = jax.ShapeDtypeStruct
    scratch = ()
    if recv is None:
        kernel, shapes, args = send_kernel, [sds((plane, outer, size, n), BF)], (lhs, rhs)
    elif split:
        kernel, shapes, args = split_kernel, [sds((2, outer, size, n // 2), BF)] * 4, (lhs, rhs, recv)
        scratch = [pltpu.VMEM((2, plane, size, n), F32)]
    else:
        kernel, shapes, args = total_kernel, [sds((plane, outer, size, n), BF)], (lhs, rhs, recv)
    return local_call(kernel, shapes, "wgrad", "v" * len(args), "v" * len(shapes), scratch, 12)(*args)


def attn_send_kernel(x_ref, dqkv_ref, ctx_ref, agrad_ref, *refs):
    *sums_refs, out_ref = refs
    _, size, cols = out_ref.shape
    outer = out_ref.shape[0] // 16
    for index, blocks in attn_pieces(x_ref, dqkv_ref, ctx_ref, agrad_ref, size):
        k, g = index % 4, index // 4
        for first, value, i in blocks:
            out_ref[(k * outer + g) * 4 + i, first : first + value.shape[0], :] = value.astype(BF)
    for sums_ref in sums_refs:
        out_ref[16 * outer] = coded(sums_ref[...])


def attn_hold(recv_ref, index, blocks, held_ref, slot, outer):
    k, g = index % 4, index // 4
    for first, value, i in blocks:
        held_ref[slot, k, i, first : first + value.shape[0], :] = value
    for i in range(4):
        arrived = recv_ref[(k * outer + g) * 4 + i]
        held_ref[slot, k, i] = held_ref[slot, k, i] + arrived.astype(F32)
    return k, g


def attn_total_kernel(x_ref, dqkv_ref, ctx_ref, agrad_ref, recv_ref, out_ref, held_ref):
    plane, outer, _, size, _ = out_ref.shape
    for index, blocks in attn_pieces(x_ref, dqkv_ref, ctx_ref, agrad_ref, size):
        slot = (index // plane) % 2
        k, g = attn_hold(recv_ref, index, blocks, held_ref, slot, outer)
        out_ref[k, g] = held_ref[slot, k].astype(BF)


def attn_split_kernel(
    x_ref, dqkv_ref, ctx_ref, agrad_ref, keep_ref, recv_ref,
    sa_ref, ka_ref, sb_ref, kb_ref, sa2_ref, ka2_ref, sb2_ref, kb2_ref, sums_ref, held_ref,
):
    plane = held_ref.shape[1]
    outer = kb_ref.shape[0] // 2
    me = lax.axis_index("dp") % plane
    sums = decoded(coded(keep_ref[...])) + decoded(recv_ref[16 * outer])
    sums_ref[...] = sums
    sa_ref[2 * outer] = coded(sums)
    for index, blocks in attn_pieces(x_ref, dqkv_ref, ctx_ref, agrad_ref, held_ref.shape[3]):
        slot = (index // plane) % 2
        k, g = attn_hold(recv_ref, index, blocks, held_ref, slot, outer)
        if k == plane - 1:
            for far in range(plane):
                y, x = divmod(far, 2)
                piece = held_ref[slot, me ^ far].astype(BF)
                (sa_ref if x else ka_ref)[y * outer + g] = piece[0]
                (sb_ref if y else kb_ref)[x * outer + g] = piece[2]
                (sa2_ref if x else ka2_ref)[y, g] = piece[1]
                (sb2_ref if y else kb2_ref)[x, g] = piece[3]


def attn_grad(x_low, dqkv, ctx, agrad, dp, sums=None, recv=None):
    size, cols = x_low.shape[1] // dp, ctx.shape[1]
    outer = dp // 4
    sds = jax.ShapeDtypeStruct
    block = lambda n: sds((n, size, cols), BF)
    args = (x_low, dqkv, ctx, agrad) + (() if sums is None else (sums,))
    scratch = ()
    if recv is None:
        kernel, shapes = attn_send_kernel, [block(16 * outer + (sums is not None))]
    else:
        args += (recv,)
        scratch = [pltpu.VMEM((2, 4, 4, size, cols), F32)]
        if sums is None:
            kernel, shapes = attn_total_kernel, [sds((4, outer, 4, size, cols), BF)]
        else:
            kernel = attn_split_kernel
            shapes = [block(2 * outer + 1)] + [block(2 * outer)] * 3
            shapes += [sds((2, outer, size, cols), BF)] * 4 + [sds(sums.shape, F32)]
    return local_call(kernel, shapes, "attn_wgrad", "v" * len(args), "v" * len(shapes), scratch, 16)(*args)


def add_low(one, two):
    return (one.astype(F32) + two.astype(F32)).astype(BF)


def fold_kernel(ka_ref, ra_ref, kb_ref, rb_ref, sa_ref, ta_ref, sb_ref, tb_ref):
    for k_ref, r_ref, s_ref, t_ref in ((ka_ref, ra_ref, sa_ref, ta_ref), (kb_ref, rb_ref, sb_ref, tb_ref)):
        for g in range(k_ref.shape[1]):
            s_ref[g] = add_low(k_ref[1, g], r_ref[1, g])
            t_ref[g] = add_low(k_ref[0, g], r_ref[0, g])


def fold_first(ka, ra, kb, rb):
    shape = jax.ShapeDtypeStruct(ka.shape[1:], BF)
    return local_call(fold_kernel, [shape] * 4, "fold_first", "vvvv", "vvvv")(ka, ra, kb, rb)


def attn_fold_kernel(ka_ref, ra_ref, kb_ref, rb_ref, old_ref, sa_ref, ta_ref, sb_ref, tb_ref, sums_ref):
    count = ta_ref.shape[0]
    for k_ref, r_ref, s_ref, t_ref in ((ka_ref, ra_ref, sa_ref, ta_ref), (kb_ref, rb_ref, sb_ref, tb_ref)):
        for g in range(count):
            s_ref[g] = add_low(k_ref[count + g], r_ref[count + g])
            t_ref[g] = add_low(k_ref[g], r_ref[g])
    sums = decoded(coded(old_ref[...])) + decoded(ra_ref[2 * count])
    sums_ref[...] = sums
    sa_ref[count] = coded(sums)


def attn_fold_first(ka, ra, kb, rb, sums):
    sds = jax.ShapeDtypeStruct
    count = ka.shape[0] // 2
    block = lambda n: sds((n,) + ka.shape[1:], BF)
    return local_call(
        attn_fold_kernel, [block(count + 1)] + [block(count)] * 3 + [sds(sums.shape, F32)], "fold_first", "vvvvv", "vvvvv"
    )(ka, ra, kb, rb, sums)


def plane_kernel(plane, ka_ref, ra_ref, kb_ref, rb_ref, send_ref, keep_ref):
    me = lax.axis_index("dp") // plane
    for far in range(ka_ref.shape[0]):
        g = me ^ far
        out_ref = send_ref if far % 2 else keep_ref
        half = ka_ref.shape[2]
        out_ref[far // 2, :, :half] = add_low(ka_ref[g], ra_ref[g])
        out_ref[far // 2, :, half:] = add_low(kb_ref[g], rb_ref[g])


def fold_second(ka, ra, kb, rb, plane, flops=AHEAD_FLOPS):
    outer, size, n = ka.shape
    return local_call(
        functools.partial(plane_kernel, plane), [jax.ShapeDtypeStruct((outer // 2, size, 2 * n), BF)] * 2,
        "fold_second", "vvvv", "vv", flops=flops,
    )(ka, ra, kb, rb)


def attn_plane_kernel(ka_ref, ra_ref, kb_ref, rb_ref, old_ref, send_ref, keep_ref, sums_ref):
    me = lax.axis_index("dp") // 4
    outer = ka_ref.shape[0]
    for far in range(outer):
        g = me ^ far
        out_ref = send_ref if far % 2 else keep_ref
        first = (far // 2) * 2
        out_ref[first] = add_low(ka_ref[g], ra_ref[g])
        out_ref[first + 1] = add_low(kb_ref[g], rb_ref[g])
    sums = decoded(coded(old_ref[...])) + decoded(ra_ref[outer])
    sums_ref[...] = sums
    send_ref[outer] = coded(sums)


def attn_fold_second(ka, ra, kb, rb, sums):
    sds = jax.ShapeDtypeStruct
    outer = ka.shape[0]
    block = lambda n: sds((n,) + ka.shape[1:], BF)
    return local_call(
        attn_plane_kernel, [block(outer + 1), block(outer), sds(sums.shape, F32)], "fold_second", "vvvvv", "vvv",
    )(ka, ra, kb, rb, sums)


def outer_kernel(keep_ref, arrived_ref, send_ref, own_ref):
    send_ref[...] = add_low(keep_ref[1], arrived_ref[1])
    own_ref[...] = keep_ref[0].astype(F32) + arrived_ref[0].astype(F32)


def fold_outer(keep, arrived):
    shape = keep.shape[1:]
    sds = jax.ShapeDtypeStruct
    return local_call(outer_kernel, [sds(shape, BF), sds(shape, F32)], "fold_outer", "vv", "vv")(keep, arrived)


def outer_pair_kernel(down_ref, ku_ref, ru_ref, send_ref, up_ref):
    size, width = ku_ref.shape[1], down_ref.shape[1]
    send_ref[0] = down_ref[...]
    for i in range(ku_ref.shape[2] // width):
        cols = slice(i * width, (i + 1) * width)
        send_ref[1, i * size : (i + 1) * size, :] = add_low(ku_ref[1, :, cols], ru_ref[1, :, cols])
    up_ref[...] = ku_ref[0].astype(F32) + ru_ref[0].astype(F32)


def fold_outer_pair(down, ku, ru):
    sds = jax.ShapeDtypeStruct
    shapes = [sds((2,) + down.shape, BF), sds(ku.shape[1:], F32)]
    return local_call(outer_pair_kernel, shapes, "fold_outer", "vvv", "vv")(down, ku, ru)


def last_pair_kernel(down_ref, up_ref, arrived_ref, down_out_ref, up_out_ref):
    size, width = up_ref.shape[0], down_ref.shape[1]
    down_out_ref[...] = down_ref[...] + arrived_ref[0].astype(F32)
    for i in range(up_ref.shape[1] // width):
        cols = slice(i * width, (i + 1) * width)
        up_out_ref[:, cols] = up_ref[:, cols] + arrived_ref[1, i * size : (i + 1) * size, :].astype(F32)


def last_pair(down, up, arrived):
    sds = jax.ShapeDtypeStruct
    return local_call(
        last_pair_kernel, [sds(down.shape, F32), sds(up.shape, F32)], "last_sum", "vvv", "ww"
    )(down, up, arrived)


def attn_outer_kernel(keep_ref, arrived_ref, old_ref, send_ref, own_ref, sums_ref):
    for i in range(2):
        send_ref[i] = add_low(keep_ref[2 + i], arrived_ref[2 + i])
        own_ref[i] = keep_ref[i].astype(F32) + arrived_ref[i].astype(F32)
    sums = decoded(coded(old_ref[...])) + decoded(arrived_ref[4])
    sums_ref[...] = sums
    send_ref[2] = coded(sums)


def attn_fold_outer(keep, arrived, sums):
    sds = jax.ShapeDtypeStruct
    tile = keep.shape[1:]
    return local_call(
        attn_outer_kernel, [sds((3,) + tile, BF), sds((2,) + tile, F32), sds(sums.shape, F32)], "fold_outer", "vvv", "vvv"
    )(keep, arrived, sums)


SUM_ROWS = 24


def unpack(sums, rows_ref, out_bias_ref, up_ref, qv_ref):
    whole = jnp.concatenate([sums[0:9], sums[9:18]], axis=1)
    width = whole.shape[1]
    rows_ref[...] = whole[0:5]
    out_bias_ref[...] = whole[5]
    up_ref[:width] = whole[6]
    up_ref[width:] = whole[7]
    qv_ref[0:1, :] = sums[8:9]
    qv_ref[1:2, :] = sums[17:18]


def attn_last_kernel(one_ref, arrived_ref, old_ref, two_ref, arrived2_ref, qkv_ref, out_ref, *sum_refs):
    _, size, cols = one_ref.shape
    qkv_ref[0] = one_ref[0] + arrived_ref[0].astype(F32)
    qkv_ref[2] = one_ref[1] + arrived_ref[1].astype(F32)
    total = two_ref[...] + arrived2_ref[...].astype(F32)
    qkv_ref[1] = total[:, :cols]
    out_ref[:, :cols] = total[: size // 2, cols:]
    out_ref[:, cols:] = total[size // 2 :, cols:]
    unpack(decoded(coded(old_ref[...])) + decoded(arrived_ref[2]), *sum_refs)


def attn_last(one, arrived, sums, two, arrived2):
    sds = jax.ShapeDtypeStruct
    _, size, cols = one.shape
    width = 2 * cols
    shapes = [
        sds((3, size, cols), F32), sds((size // 2, width), F32), sds((5, width), F32), sds((width,), F32),
        sds((2 * width,), F32), sds((2, cols), F32),
    ]
    return local_call(attn_last_kernel, shapes, "last_sum", "vvvvv", "w" * 6)(one, arrived, sums, two, arrived2)


def pack_kernel(mid_ref, mlp_ref, up_own_ref, up_oth_ref, qv_own_ref, qv_oth_ref, keep_ref, send_ref):
    cols = keep_ref.shape[1]
    row = lambda value: jnp.sum(value, axis=0, keepdims=True)
    for out_ref, up_ref, qv_ref in ((keep_ref, up_own_ref, qv_own_ref), (send_ref, up_oth_ref, qv_oth_ref)):
        rows = [row(mid_ref[0]), row(mid_ref[1])] + [row(mlp_ref[i]) for i in range(3)] + [row(mid_ref[2])]
        rows += [row(up_ref[:, i * 2 * cols : (i + 1) * 2 * cols]) for i in range(2)]
        rows.append(jnp.concatenate([row(qv_ref[0]), row(qv_ref[1])], axis=1))
        for i, value in enumerate(rows):
            out_ref[i : i + 1, :] = value[:, :cols]
            out_ref[9 + i : 10 + i, :] = value[:, cols:]
        out_ref[18:, :] = jnp.zeros((SUM_ROWS - 18, cols), F32)


def pack_sums(sums_mid, sums_mlp, up_own, up_oth, qv_own, qv_oth):
    shape = jax.ShapeDtypeStruct((SUM_ROWS, qv_own.shape[2]), F32)
    return local_call(pack_kernel, [shape] * 2, "pack_sums", "v" * 6, "vv")(sums_mid, sums_mlp, up_own, up_oth, qv_own, qv_oth)


def mid_kernel(
    pg_own_ref, pg_oth_ref, mgrad_ref, normed_ref, inv_ref, wu_own_ref, wu_oth_ref, wo_own_ref, wo_oth_ref, ga_ref,
    qkv_hbm, prob_hbm, migrad_hbm, agrad_ref, cg_own_ref, cg_oth_ref, sums_ref, qkv_ref, prob_ref, migrad_ref, sems,
):
    def product(first):
        rows = slice(first, first + BLOCK)
        return mm(pg_own_ref[rows, :], wu_own_ref[...], NT) + mm(pg_oth_ref[rows, :], wu_oth_ref[...], NT)

    sums = None
    count = mgrad_ref.shape[0]
    copies = Copies(sems)
    copies.start(qkv_hbm, qkv_ref)
    copies.start(prob_hbm, prob_ref)
    cols = cg_own_ref.shape[1]
    wo = jnp.concatenate([wo_own_ref[...], wo_oth_ref[...]], axis=0)
    ready = product(0)
    for first in range(0, count, BLOCK):
        back = ready
        if first + BLOCK < count:
            ready = product(first + BLOCK)
        for r in range(0, BLOCK, ROWS):
            part = slice(first + r, first + r + ROWS)
            e = back[r : r + ROWS] + mgrad_ref[part, :].astype(F32)
            normed = normed_ref[part, :].astype(F32)
            migrad = normalize_back(e * ga_ref[...], normed, inv_ref[part, :])
            migrad_ref[part, :] = migrad
            agrad = migrad.astype(BF)
            agrad_ref[part, :] = agrad
            new = [fold8(e * normed), fold8(e), fold8(agrad.astype(F32))]
            sums = new if sums is None else [x + y for x, y in zip(sums, new)]
        rows = slice(first, first + BLOCK)
        copies.start(migrad_ref.at[rows, :], migrad_hbm.at[rows, :])
        cgrad = mm(agrad_ref[rows, :], wo, NT).astype(BF)
        cg_own_ref[rows, :] = cgrad[:, :cols]
        cg_oth_ref[rows, :] = cgrad[:, cols:]
    sums_ref[...] = jnp.stack(sums)
    copies.wait_all()


def mid_grads(pg_own, pg_oth, mgrad, normed, inv, wu_own, wu_oth, wo_own, wo_oth, ga, qkv, probs):
    rows, width = mgrad.shape
    cols = wo_own.shape[0]
    sds = jax.ShapeDtypeStruct
    return local_call(
        mid_kernel,
        [
            sds((rows, width), F32), sds((rows, width), BF), sds((rows, cols), BF), sds((rows, cols), BF),
            sds((3, 8, width), F32), sds(qkv.shape, BF), sds(probs.shape, BF),
        ],
        "mid_grads", "vvvvvvvvvvhh", "hvvvvvv",
        [pltpu.VMEM((rows, width), F32)] + [pltpu.SemaphoreType.DMA((rows // BLOCK + 2,))], 20,
    )(pg_own, pg_oth, mgrad, normed, inv, wu_own, wu_oth, wo_own, wo_oth, ga, qkv, probs)


def attend_back_kernel(qkv_ref, prob_ref, cg_ref, *refs):
    if len(refs) > 2:
        next_qkv_hbm, next_prob_hbm, dqkv_ref, sums_ref, next_qkv_ref, next_prob_ref, sems = refs
        copies = Copies(sems)
        copies.start(next_qkv_hbm, next_qkv_ref)
        copies.start(next_prob_hbm, next_prob_ref)
    else:
        dqkv_ref, sums_ref = refs
    rows_all, cols = cg_ref.shape
    scale_a, scale_b = half_masks(LEN, HD**-0.5)
    one_a, one_b = half_masks(LEN)
    units = [(s, j) for s in range(rows_all // LEN) for j in range(cols // PAIR)]
    sums = {}

    def load(unit, i):
        s, j = unit
        return qkv_ref[s * LEN : (s + 1) * LEN, i * cols + j * PAIR : i * cols + (j + 1) * PAIR]

    def grad_probs(unit):
        s, j = unit
        v2 = load(unit, 2)
        g2 = cg_ref[s * LEN : (s + 1) * LEN, j * PAIR : (j + 1) * PAIR]
        return mm(g2, jnp.concatenate([v2 * one_a, v2 * one_b], axis=0), NT)

    def finish(unit, dprobs):
        s, j = unit
        rows = slice(s * LEN, (s + 1) * LEN)
        tall, flat = [], []
        for h in range(2):
            lanes = slice(h * LEN, (h + 1) * LEN)
            ds, low = [], []
            for r in range(0, LEN, SOFT):
                low.append(prob_ref[s, j, r : r + SOFT, lanes])
                p = low[-1].astype(F32)
                dp = dprobs[r : r + SOFT, lanes]
                ds.append((p * (dp - jnp.sum(p * dp, axis=1, keepdims=True))).astype(BF))
            flat.append(jnp.concatenate(ds, axis=0))
            tall.append(jnp.concatenate(low, axis=0))
        q2, k2 = load(unit, 0), load(unit, 1)
        g2 = cg_ref[rows, j * PAIR : (j + 1) * PAIR]
        qcat = jnp.concatenate([q2 * scale_a, q2 * scale_b], axis=0)
        kcat = jnp.concatenate([k2 * scale_a, k2 * scale_b], axis=0)
        gcat = jnp.concatenate([g2 * one_a, g2 * one_b], axis=0)
        dq = mm(jnp.concatenate(flat, axis=1), kcat).astype(BF)
        dk = mm(jnp.concatenate(flat, axis=0), qcat, TN).astype(BF)
        dv = mm(jnp.concatenate(tall, axis=0), gcat, TN).astype(BF)
        for i, value in enumerate((dq, dk, dv)):
            dqkv_ref[rows, i * cols + j * PAIR : i * cols + (j + 1) * PAIR] = value
        return fold8(dq.astype(F32)), fold8(dv.astype(F32))

    pending = [grad_probs(u) for u in units[:AHEAD]]
    for i, unit in enumerate(units):
        if i + AHEAD < len(units):
            pending.append(grad_probs(units[i + AHEAD]))
        new_q, new_v = finish(unit, pending.pop(0))
        j = unit[1]
        if j in sums:
            new_q, new_v = sums[j][0] + new_q, sums[j][1] + new_v
        sums[j] = (new_q, new_v)
    for j, (sum_q, sum_v) in sums.items():
        sums_ref[0, :, j * PAIR : (j + 1) * PAIR] = sum_q
        sums_ref[1, :, j * PAIR : (j + 1) * PAIR] = sum_v
    if len(refs) > 2:
        copies.wait_all()


def attend_back(qkv, probs, cgrad, *following):
    sds = jax.ShapeDtypeStruct
    shapes = [sds(qkv.shape, BF), sds((2, 8, cgrad.shape[1]), F32)] + [sds(a.shape, a.dtype) for a in following]
    return local_call(
        attend_back_kernel, shapes, "attend_back", "vvv" + "h" * len(following), "v" * len(shapes),
        [pltpu.SemaphoreType.DMA((2,))] if following else [], 12,
    )(qkv, probs, cgrad, *following)


def token_kernel(first, own_ref, oth_ref, migrad_hbm, w_own_ref, w_oth_ref, *refs):
    out_hbm, migrad_ref, out_ref, sems = refs[-4:]
    copies = Copies(sems)
    count = migrad_ref.shape[0]
    rows = slice(first, first + count)
    copies.start(migrad_hbm.at[rows, :], migrad_ref, "in")
    w = jnp.concatenate([side_by_side(w_own_ref), side_by_side(w_oth_ref)], axis=1)
    copies.wait("in")
    for r in range(0, count, 256):
        part = slice(first + r, first + r + 256)
        grads = jnp.concatenate([own_ref[part, :], oth_ref[part, :]], axis=1)
        out_ref[r : r + 256, :] = mm(grads, w, NT) + migrad_ref[r : r + 256, :]
        copies.start(out_ref.at[r : r + 256, :], out_hbm.at[part, :])
    copies.wait_all()


def token_grads(dqkv_own, dqkv_oth, migrad, w_own, w_oth, begun=None):
    rows, width = migrad.shape
    half = rows // 2
    extra = () if begun is None else (begun,)
    return local_call(
        functools.partial(token_kernel, half * len(extra)), [jax.ShapeDtypeStruct(migrad.shape, F32)], "token_grads",
        "vvhvv" + "h" * len(extra), "h",
        [pltpu.VMEM((half, width), F32)] * 2 + [pltpu.SemaphoreType.DMA((1 + half // 256,))], 16,
        aliases={5: 0} if extra else None,
    )(dqkv_own, dqkv_oth, migrad, w_own, w_oth, *extra)[0]


def per_device(
    tokens, timesteps, src_len, tgt_len, sample_weight, w_qkv, bias_qv, w_out, bias_out, gain_attn, shift_attn,
    w_up, bias_up, w_down, bias_down, gain_mlp, shift_mlp, cotangent,
):
    rows, width = tokens.shape
    dp = lax.axis_size("dp")
    mp_index = lax.axis_index("mp")
    cols = bias_qv.shape[1]
    ff = bias_up.shape[0]
    plane = 4

    def swap(value):
        return lax.ppermute(value, "mp", [(0, 1), (1, 0)])

    def after(value, *earlier):
        return lax.optimization_barrier((value, *earlier))[0]

    qkv_oth_w = swap(w_qkv)
    wo_oth = swap(w_out)
    wu_oth = swap(w_up)
    wd_oth = swap(w_down)
    biases = prepare(bias_qv, bias_up)
    biases_oth = swap(biases)

    qkv_own, prob_own, ctx_own, ctx_own_h, x_low, x_low_h, table = attend(
        src_len, tgt_len, (tokens, timesteps), w_qkv, biases
    )
    qkv_oth, prob_oth, ctx_oth, ctx_oth_h, wo_own = attend(src_len, tgt_len, (x_low,), qkv_oth_w, biases_oth, w_out)
    (normed, inv, mid_low, hid_own, hid_oth, dg_own, dg_oth, layer_out, mgrad, sums_mlp) = mlp(
        src_len, tgt_len, sample_weight, tokens, table, ctx_own, ctx_oth, cotangent, wo_own, wo_oth, bias_out,
        gain_attn, shift_attn, w_up, wu_oth, biases, biases_oth, w_down, wd_oth, bias_down, gain_mlp, shift_mlp,
    )
    split = dp == 16
    in_plane = [[base + k for k in range(plane)] for base in range(0, dp, plane)]
    across = [[base * plane + k for base in range(dp // plane)] for k in range(plane)]

    def hop(value, bits):
        return lax.ppermute(value, "dp", [(i, i ^ bits) for i in range(dp)])

    def along(sa, ka, sb, kb):
        return ka, hop(sa, 1), kb, hop(sb, 2)

    def across(sa, ta, sb, tb):
        return ta, hop(sa, 2), tb, hop(sb, 1)

    (down_send,) = weight_grad(hid_oth, mgrad, dp, plane)
    down_recv = swap(down_send)
    pg_own, pg_oth, sum_up_own, sum_up_oth = pre_grads(after(mgrad, down_send), w_down, wd_oth, dg_own, dg_oth)
    down = weight_grad(hid_own, after(mgrad, pg_own), dp, plane, down_recv, split)
    if split:
        down = along(*down)
    (up_send,) = weight_grad(after(mid_low, down[0]), pg_oth, dp, plane)
    up_recv = swap(up_send)
    migrad, agrad, cg_own, cg_oth, sums_mid, qkv_oth, prob_oth = mid_grads(
        pg_own, pg_oth, after(mgrad, up_send), normed, inv, w_up, wu_oth, wo_own, wo_oth, gain_attn, qkv_oth, prob_oth
    )
    up = weight_grad(after(mid_low, agrad), pg_own, dp, plane, up_recv, split)
    if split:
        up = along(*up)
        down = across(*fold_first(after(down[0], up[0]), *down[1:]))
    dqkv_oth, sum_qv_oth, qkv_own, prob_own = attend_back(
        qkv_oth, prob_oth, after(cg_oth, up[0], down[0]), qkv_own, prob_own
    )
    dqkv_own, sum_qv_own = attend_back(qkv_own, prob_own, cg_own)
    keep, send = pack_sums(sums_mid, sums_mlp, sum_up_own, sum_up_oth, sum_qv_own, sum_qv_oth)
    attn_args = (x_low_h, dqkv_oth, ctx_oth_h, after(agrad, keep), dp)
    (attn_send,) = attn_grad(*attn_args, send) if split else attn_grad(*attn_args)
    attn_recv = swap(attn_send)
    attn_args = (x_low_h, dqkv_own, ctx_own_h)
    if split:
        up = across(*fold_first(after(up[0], attn_send), *up[1:]))
        send, keep_down = fold_second(after(down[0], up[0]), *down[1:], plane)
        down = keep_down, hop(send, plane)
        *parts, sums = attn_grad(*attn_args, after(agrad, keep_down), dp, keep, attn_recv)
        one = along(*parts[:4])
        send, keep_up = fold_second(after(up[0], one[0]), *up[1:], plane)
        up = keep_up, hop(send, plane)
        send_down, own_down = fold_outer(after(down[0], keep_up), down[1])
        two = along(*parts[4:])
        token_args = dqkv_own, dqkv_oth, after(migrad, own_down), w_qkv, qkv_oth_w
        begun = token_grads(*token_args)
        *folded, sums = attn_fold_first(after(one[0], begun), *one[1:], sums)
        one = across(*folded)
        send, own_up = fold_outer_pair(after(send_down, one[0]), *up)
        arrived = hop(send, 2 * plane)
        tokens_grad = token_grads(*token_args[:3], w_qkv, qkv_oth_w, after(begun, own_up))
        two = across(*fold_first(after(two[0], tokens_grad), *two[1:]))
        send, keep_one, sums = attn_fold_second(after(one[0], two[0]), *one[1:], sums)
        one = keep_one, hop(send, plane)
        grad_w_down, grad_w_up = last_pair(after(own_down, keep_one), own_up, arrived)
        send, keep_two = fold_second(after(two[0], grad_w_up), *two[1:], plane, LATE_FLOPS)
        two = keep_two, hop(send, plane)
        send, own_one, sums = attn_fold_outer(after(one[0], keep_two), one[1], sums)
        one = own_one, hop(send, 2 * plane)
        send, own_two = fold_outer(after(two[0], own_one), two[1])
        two = own_two, hop(send, 2 * plane)
        grad_w_qkv, grad_w_out, grad_rows, grad_bias_out, grad_bias_up, grad_bias_qv = attn_last(*one, sums, *two)
    else:
        in_plane = [[base + k for k in range(plane)] for base in range(0, dp, plane)]
        outside = [[base * plane + k for base in range(dp // plane)] for k in range(plane)]

        def scatter(value):
            value = lax.psum_scatter(value, "dp", scatter_dimension=0, axis_index_groups=in_plane)
            return lax.psum_scatter(value, "dp", scatter_dimension=0, axis_index_groups=outside).astype(F32)

        (attn,) = attn_grad(*attn_args, agrad, dp, None, attn_recv)
        tokens_grad = token_grads(dqkv_own, dqkv_oth, after(migrad, attn), w_qkv, qkv_oth_w)
        grad_w_down, grad_w_up, attn = scatter(down[0]), scatter(up[0]), scatter(attn)
        half = attn.shape[1] // 2
        grad_w_qkv, grad_w_out = attn[:3], jnp.concatenate([attn[3, :half], attn[3, half:]], axis=1)
        sums = lax.psum(keep + swap(send), "dp")
        whole = jnp.concatenate([sums[0:9], sums[9:18]], axis=1)
        grad_rows, grad_bias_out, grad_bias_up = whole[0:5], whole[5], whole[6:8].reshape(-1)
        grad_bias_qv = jnp.stack([sums[8], sums[17]])
    return (
        layer_out, tokens_grad, grad_w_qkv, grad_w_out, grad_w_up, grad_w_down,
        grad_bias_qv, grad_bias_up, grad_bias_out, grad_rows,
    )


def solution(mesh):
    in_specs = (
        P(("dp", "mp"), None), P("dp"), P("dp"), P("dp"), P("dp"),
        P(None, None, "mp"), P(None, "mp"), P("mp", None), P(), P(), P(),
        P(None, "mp"), P("mp"), P("mp", None), P(), P(), P(), P(("dp", "mp"), None),
    )
    out_specs = (
        P(("dp", "mp"), None), P(("dp", "mp"), None), P(None, "dp", "mp"), P(("mp", "dp"), None),
        P("dp", "mp"), P(("mp", "dp"), None), P(None, "mp"), P("mp"), P(), P(),
    )
    return jax.shard_map(per_device, mesh=mesh, in_specs=in_specs, out_specs=out_specs, check_vma=False)
```

```python
import functools
import math

import jax
import jax.numpy as jnp
from jax import lax
from jax.experimental import pallas as pl
from jax.experimental.pallas import tpu as pltpu
from jax.sharding import PartitionSpec as P

HD = 64
LEN = 128
PAIR = 2 * HD
NORM_EPS = 1e-05
MASK_FILL = -1e30
BF = jnp.bfloat16
F32 = jnp.float32
MIB = 1 << 20
ROWS = 16
SOFT = 32
BLOCK = 512
MLP_BLOCK = 256
MLP_ROWS = 32
AHEAD = 2

NN = (((1,), (0,)), ((), ()))
NT = (((1,), (1,)), ((), ()))
TN = (((0,), (0,)), ((), ()))

SPECS = {
    "v": pl.BlockSpec(memory_space=pltpu.VMEM),
    "h": pl.BlockSpec(memory_space=pltpu.HBM),
    "w": pl.BlockSpec(memory_space=pltpu.VMEM),
}
AHEAD_FLOPS = 3 * 10**10
LATE_FLOPS = 10**9


def mm(a, b, dims=NN):
    return lax.dot_general(a, b, dims, preferred_element_type=F32)


def params(mib):
    return pltpu.CompilerParams(vmem_limit_bytes=mib * MIB)


def local_call(kernel, out_shape, name, ins, outs, scratch=(), mib=16, flops=0, aliases=None):
    forced = {"v": pltpu.VMEM, "h": pltpu.HBM, "w": pltpu.HBM}

    def call(*args):
        args = [pltpu.with_memory_space_constraint(a, pltpu.HBM) if c in "hw" else a for a, c in zip(args, ins)]
        return pl.pallas_call(
            kernel,
            in_specs=[SPECS[c] for c in ins],
            out_specs=[SPECS[c] for c in outs],
            out_shape=[forced[c](a.shape, a.dtype) for a, c in zip(out_shape, outs)],
            scratch_shapes=list(scratch),
            input_output_aliases=aliases or {},
            compiler_params=params(mib),
            cost_estimate=pl.CostEstimate(flops=flops, bytes_accessed=0, transcendentals=0) if flops else None,
            name=name,
        )(*args)

    return call


class Copies:
    def __init__(self, sems):
        self.sems = sems
        self.started = []
        self.waiting = {}

    def start(self, src, dst, key=None):
        copy = pltpu.make_async_copy(src, dst, self.sems.at[len(self.started)])
        copy.start()
        self.started.append(copy)
        self.waiting.setdefault(key, []).append(copy)

    def wait(self, key=None):
        for copy in self.waiting.pop(key, ()):
            copy.wait()

    def wait_all(self):
        for key in list(self.waiting):
            self.wait(key)


def prepare_kernel(bqv_ref, bu_ref, bias_ref):
    cols = bqv_ref.shape[1]
    up = bu_ref[...].astype(F32).reshape(1, -1)
    rows = [bqv_ref[...].astype(F32)]
    rows += [up[:, i * cols : (i + 1) * cols] for i in range(up.shape[1] // cols)]
    rows += [jnp.zeros((bias_ref.shape[0] - 1 - len(rows), cols), F32)]
    bias_ref[...] = jnp.concatenate(rows, axis=0).astype(BF)


def prepare(bias_qv, bias_up):
    cols = bias_qv.shape[1]
    rows = -(-(2 + bias_up.shape[0] // cols) // 8) * 8
    return local_call(prepare_kernel, [jax.ShapeDtypeStruct((rows, cols), BF)], "prepare", "ww", "v")(bias_qv, bias_up)[0]


def fill_table(table_ref, steps_ref, base):
    seqs, width = table_ref.shape
    half = width // 2
    lane = lax.broadcasted_iota(jnp.int32, (seqs, half), 1).astype(F32)
    frequency = jnp.exp(-math.log(10000.0) * lane / half)
    row = lax.broadcasted_iota(jnp.int32, (seqs, half), 0)
    angles = jnp.zeros((seqs, half), F32)
    for s in range(seqs):
        angles = jnp.where(row == s, steps_ref[base + s].astype(F32), angles)
    angles = angles * frequency
    table_ref[:, :half] = jnp.sin(angles)
    table_ref[:, half:] = jnp.cos(angles)


def half_masks(rows, value=1.0):
    lane = lax.broadcasted_iota(jnp.int32, (rows, PAIR), 1)
    first = jnp.where(lane < HD, value, 0.0).astype(BF)
    second = jnp.where(lane < HD, 0.0, value).astype(BF)
    return first, second


def fold8(value):
    rows, cols = value.shape
    return jnp.sum(value.reshape(rows // 8, 8, cols), axis=0)


def side_by_side(ref):
    return jnp.concatenate([ref[i] for i in range(ref.shape[0])], axis=1)


def attend_kernel(first, src_hbm, tgt_hbm, *refs):
    if first:
        (tok_hbm, steps_hbm, w_hbm, bias_ref, qkv_out, prob_out, ctx_ref, ctx_out, x_ref, x_out, table_ref,
         src_ref, tgt_ref, qkv_ref, prob_ref, sems, steps_ref, tok_ref, w_ref) = refs
    else:
        (x_ref, w_ref, bias_ref, next_hbm, qkv_out, prob_out, ctx_ref, ctx_out, next_ref,
         src_ref, tgt_ref, qkv_ref, prob_ref, sems) = refs
    copies = Copies(sems)
    copies.start(src_hbm, src_ref, "m")
    copies.start(tgt_hbm, tgt_ref, "m")
    seqs = x_ref.shape[0] // LEN
    cols = w_ref.shape[2]
    base = lax.axis_index("mp") * seqs
    if first:
        copies.start(steps_hbm, steps_ref, "t")
        blocks = [slice(start, start + BLOCK) for start in range(0, x_ref.shape[0], BLOCK)]
        copies.start(tok_hbm.at[blocks[0], :], tok_ref.at[blocks[0], :], 0)
        for i in range(3):
            copies.start(w_hbm.at[i], w_ref.at[i], "w")
        for rows in blocks[1:]:
            copies.start(tok_hbm.at[rows, :], tok_ref.at[rows, :], rows.start)
        copies.wait("t")
        fill_table(table_ref, steps_ref, base)
    else:
        copies.start(next_hbm, next_ref)
    bias_q = bias_ref[0:1, :].astype(F32)
    bias_v = bias_ref[1:2, :].astype(F32)
    scale_a, scale_b = half_masks(LEN, HD**-0.5)
    one_a, one_b = half_masks(LEN)
    key_pos = lax.broadcasted_iota(jnp.int32, (SOFT, LEN), 1)

    def project(start):
        if first:
            copies.wait(start)
            for s in range(start // LEN, (start + BLOCK) // LEN):
                row = table_ref[s : s + 1, :]
                for r in range(s * LEN, (s + 1) * LEN, ROWS):
                    x_ref[r : r + ROWS, :] = (tok_ref[r : r + ROWS, :].astype(F32) + row).astype(BF)
        rows = slice(start, start + BLOCK)
        full = mm(x_ref[rows, :], w)
        qkv_ref[rows, :cols] = (full[:, :cols] + bias_q).astype(BF)
        qkv_ref[rows, cols : 2 * cols] = full[:, cols : 2 * cols].astype(BF)
        qkv_ref[rows, 2 * cols :] = (full[:, 2 * cols :] + bias_v).astype(BF)
        copies.start(qkv_ref.at[rows, :], qkv_out.at[rows, :])
        if first:
            copies.start(x_ref.at[rows, :], x_out.at[rows, :])

    def score(unit):
        s, j = unit
        rows = slice(s * LEN, (s + 1) * LEN)
        q2 = qkv_ref[rows, j * PAIR : (j + 1) * PAIR]
        k2 = qkv_ref[rows, cols + j * PAIR : cols + (j + 1) * PAIR]
        return mm(q2, jnp.concatenate([k2 * scale_a, k2 * scale_b], axis=0), NT)

    def finish(unit, scores):
        s, j = unit
        rows = slice(s * LEN, (s + 1) * LEN)
        live = key_pos < src_ref[base + s] + tgt_ref[base + s]
        low = []
        for r in range(0, LEN, SOFT):
            halves = []
            for h in range(2):
                part = jnp.where(live, scores[r : r + SOFT, h * LEN : (h + 1) * LEN], MASK_FILL)
                e = jnp.exp(part - jnp.max(part, axis=1, keepdims=True))
                halves.append(e * (1.0 / jnp.sum(e, axis=1, keepdims=True)))
            low.append(jnp.concatenate(halves, axis=1).astype(BF))
            prob_ref[s, j, r : r + SOFT, :] = low[-1]
        v2 = qkv_ref[rows, 2 * cols + j * PAIR : 2 * cols + (j + 1) * PAIR]
        vcat = jnp.concatenate([v2 * one_a, v2 * one_b], axis=0)
        ctx_ref[rows, j * PAIR : (j + 1) * PAIR] = mm(jnp.concatenate(low, axis=0), vcat).astype(BF)

    count = x_ref.shape[0]
    if first:
        copies.wait(0)
        copies.wait("w")
    w = side_by_side(w_ref)
    project(0)
    copies.wait("m")
    for start in range(0, count, BLOCK):
        if start + BLOCK < count:
            project(start + BLOCK)
        units = [(s, j) for s in range(start // LEN, (start + BLOCK) // LEN) for j in range(cols // PAIR)]
        pending = [score(u) for u in units[:AHEAD]]
        for i, unit in enumerate(units):
            if i + AHEAD < len(units):
                pending.append(score(units[i + AHEAD]))
            finish(unit, pending.pop(0))
            if unit[1] == cols // PAIR - 1:
                copies.start(prob_ref.at[unit[0]], prob_out.at[unit[0]])
        rows = slice(start, start + BLOCK)
        copies.start(ctx_ref.at[rows, :], ctx_out.at[rows, :])
    copies.wait_all()


def attend(src, tgt, x_args, w_half, bias_half, following=None):
    first = len(x_args) == 2
    rows, width = x_args[0].shape
    cols = w_half.shape[2]
    sds = jax.ShapeDtypeStruct
    shapes = [
        sds((rows, 3 * cols), BF),
        sds((rows // LEN, cols // PAIR, LEN, 2 * LEN), BF),
        sds((rows, cols), BF),
        sds((rows, cols), BF),
        sds((rows, width), BF),
        sds((rows, width), BF),
        sds((rows // LEN, width), F32),
    ]
    if not first:
        shapes = shapes[:4] + [sds(following.shape, BF)]
    scratch = [
        pltpu.SMEM(src.shape, jnp.int32),
        pltpu.SMEM(tgt.shape, jnp.int32),
        pltpu.VMEM(shapes[0].shape, BF),
        pltpu.VMEM(shapes[1].shape, BF),
        pltpu.SemaphoreType.DMA((4 * rows // BLOCK + rows // LEN + 6,)),
    ]
    if first:
        scratch += [pltpu.SMEM(x_args[1].shape, jnp.int32), pltpu.VMEM((rows, width), BF), pltpu.VMEM(w_half.shape, BF)]
    return local_call(
        functools.partial(attend_kernel, first), shapes, "attend",
        "hhhhhv" if first else "hhvvvh", "hhvhvhv" if first else "hhvhv", scratch, 20,
    )(src, tgt, *x_args, w_half, bias_half, *(() if first else (following,)))


def normalize(value):
    centred = value - jnp.mean(value, axis=1, keepdims=True)
    inv_std = lax.rsqrt(jnp.mean(centred * centred, axis=1, keepdims=True) + NORM_EPS)
    return centred * inv_std, inv_std


def normalize_back(scaled, normed, inv_std):
    return inv_std * (
        scaled
        - jnp.mean(scaled, axis=1, keepdims=True)
        - normed * jnp.mean(scaled * normed, axis=1, keepdims=True)
    )


def gelu_pair(v):
    cdf = 0.5 + 0.5 * lax.erf(v * math.sqrt(0.5))
    return v * cdf, cdf + v * jnp.exp2(v * v * (-0.5 * math.log2(math.e))) * (1.0 / math.sqrt(2.0 * math.pi))


def mlp_kernel(
    src_hbm, tgt_hbm, weight_hbm, tok_ref, table_ref, ctx_own_ref, ctx_oth_ref, cot_hbm,
    wo_own_ref, wo_oth_ref, bo_ref, ga_ref, sa_ref,
    wu_own_ref, wu_oth_ref, bu_own_ref, bu_oth_ref, wd_own_ref, wd_oth_ref, bd_ref, gm_ref, sm_ref,
    normed_ref, inv_ref, mid_ref, hid_own_ref, hid_oth_ref, dg_own_ref, dg_oth_ref,
    out_hbm, mgrad_ref, sums_ref, normed_f32, out_ref, cot_ref, src_ref, tgt_ref, weight_ref, sems,
):
    count = tok_ref.shape[0]
    base = lax.axis_index("mp") * (count // LEN)
    copies = Copies(sems)
    for hbm, smem in ((src_hbm, src_ref), (tgt_hbm, tgt_ref), (weight_hbm, weight_ref)):
        copies.start(hbm, smem, 0)
    for start in range(0, count, MLP_BLOCK):
        copies.start(cot_hbm.at[start : start + MLP_BLOCK, :], cot_ref.at[start : start + MLP_BLOCK, :], start)
    wo = jnp.concatenate([wo_own_ref[...], wo_oth_ref[...]], axis=0)
    halves = (
        (wu_own_ref, bu_own_ref, wd_own_ref, hid_own_ref, dg_own_ref),
        (wu_oth_ref, bu_oth_ref, wd_oth_ref, hid_oth_ref, dg_oth_ref),
    )

    def first_norm(start):
        rows = slice(start, start + MLP_BLOCK)
        attn_out = mm(jnp.concatenate([ctx_own_ref[rows, :], ctx_oth_ref[rows, :]], axis=1), wo)
        for r in range(0, MLP_BLOCK, MLP_ROWS):
            part = slice(start + r, start + r + MLP_ROWS)
            table_row = table_ref[(start + r) // LEN : (start + r) // LEN + 1, :]
            start_x = tok_ref[part, :].astype(F32) + table_row
            normed, inv = normalize(start_x + attn_out[r : r + MLP_ROWS] + bo_ref[...])
            normed_f32[part, :] = normed
            normed_ref[part, :] = normed.astype(BF)
            inv_ref[part, :] = inv
            mid_x = normed * ga_ref[...] + sa_ref[...]
            mid_ref[part, :] = mid_x.astype(BF)

    def up(unit):
        start, half = unit
        return mm(mid_ref[start : start + MLP_BLOCK, :], halves[half][0][...])

    def activate(unit, pre):
        start, half = unit
        _, bu_ref, wd_ref, hid_ref, dg_ref = halves[half]
        bias = jnp.concatenate([bu_ref[i : i + 1, :] for i in range(2, 2 + wd_ref.shape[0] // bu_ref.shape[1])], axis=1).astype(F32)
        for r in range(0, MLP_BLOCK, MLP_ROWS):
            part = slice(start + r, start + r + MLP_ROWS)
            hidden, slope = gelu_pair(pre[r : r + MLP_ROWS] + bias)
            hid_ref[part, :] = hidden.astype(BF)
            dg_ref[part, :] = slope.astype(BF)
        return mm(hid_ref[start : start + MLP_BLOCK, :], wd_ref[...])

    pos = lax.broadcasted_iota(jnp.int32, (MLP_ROWS, 1), 0)

    def second_norm(start, mlp_out, sums):
        for r in range(0, MLP_BLOCK, MLP_ROWS):
            part = slice(start + r, start + r + MLP_ROWS)
            seq = base + (start + r) // LEN
            mid_x = normed_f32[part, :] * ga_ref[...] + sa_ref[...]
            normed2, inv2 = normalize(mid_x + (mlp_out[r : r + MLP_ROWS] + bd_ref[...]))
            out_ref[part, :] = normed2 * gm_ref[...] + sm_ref[...]
            here = pos + (start + r) % LEN
            inside = (here >= src_ref[seq]) & (here < src_ref[seq] + tgt_ref[seq])
            e = cot_ref[part, :].astype(F32) * jnp.where(inside, weight_ref[seq], 0.0)
            mgrad = normalize_back(e * gm_ref[...], normed2, inv2).astype(BF)
            mgrad_ref[part, :] = mgrad
            new = [fold8(mgrad.astype(F32)), fold8(e * normed2), fold8(e)]
            sums = new if sums is None else [x + y for x, y in zip(sums, new)]
        return sums

    sums = None
    first_norm(0)
    for start in range(0, count, MLP_BLOCK):
        copies.wait(start)
    units = [(start, half) for start in range(0, count, MLP_BLOCK) for half in range(2)]
    ready = up(units[0])
    waiting = None
    total = None
    for i, unit in enumerate(units):
        start, half = unit
        pre = ready
        if half == 0 and start + MLP_BLOCK < count:
            first_norm(start + MLP_BLOCK)
        if i + 1 < len(units):
            ready = up(units[i + 1])
        down = activate(unit, pre)
        if half == 0:
            if waiting is not None:
                sums = second_norm(*waiting, sums)
            total = down
        else:
            waiting = (start, total + down)
    done = slice(0, count - MLP_BLOCK)
    copies.start(out_ref.at[done, :], out_hbm.at[done, :])
    sums = second_norm(*waiting, sums)
    sums_ref[...] = jnp.stack(sums)
    done = slice(count - MLP_BLOCK, count)
    copies.start(out_ref.at[done, :], out_hbm.at[done, :])
    copies.wait_all()


def mlp(src, tgt, weight, tokens, table, ctx_own, ctx_oth, cot, wo_own, wo_oth, bo, ga, sa,
        wu_own, wu_oth, bu_own, bu_oth, wd_own, wd_oth, bd, gm, sm):
    rows, width = tokens.shape
    ff = wu_own.shape[1]
    sds = jax.ShapeDtypeStruct
    args = (src, tgt, weight, tokens, table, ctx_own, ctx_oth, cot, wo_own, wo_oth, bo, ga, sa,
            wu_own, wu_oth, bu_own, bu_oth, wd_own, wd_oth, bd, gm, sm)
    return local_call(
        mlp_kernel,
        [
            sds((rows, width), BF), sds((rows, 1), F32), sds((rows, width), BF),
            sds((rows, ff), BF), sds((rows, ff), BF), sds((rows, ff), BF), sds((rows, ff), BF),
            sds((rows, width), F32), sds((rows, width), BF), sds((3, 8, width), F32),
        ],
        "mlp",
        "hhhvvvvh" + "v" * 14,
        "vvvvvvvhvv",
        [pltpu.VMEM((rows, width), F32)] * 2 + [
            pltpu.VMEM((rows, width), BF), pltpu.SMEM(src.shape, jnp.int32), pltpu.SMEM(tgt.shape, jnp.int32),
            pltpu.SMEM(weight.shape, F32), pltpu.SemaphoreType.DMA((4 * rows // MLP_BLOCK + 3,)),
        ],
        20,
    )(*args)


def pre_kernel(mgrad_ref, wd_own_ref, wd_oth_ref, dg_own_ref, dg_oth_ref, pg_own_ref, pg_oth_ref, sum_own_ref, sum_oth_ref):
    halves = ((wd_oth_ref, dg_oth_ref, pg_oth_ref, sum_oth_ref), (wd_own_ref, dg_own_ref, pg_own_ref, sum_own_ref))
    units = [(h, c) for h in halves for c in range(0, wd_own_ref.shape[0], 512)]

    def product(unit):
        (wd_ref, _, _, _), c = unit
        return mm(mgrad_ref[...], wd_ref[c : c + 512, :], NT)

    ready = product(units[0])
    for i, ((_, dg_ref, pg_ref, sum_ref), c) in enumerate(units):
        full = ready
        if i + 1 < len(units):
            ready = product(units[i + 1])
        sums = None
        for r in range(0, full.shape[0], 32):
            pg = (full[r : r + 32] * dg_ref[r : r + 32, c : c + 512].astype(F32)).astype(BF)
            pg_ref[r : r + 32, c : c + 512] = pg
            new = fold8(pg.astype(F32))
            sums = new if sums is None else sums + new
        sum_ref[:, c : c + 512] = sums


def pre_grads(mgrad, wd_own, wd_oth, dg_own, dg_oth):
    rows = mgrad.shape[0]
    ff = wd_own.shape[0]
    sds = jax.ShapeDtypeStruct
    return local_call(
        pre_kernel,
        [sds((rows, ff), BF), sds((rows, ff), BF), sds((8, ff), F32), sds((8, ff), F32)],
        "pre_grads", "vvvvv", "vvvv", mib=12,
    )(mgrad, wd_own, wd_oth, dg_own, dg_oth)


def weight_pieces(lhs_ref, rhs_ref, size, chunk=384):
    m = lhs_ref.shape[1]
    ready = mm(lhs_ref[:, :chunk], rhs_ref[...], TN)
    for start in range(0, m, chunk):
        full = ready
        if start + chunk < m:
            ready = mm(lhs_ref[:, start + chunk : start + 2 * chunk], rhs_ref[...], TN)
        for first in range(0, chunk, size):
            yield (start + first) // size, full[first : first + size]


def attn_pieces(x_ref, dqkv_ref, ctx_ref, agrad_ref, size):
    cols = ctx_ref.shape[1]
    half = size // 2
    out_full = mm(ctx_ref[...], agrad_ref[...], TN)
    for index, qkv in weight_pieces(x_ref, dqkv_ref, size):
        rows = out_full[index * half : (index + 1) * half]
        blocks = [(0, qkv[:, i * cols : (i + 1) * cols], i) for i in range(3)]
        yield index, blocks + [(c * half, rows[:, c * cols : (c + 1) * cols], 3) for c in range(2)]


def coded(sums):
    high = sums.astype(BF).astype(F32)
    return jnp.concatenate([high, sums - high], axis=0).astype(BF)


def decoded(block):
    value = block.astype(F32)
    half = value.shape[0] // 2
    return value[:half] + value[half:]


def send_kernel(lhs_ref, rhs_ref, out_ref):
    plane, _, size, _ = out_ref.shape
    for index, value in weight_pieces(lhs_ref, rhs_ref, size):
        out_ref[index % plane, index // plane] = value.astype(BF)


def total_kernel(lhs_ref, rhs_ref, recv_ref, out_ref):
    plane, _, size, _ = out_ref.shape
    for index, value in weight_pieces(lhs_ref, rhs_ref, size):
        k, g = index % plane, index // plane
        out_ref[k, g] = (value + recv_ref[k, g].astype(F32)).astype(BF)


def split_kernel(lhs_ref, rhs_ref, recv_ref, sa_ref, ka_ref, sb_ref, kb_ref, held_ref):
    plane, size = held_ref.shape[1], held_ref.shape[2]
    me = lax.axis_index("dp") % plane
    for index, value in weight_pieces(lhs_ref, rhs_ref, size):
        k, g = index % plane, index // plane
        slot = g % held_ref.shape[0]
        held_ref[slot, k] = value + recv_ref[k, g].astype(F32)
        if k == plane - 1:
            for far in range(plane):
                y, x = divmod(far, 2)
                piece = held_ref[slot, me ^ far].astype(BF)
                half = piece.shape[1] // 2
                (sa_ref if x else ka_ref)[y, g] = piece[:, :half]
                (sb_ref if y else kb_ref)[x, g] = piece[:, half:]


def weight_grad(lhs, rhs, dp, plane, recv=None, split=False):
    size, n = lhs.shape[1] // dp, rhs.shape[1]
    outer = dp // plane
    sds = jax.ShapeDtypeStruct
    scratch = ()
    if recv is None:
        kernel, shapes, args = send_kernel, [sds((plane, outer, size, n), BF)], (lhs, rhs)
    elif split:
        kernel, shapes, args = split_kernel, [sds((2, outer, size, n // 2), BF)] * 4, (lhs, rhs, recv)
        scratch = [pltpu.VMEM((2, plane, size, n), F32)]
    else:
        kernel, shapes, args = total_kernel, [sds((plane, outer, size, n), BF)], (lhs, rhs, recv)
    return local_call(kernel, shapes, "wgrad", "v" * len(args), "v" * len(shapes), scratch, 12)(*args)


def attn_send_kernel(x_ref, dqkv_ref, ctx_ref, agrad_ref, *refs):
    *sums_refs, out_ref = refs
    _, size, cols = out_ref.shape
    outer = out_ref.shape[0] // 16
    for index, blocks in attn_pieces(x_ref, dqkv_ref, ctx_ref, agrad_ref, size):
        k, g = index % 4, index // 4
        for first, value, i in blocks:
            out_ref[(k * outer + g) * 4 + i, first : first + value.shape[0], :] = value.astype(BF)
    for sums_ref in sums_refs:
        out_ref[16 * outer] = coded(sums_ref[...])


def attn_hold(recv_ref, index, blocks, held_ref, slot, outer):
    k, g = index % 4, index // 4
    for first, value, i in blocks:
        held_ref[slot, k, i, first : first + value.shape[0], :] = value
    for i in range(4):
        arrived = recv_ref[(k * outer + g) * 4 + i]
        held_ref[slot, k, i] = held_ref[slot, k, i] + arrived.astype(F32)
    return k, g


def attn_total_kernel(x_ref, dqkv_ref, ctx_ref, agrad_ref, recv_ref, out_ref, held_ref):
    plane, outer, _, size, _ = out_ref.shape
    for index, blocks in attn_pieces(x_ref, dqkv_ref, ctx_ref, agrad_ref, size):
        slot = (index // plane) % 2
        k, g = attn_hold(recv_ref, index, blocks, held_ref, slot, outer)
        out_ref[k, g] = held_ref[slot, k].astype(BF)


def attn_split_kernel(
    x_ref, dqkv_ref, ctx_ref, agrad_ref, keep_ref, recv_ref,
    sa_ref, ka_ref, sb_ref, kb_ref, sa2_ref, ka2_ref, sb2_ref, kb2_ref, sums_ref, held_ref,
):
    plane = held_ref.shape[1]
    outer = kb_ref.shape[0] // 2
    me = lax.axis_index("dp") % plane
    sums = decoded(coded(keep_ref[...])) + decoded(recv_ref[16 * outer])
    sums_ref[...] = sums
    sa_ref[2 * outer] = coded(sums)
    for index, blocks in attn_pieces(x_ref, dqkv_ref, ctx_ref, agrad_ref, held_ref.shape[3]):
        slot = (index // plane) % 2
        k, g = attn_hold(recv_ref, index, blocks, held_ref, slot, outer)
        if k == plane - 1:
            for far in range(plane):
                y, x = divmod(far, 2)
                piece = held_ref[slot, me ^ far].astype(BF)
                (sa_ref if x else ka_ref)[y * outer + g] = piece[0]
                (sb_ref if y else kb_ref)[x * outer + g] = piece[2]
                (sa2_ref if x else ka2_ref)[y, g] = piece[1]
                (sb2_ref if y else kb2_ref)[x, g] = piece[3]


def attn_grad(x_low, dqkv, ctx, agrad, dp, sums=None, recv=None):
    size, cols = x_low.shape[1] // dp, ctx.shape[1]
    outer = dp // 4
    sds = jax.ShapeDtypeStruct
    block = lambda n: sds((n, size, cols), BF)
    args = (x_low, dqkv, ctx, agrad) + (() if sums is None else (sums,))
    scratch = ()
    if recv is None:
        kernel, shapes = attn_send_kernel, [block(16 * outer + (sums is not None))]
    else:
        args += (recv,)
        scratch = [pltpu.VMEM((2, 4, 4, size, cols), F32)]
        if sums is None:
            kernel, shapes = attn_total_kernel, [sds((4, outer, 4, size, cols), BF)]
        else:
            kernel = attn_split_kernel
            shapes = [block(2 * outer + 1)] + [block(2 * outer)] * 3
            shapes += [sds((2, outer, size, cols), BF)] * 4 + [sds(sums.shape, F32)]
    return local_call(kernel, shapes, "attn_wgrad", "v" * len(args), "v" * len(shapes), scratch, 16)(*args)


def add_low(one, two):
    return (one.astype(F32) + two.astype(F32)).astype(BF)


def fold_kernel(ka_ref, ra_ref, kb_ref, rb_ref, sa_ref, ta_ref, sb_ref, tb_ref):
    for k_ref, r_ref, s_ref, t_ref in ((ka_ref, ra_ref, sa_ref, ta_ref), (kb_ref, rb_ref, sb_ref, tb_ref)):
        for g in range(k_ref.shape[1]):
            s_ref[g] = add_low(k_ref[1, g], r_ref[1, g])
            t_ref[g] = add_low(k_ref[0, g], r_ref[0, g])


def fold_first(ka, ra, kb, rb):
    shape = jax.ShapeDtypeStruct(ka.shape[1:], BF)
    return local_call(fold_kernel, [shape] * 4, "fold_first", "vvvv", "vvvv")(ka, ra, kb, rb)


def attn_fold_kernel(ka_ref, ra_ref, kb_ref, rb_ref, old_ref, sa_ref, ta_ref, sb_ref, tb_ref, sums_ref):
    count = ta_ref.shape[0]
    for k_ref, r_ref, s_ref, t_ref in ((ka_ref, ra_ref, sa_ref, ta_ref), (kb_ref, rb_ref, sb_ref, tb_ref)):
        for g in range(count):
            s_ref[g] = add_low(k_ref[count + g], r_ref[count + g])
            t_ref[g] = add_low(k_ref[g], r_ref[g])
    sums = decoded(coded(old_ref[...])) + decoded(ra_ref[2 * count])
    sums_ref[...] = sums
    sa_ref[count] = coded(sums)


def attn_fold_first(ka, ra, kb, rb, sums):
    sds = jax.ShapeDtypeStruct
    count = ka.shape[0] // 2
    block = lambda n: sds((n,) + ka.shape[1:], BF)
    return local_call(
        attn_fold_kernel, [block(count + 1)] + [block(count)] * 3 + [sds(sums.shape, F32)], "fold_first", "vvvvv", "vvvvv"
    )(ka, ra, kb, rb, sums)


def plane_kernel(plane, ka_ref, ra_ref, kb_ref, rb_ref, send_ref, keep_ref):
    me = lax.axis_index("dp") // plane
    for far in range(ka_ref.shape[0]):
        g = me ^ far
        out_ref = send_ref if far % 2 else keep_ref
        half = ka_ref.shape[2]
        out_ref[far // 2, :, :half] = add_low(ka_ref[g], ra_ref[g])
        out_ref[far // 2, :, half:] = add_low(kb_ref[g], rb_ref[g])


def fold_second(ka, ra, kb, rb, plane, flops=AHEAD_FLOPS):
    outer, size, n = ka.shape
    return local_call(
        functools.partial(plane_kernel, plane), [jax.ShapeDtypeStruct((outer // 2, size, 2 * n), BF)] * 2,
        "fold_second", "vvvv", "vv", flops=flops,
    )(ka, ra, kb, rb)


def attn_plane_kernel(ka_ref, ra_ref, kb_ref, rb_ref, old_ref, send_ref, keep_ref, sums_ref):
    me = lax.axis_index("dp") // 4
    outer = ka_ref.shape[0]
    for far in range(outer):
        g = me ^ far
        out_ref = send_ref if far % 2 else keep_ref
        first = (far // 2) * 2
        out_ref[first] = add_low(ka_ref[g], ra_ref[g])
        out_ref[first + 1] = add_low(kb_ref[g], rb_ref[g])
    sums = decoded(coded(old_ref[...])) + decoded(ra_ref[outer])
    sums_ref[...] = sums
    send_ref[outer] = coded(sums)


def attn_fold_second(ka, ra, kb, rb, sums):
    sds = jax.ShapeDtypeStruct
    outer = ka.shape[0]
    block = lambda n: sds((n,) + ka.shape[1:], BF)
    return local_call(
        attn_plane_kernel, [block(outer + 1), block(outer), sds(sums.shape, F32)], "fold_second", "vvvvv", "vvv",
    )(ka, ra, kb, rb, sums)


def outer_kernel(keep_ref, arrived_ref, send_ref, own_ref):
    send_ref[...] = add_low(keep_ref[1], arrived_ref[1])
    own_ref[...] = keep_ref[0].astype(F32) + arrived_ref[0].astype(F32)


def fold_outer(keep, arrived):
    shape = keep.shape[1:]
    sds = jax.ShapeDtypeStruct
    return local_call(outer_kernel, [sds(shape, BF), sds(shape, F32)], "fold_outer", "vv", "vv")(keep, arrived)


def outer_pair_kernel(down_ref, ku_ref, ru_ref, send_ref, up_ref):
    size, width = ku_ref.shape[1], down_ref.shape[1]
    send_ref[0] = down_ref[...]
    for i in range(ku_ref.shape[2] // width):
        cols = slice(i * width, (i + 1) * width)
        send_ref[1, i * size : (i + 1) * size, :] = add_low(ku_ref[1, :, cols], ru_ref[1, :, cols])
    up_ref[...] = ku_ref[0].astype(F32) + ru_ref[0].astype(F32)


def fold_outer_pair(down, ku, ru):
    sds = jax.ShapeDtypeStruct
    shapes = [sds((2,) + down.shape, BF), sds(ku.shape[1:], F32)]
    return local_call(outer_pair_kernel, shapes, "fold_outer", "vvv", "vv")(down, ku, ru)


def last_pair_kernel(down_ref, up_ref, arrived_ref, down_out_ref, up_out_ref):
    size, width = up_ref.shape[0], down_ref.shape[1]
    down_out_ref[...] = down_ref[...] + arrived_ref[0].astype(F32)
    for i in range(up_ref.shape[1] // width):
        cols = slice(i * width, (i + 1) * width)
        up_out_ref[:, cols] = up_ref[:, cols] + arrived_ref[1, i * size : (i + 1) * size, :].astype(F32)


def last_pair(down, up, arrived):
    sds = jax.ShapeDtypeStruct
    return local_call(
        last_pair_kernel, [sds(down.shape, F32), sds(up.shape, F32)], "last_sum", "vvv", "ww"
    )(down, up, arrived)


def attn_outer_kernel(keep_ref, arrived_ref, old_ref, send_ref, own_ref, sums_ref):
    for i in range(2):
        send_ref[i] = add_low(keep_ref[2 + i], arrived_ref[2 + i])
        own_ref[i] = keep_ref[i].astype(F32) + arrived_ref[i].astype(F32)
    sums = decoded(coded(old_ref[...])) + decoded(arrived_ref[4])
    sums_ref[...] = sums
    send_ref[2] = coded(sums)


def attn_fold_outer(keep, arrived, sums):
    sds = jax.ShapeDtypeStruct
    tile = keep.shape[1:]
    return local_call(
        attn_outer_kernel, [sds((3,) + tile, BF), sds((2,) + tile, F32), sds(sums.shape, F32)], "fold_outer", "vvv", "vvv"
    )(keep, arrived, sums)


SUM_ROWS = 24


def unpack(sums, rows_ref, out_bias_ref, up_ref, qv_ref):
    whole = jnp.concatenate([sums[0:9], sums[9:18]], axis=1)
    width = whole.shape[1]
    rows_ref[...] = whole[0:5]
    out_bias_ref[...] = whole[5]
    up_ref[:width] = whole[6]
    up_ref[width:] = whole[7]
    qv_ref[0:1, :] = sums[8:9]
    qv_ref[1:2, :] = sums[17:18]


def attn_last_kernel(one_ref, arrived_ref, old_ref, two_ref, arrived2_ref, qkv_ref, out_ref, *sum_refs):
    _, size, cols = one_ref.shape
    qkv_ref[0] = one_ref[0] + arrived_ref[0].astype(F32)
    qkv_ref[2] = one_ref[1] + arrived_ref[1].astype(F32)
    total = two_ref[...] + arrived2_ref[...].astype(F32)
    qkv_ref[1] = total[:, :cols]
    out_ref[:, :cols] = total[: size // 2, cols:]
    out_ref[:, cols:] = total[size // 2 :, cols:]
    unpack(decoded(coded(old_ref[...])) + decoded(arrived_ref[2]), *sum_refs)


def attn_last(one, arrived, sums, two, arrived2):
    sds = jax.ShapeDtypeStruct
    _, size, cols = one.shape
    width = 2 * cols
    shapes = [
        sds((3, size, cols), F32), sds((size // 2, width), F32), sds((5, width), F32), sds((width,), F32),
        sds((2 * width,), F32), sds((2, cols), F32),
    ]
    return local_call(attn_last_kernel, shapes, "last_sum", "vvvvv", "w" * 6)(one, arrived, sums, two, arrived2)


def pack_kernel(mid_ref, mlp_ref, up_own_ref, up_oth_ref, qv_own_ref, qv_oth_ref, keep_ref, send_ref):
    cols = keep_ref.shape[1]
    row = lambda value: jnp.sum(value, axis=0, keepdims=True)
    for out_ref, up_ref, qv_ref in ((keep_ref, up_own_ref, qv_own_ref), (send_ref, up_oth_ref, qv_oth_ref)):
        rows = [row(mid_ref[0]), row(mid_ref[1])] + [row(mlp_ref[i]) for i in range(3)] + [row(mid_ref[2])]
        rows += [row(up_ref[:, i * 2 * cols : (i + 1) * 2 * cols]) for i in range(2)]
        rows.append(jnp.concatenate([row(qv_ref[0]), row(qv_ref[1])], axis=1))
        for i, value in enumerate(rows):
            out_ref[i : i + 1, :] = value[:, :cols]
            out_ref[9 + i : 10 + i, :] = value[:, cols:]
        out_ref[18:, :] = jnp.zeros((SUM_ROWS - 18, cols), F32)


def pack_sums(sums_mid, sums_mlp, up_own, up_oth, qv_own, qv_oth):
    shape = jax.ShapeDtypeStruct((SUM_ROWS, qv_own.shape[2]), F32)
    return local_call(pack_kernel, [shape] * 2, "pack_sums", "v" * 6, "vv")(sums_mid, sums_mlp, up_own, up_oth, qv_own, qv_oth)


def mid_kernel(
    pg_own_ref, pg_oth_ref, mgrad_ref, normed_ref, inv_ref, wu_own_ref, wu_oth_ref, wo_own_ref, wo_oth_ref, ga_ref,
    qkv_hbm, prob_hbm, migrad_hbm, agrad_ref, cg_own_ref, cg_oth_ref, sums_ref, qkv_ref, prob_ref, migrad_ref, sems,
):
    def product(first):
        rows = slice(first, first + BLOCK)
        return mm(pg_own_ref[rows, :], wu_own_ref[...], NT) + mm(pg_oth_ref[rows, :], wu_oth_ref[...], NT)

    sums = None
    count = mgrad_ref.shape[0]
    copies = Copies(sems)
    copies.start(qkv_hbm, qkv_ref)
    copies.start(prob_hbm, prob_ref)
    cols = cg_own_ref.shape[1]
    wo = jnp.concatenate([wo_own_ref[...], wo_oth_ref[...]], axis=0)
    ready = product(0)
    for first in range(0, count, BLOCK):
        back = ready
        if first + BLOCK < count:
            ready = product(first + BLOCK)
        for r in range(0, BLOCK, ROWS):
            part = slice(first + r, first + r + ROWS)
            e = back[r : r + ROWS] + mgrad_ref[part, :].astype(F32)
            normed = normed_ref[part, :].astype(F32)
            migrad = normalize_back(e * ga_ref[...], normed, inv_ref[part, :])
            migrad_ref[part, :] = migrad
            agrad = migrad.astype(BF)
            agrad_ref[part, :] = agrad
            new = [fold8(e * normed), fold8(e), fold8(agrad.astype(F32))]
            sums = new if sums is None else [x + y for x, y in zip(sums, new)]
        rows = slice(first, first + BLOCK)
        copies.start(migrad_ref.at[rows, :], migrad_hbm.at[rows, :])
        cgrad = mm(agrad_ref[rows, :], wo, NT).astype(BF)
        cg_own_ref[rows, :] = cgrad[:, :cols]
        cg_oth_ref[rows, :] = cgrad[:, cols:]
    sums_ref[...] = jnp.stack(sums)
    copies.wait_all()


def mid_grads(pg_own, pg_oth, mgrad, normed, inv, wu_own, wu_oth, wo_own, wo_oth, ga, qkv, probs):
    rows, width = mgrad.shape
    cols = wo_own.shape[0]
    sds = jax.ShapeDtypeStruct
    return local_call(
        mid_kernel,
        [
            sds((rows, width), F32), sds((rows, width), BF), sds((rows, cols), BF), sds((rows, cols), BF),
            sds((3, 8, width), F32), sds(qkv.shape, BF), sds(probs.shape, BF),
        ],
        "mid_grads", "vvvvvvvvvvhh", "hvvvvvv",
        [pltpu.VMEM((rows, width), F32)] + [pltpu.SemaphoreType.DMA((rows // BLOCK + 2,))], 20,
    )(pg_own, pg_oth, mgrad, normed, inv, wu_own, wu_oth, wo_own, wo_oth, ga, qkv, probs)


def attend_back_kernel(qkv_ref, prob_ref, cg_ref, *refs):
    if len(refs) > 2:
        next_qkv_hbm, next_prob_hbm, dqkv_ref, sums_ref, next_qkv_ref, next_prob_ref, sems = refs
        copies = Copies(sems)
        copies.start(next_qkv_hbm, next_qkv_ref)
        copies.start(next_prob_hbm, next_prob_ref)
    else:
        dqkv_ref, sums_ref = refs
    rows_all, cols = cg_ref.shape
    scale_a, scale_b = half_masks(LEN, HD**-0.5)
    one_a, one_b = half_masks(LEN)
    units = [(s, j) for s in range(rows_all // LEN) for j in range(cols // PAIR)]
    sums = {}

    def load(unit, i):
        s, j = unit
        return qkv_ref[s * LEN : (s + 1) * LEN, i * cols + j * PAIR : i * cols + (j + 1) * PAIR]

    def grad_probs(unit):
        s, j = unit
        v2 = load(unit, 2)
        g2 = cg_ref[s * LEN : (s + 1) * LEN, j * PAIR : (j + 1) * PAIR]
        return mm(g2, jnp.concatenate([v2 * one_a, v2 * one_b], axis=0), NT)

    def finish(unit, dprobs):
        s, j = unit
        rows = slice(s * LEN, (s + 1) * LEN)
        tall, flat = [], []
        for h in range(2):
            lanes = slice(h * LEN, (h + 1) * LEN)
            ds, low = [], []
            for r in range(0, LEN, SOFT):
                low.append(prob_ref[s, j, r : r + SOFT, lanes])
                p = low[-1].astype(F32)
                dp = dprobs[r : r + SOFT, lanes]
                ds.append((p * (dp - jnp.sum(p * dp, axis=1, keepdims=True))).astype(BF))
            flat.append(jnp.concatenate(ds, axis=0))
            tall.append(jnp.concatenate(low, axis=0))
        q2, k2 = load(unit, 0), load(unit, 1)
        g2 = cg_ref[rows, j * PAIR : (j + 1) * PAIR]
        qcat = jnp.concatenate([q2 * scale_a, q2 * scale_b], axis=0)
        kcat = jnp.concatenate([k2 * scale_a, k2 * scale_b], axis=0)
        gcat = jnp.concatenate([g2 * one_a, g2 * one_b], axis=0)
        dq = mm(jnp.concatenate(flat, axis=1), kcat).astype(BF)
        dk = mm(jnp.concatenate(flat, axis=0), qcat, TN).astype(BF)
        dv = mm(jnp.concatenate(tall, axis=0), gcat, TN).astype(BF)
        for i, value in enumerate((dq, dk, dv)):
            dqkv_ref[rows, i * cols + j * PAIR : i * cols + (j + 1) * PAIR] = value
        return fold8(dq.astype(F32)), fold8(dv.astype(F32))

    pending = [grad_probs(u) for u in units[:AHEAD]]
    for i, unit in enumerate(units):
        if i + AHEAD < len(units):
            pending.append(grad_probs(units[i + AHEAD]))
        new_q, new_v = finish(unit, pending.pop(0))
        j = unit[1]
        if j in sums:
            new_q, new_v = sums[j][0] + new_q, sums[j][1] + new_v
        sums[j] = (new_q, new_v)
    for j, (sum_q, sum_v) in sums.items():
        sums_ref[0, :, j * PAIR : (j + 1) * PAIR] = sum_q
        sums_ref[1, :, j * PAIR : (j + 1) * PAIR] = sum_v
    if len(refs) > 2:
        copies.wait_all()


def attend_back(qkv, probs, cgrad, *following):
    sds = jax.ShapeDtypeStruct
    shapes = [sds(qkv.shape, BF), sds((2, 8, cgrad.shape[1]), F32)] + [sds(a.shape, a.dtype) for a in following]
    return local_call(
        attend_back_kernel, shapes, "attend_back", "vvv" + "h" * len(following), "v" * len(shapes),
        [pltpu.SemaphoreType.DMA((2,))] if following else [], 12,
    )(qkv, probs, cgrad, *following)


def token_kernel(first, own_ref, oth_ref, migrad_hbm, w_own_ref, w_oth_ref, *refs):
    out_hbm, migrad_ref, out_ref, sems = refs[-4:]
    copies = Copies(sems)
    count = migrad_ref.shape[0]
    rows = slice(first, first + count)
    copies.start(migrad_hbm.at[rows, :], migrad_ref, "in")
    w = jnp.concatenate([side_by_side(w_own_ref), side_by_side(w_oth_ref)], axis=1)
    copies.wait("in")
    for r in range(0, count, 256):
        part = slice(first + r, first + r + 256)
        grads = jnp.concatenate([own_ref[part, :], oth_ref[part, :]], axis=1)
        out_ref[r : r + 256, :] = mm(grads, w, NT) + migrad_ref[r : r + 256, :]
        copies.start(out_ref.at[r : r + 256, :], out_hbm.at[part, :])
    copies.wait_all()


def token_grads(dqkv_own, dqkv_oth, migrad, w_own, w_oth, begun=None):
    rows, width = migrad.shape
    half = rows // 2
    extra = () if begun is None else (begun,)
    return local_call(
        functools.partial(token_kernel, half * len(extra)), [jax.ShapeDtypeStruct(migrad.shape, F32)], "token_grads",
        "vvhvv" + "h" * len(extra), "h",
        [pltpu.VMEM((half, width), F32)] * 2 + [pltpu.SemaphoreType.DMA((1 + half // 256,))], 16,
        aliases={5: 0} if extra else None,
    )(dqkv_own, dqkv_oth, migrad, w_own, w_oth, *extra)[0]


def per_device(
    tokens, timesteps, src_len, tgt_len, sample_weight, w_qkv, bias_qv, w_out, bias_out, gain_attn, shift_attn,
    w_up, bias_up, w_down, bias_down, gain_mlp, shift_mlp, cotangent,
):
    rows, width = tokens.shape
    dp = lax.axis_size("dp")
    mp_index = lax.axis_index("mp")
    cols = bias_qv.shape[1]
    ff = bias_up.shape[0]
    plane = 4

    def swap(value):
        return lax.ppermute(value, "mp", [(0, 1), (1, 0)])

    def after(value, *earlier):
        return lax.optimization_barrier((value, *earlier))[0]

    qkv_oth_w = swap(w_qkv)
    wo_oth = swap(w_out)
    wu_oth = swap(w_up)
    wd_oth = swap(w_down)
    biases = prepare(bias_qv, bias_up)
    biases_oth = swap(biases)

    qkv_own, prob_own, ctx_own, ctx_own_h, x_low, x_low_h, table = attend(
        src_len, tgt_len, (tokens, timesteps), w_qkv, biases
    )
    qkv_oth, prob_oth, ctx_oth, ctx_oth_h, wo_own = attend(src_len, tgt_len, (x_low,), qkv_oth_w, biases_oth, w_out)
    (normed, inv, mid_low, hid_own, hid_oth, dg_own, dg_oth, layer_out, mgrad, sums_mlp) = mlp(
        src_len, tgt_len, sample_weight, tokens, table, ctx_own, ctx_oth, cotangent, wo_own, wo_oth, bias_out,
        gain_attn, shift_attn, w_up, wu_oth, biases, biases_oth, w_down, wd_oth, bias_down, gain_mlp, shift_mlp,
    )
    split = dp == 16
    in_plane = [[base + k for k in range(plane)] for base in range(0, dp, plane)]
    across = [[base * plane + k for base in range(dp // plane)] for k in range(plane)]

    def hop(value, bits):
        return lax.ppermute(value, "dp", [(i, i ^ bits) for i in range(dp)])

    def along(sa, ka, sb, kb):
        return ka, hop(sa, 1), kb, hop(sb, 2)

    def across(sa, ta, sb, tb):
        return ta, hop(sa, 2), tb, hop(sb, 1)

    (down_send,) = weight_grad(hid_oth, mgrad, dp, plane)
    down_recv = swap(down_send)
    pg_own, pg_oth, sum_up_own, sum_up_oth = pre_grads(after(mgrad, down_send), w_down, wd_oth, dg_own, dg_oth)
    down = weight_grad(hid_own, after(mgrad, pg_own), dp, plane, down_recv, split)
    if split:
        down = along(*down)
    (up_send,) = weight_grad(after(mid_low, down[0]), pg_oth, dp, plane)
    up_recv = swap(up_send)
    migrad, agrad, cg_own, cg_oth, sums_mid, qkv_oth, prob_oth = mid_grads(
        pg_own, pg_oth, after(mgrad, up_send), normed, inv, w_up, wu_oth, wo_own, wo_oth, gain_attn, qkv_oth, prob_oth
    )
    up = weight_grad(after(mid_low, agrad), pg_own, dp, plane, up_recv, split)
    if split:
        up = along(*up)
        down = across(*fold_first(after(down[0], up[0]), *down[1:]))
    dqkv_oth, sum_qv_oth, qkv_own, prob_own = attend_back(
        qkv_oth, prob_oth, after(cg_oth, up[0], down[0]), qkv_own, prob_own
    )
    dqkv_own, sum_qv_own = attend_back(qkv_own, prob_own, cg_own)
    keep, send = pack_sums(sums_mid, sums_mlp, sum_up_own, sum_up_oth, sum_qv_own, sum_qv_oth)
    attn_args = (x_low_h, dqkv_oth, ctx_oth_h, after(agrad, keep), dp)
    (attn_send,) = attn_grad(*attn_args, send) if split else attn_grad(*attn_args)
    attn_recv = swap(attn_send)
    attn_args = (x_low_h, dqkv_own, ctx_own_h)
    if split:
        up = across(*fold_first(after(up[0], attn_send), *up[1:]))
        send, keep_down = fold_second(after(down[0], up[0]), *down[1:], plane)
        down = keep_down, hop(send, plane)
        *parts, sums = attn_grad(*attn_args, after(agrad, keep_down), dp, keep, attn_recv)
        one = along(*parts[:4])
        send, keep_up = fold_second(after(up[0], one[0]), *up[1:], plane)
        up = keep_up, hop(send, plane)
        send_down, own_down = fold_outer(after(down[0], keep_up), down[1])
        two = along(*parts[4:])
        token_args = dqkv_own, dqkv_oth, after(migrad, own_down), w_qkv, qkv_oth_w
        begun = token_grads(*token_args)
        *folded, sums = attn_fold_first(after(one[0], begun), *one[1:], sums)
        one = across(*folded)
        tokens_grad = token_grads(*token_args[:3], w_qkv, qkv_oth_w, after(begun, one[0]))
        send, own_up = fold_outer_pair(after(send_down, tokens_grad), *up)
        arrived = hop(send, 2 * plane)
        two = across(*fold_first(after(two[0], own_up), *two[1:]))
        send, keep_one, sums = attn_fold_second(after(one[0], two[0]), *one[1:], sums)
        one = keep_one, hop(send, plane)
        grad_w_down, grad_w_up = last_pair(after(own_down, keep_one), own_up, arrived)
        send, keep_two = fold_second(after(two[0], grad_w_up), *two[1:], plane, LATE_FLOPS)
        two = keep_two, hop(send, plane)
        send, own_one, sums = attn_fold_outer(after(one[0], keep_two), one[1], sums)
        one = own_one, hop(send, 2 * plane)
        send, own_two = fold_outer(after(two[0], own_one), two[1])
        two = own_two, hop(send, 2 * plane)
        grad_w_qkv, grad_w_out, grad_rows, grad_bias_out, grad_bias_up, grad_bias_qv = attn_last(*one, sums, *two)
    else:
        in_plane = [[base + k for k in range(plane)] for base in range(0, dp, plane)]
        outside = [[base * plane + k for base in range(dp // plane)] for k in range(plane)]

        def scatter(value):
            value = lax.psum_scatter(value, "dp", scatter_dimension=0, axis_index_groups=in_plane)
            return lax.psum_scatter(value, "dp", scatter_dimension=0, axis_index_groups=outside).astype(F32)

        (attn,) = attn_grad(*attn_args, agrad, dp, None, attn_recv)
        tokens_grad = token_grads(dqkv_own, dqkv_oth, after(migrad, attn), w_qkv, qkv_oth_w)
        grad_w_down, grad_w_up, attn = scatter(down[0]), scatter(up[0]), scatter(attn)
        half = attn.shape[1] // 2
        grad_w_qkv, grad_w_out = attn[:3], jnp.concatenate([attn[3, :half], attn[3, half:]], axis=1)
        sums = lax.psum(keep + swap(send), "dp")
        whole = jnp.concatenate([sums[0:9], sums[9:18]], axis=1)
        grad_rows, grad_bias_out, grad_bias_up = whole[0:5], whole[5], whole[6:8].reshape(-1)
        grad_bias_qv = jnp.stack([sums[8], sums[17]])
    return (
        layer_out, tokens_grad, grad_w_qkv, grad_w_out, grad_w_up, grad_w_down,
        grad_bias_qv, grad_bias_up, grad_bias_out, grad_rows,
    )


def solution(mesh):
    in_specs = (
        P(("dp", "mp"), None), P("dp"), P("dp"), P("dp"), P("dp"),
        P(None, None, "mp"), P(None, "mp"), P("mp", None), P(), P(), P(),
        P(None, "mp"), P("mp"), P("mp", None), P(), P(), P(), P(("dp", "mp"), None),
    )
    out_specs = (
        P(("dp", "mp"), None), P(("dp", "mp"), None), P(None, "dp", "mp"), P(("mp", "dp"), None),
        P("dp", "mp"), P(("mp", "dp"), None), P(None, "mp"), P("mp"), P(), P(),
    )
    return jax.shard_map(per_device, mesh=mesh, in_specs=in_specs, out_specs=out_specs, check_vma=False)
```
